32 devices in a mesh: gx: 8 (over z, core), gy: 4 (over y, x).
Axes of the slice: x: 2, y: 2, z: 4, core: 2. Of those that a mesh axis runs over, the one named last changes fastest.
Arguments:
- estimate: float32 [256, 512, 128], P('gx', 'gy'), may hold values from 0.4 to 2.5
- view_one: float32 [256, 512, 128], P('gx', 'gy'), may hold values from 0.2 to 5
- view_two: float32 [256, 512, 128], P('gx', 'gy'), may hold values from 0.2 to 5
- psf_one: float32 [3, 21], replicated, may hold values from 0 to 2, as said below
- psf_two: float32 [3, 21], replicated, may hold values from 0 to 2, as said below
Outputs:
- updated: float32 [256, 512, 128], P('gx', 'gy')
The draws below stay inside these ranges and needn't reach their ends.
Inputs may be any that keep to these rules, and one draw needn't show every extreme that they name: `psf_one`: every entry is positive. `psf_two`: every entry is positive.
All inputs are finite; a program needn't handle non-finite values.
Results may differ from the reference program's by a relative error of at most 0.00005.
Values sent between devices are 32-bit elements; how exact they have to be, the bound alone decides.
No kernel may reach another device: no remote copies, remote signals or barrier semaphores. Data moves between devices by JAX's collectives and lax.ppermute only.
A program may use at most 192 MiB of HBM per device.

```python
import math
import jax
import jax.numpy as jnp
from jax import lax

CZ = 128
TAPS = 21
ITERS = 2
NX = 256
NY = 512


def shaped_kernels(key):
    key_core, key_halo, key_amp, key_axial, key_rough = jax.random.split(key, 5)
    core = jnp.exp(jax.random.uniform(key_core, (2,), jnp.float32, jnp.log(1.5), jnp.log(3.0)))
    broad = jnp.exp(jax.random.uniform(key_halo, (2,), jnp.float32, jnp.log(6.0), jnp.log(10.0)))
    amplitude = jax.random.uniform(key_amp, (2,), jnp.float32, 0.3, 0.4)
    axial = jnp.exp(jax.random.uniform(key_axial, (1,), jnp.float32, jnp.log(3.0), jnp.log(6.0)))
    offsets = jnp.arange(TAPS, dtype=jnp.float32) - (TAPS - 1) // 2
    squared = offsets[None, :] ** 2
    lateral_rows = jnp.exp(-squared / (2.0 * core[:, None] ** 2)) + amplitude[:, None] * jnp.exp(-squared / (2.0 * broad[:, None] ** 2))
    axial_row = jnp.exp(-squared / (2.0 * axial[:, None] ** 2))
    shape_rows = jnp.concatenate([lateral_rows, axial_row], axis=0)
    rough = jax.random.uniform(key_rough, (3, TAPS), jnp.float32, 0.5, 1.5)
    return (0.9 * shape_rows * rough).astype(jnp.float32)


def draw_psf_one(key, part):
    key = jax.random.fold_in(key, 11)
    return shaped_kernels(key)


def draw_psf_two(key, part):
    key = jax.random.fold_in(key, 23)
    return shaped_kernels(key)


def block_levels(stream_key, dims, shards, low, high):
    level = 1.0
    for axis_at, blocks in shards:
        steps = jax.random.uniform(jax.random.fold_in(jax.random.fold_in(stream_key, 6), axis_at), (blocks,), jnp.float32, low / len(shards), high / len(shards))
        level = level * jnp.repeat(jnp.exp(steps), dims[axis_at] // blocks).reshape((-1,) + (1,) * (len(dims) - 1 - axis_at))
    return level


def setup_inputs(seed: int = 0) -> dict:
    key_of = jax.random.split(jax.random.key(seed), 6)
    estimate = jnp.clip(jnp.exp(math.log(2.5) - 1.8325814 * jax.random.uniform(key_of[0], (NX, NY, CZ), jnp.float32) ** block_levels(key_of[0], (NX, NY, CZ), ((0, 8), (1, 4)), -0.2, 0.2)), 0.4, 2.5)
    view_one = jnp.clip(jnp.exp(math.log(5.0) - 3.218876 * jax.random.uniform(key_of[1], (NX, NY, CZ), jnp.float32) ** block_levels(key_of[1], (NX, NY, CZ), ((0, 8), (1, 4)), -0.2, 0.2)), 0.2, 5.0)
    view_two = jnp.clip(jnp.exp(math.log(5.0) - 3.218876 * jax.random.uniform(key_of[2], (NX, NY, CZ), jnp.float32) ** block_levels(key_of[2], (NX, NY, CZ), ((0, 8), (1, 4)), -0.2, 0.2)), 0.2, 5.0)
    psf_one = draw_psf_one(jax.random.fold_in(key_of[5], 71), 0)
    psf_two = draw_psf_two(jax.random.fold_in(key_of[5], 71), 0)
    return {"estimate": estimate, "view_one": view_one, "view_two": view_two, "psf_one": psf_one, "psf_two": psf_two}


def one_pass(volume, kernel, axis, adjoint):
    taps = kernel.shape[0]
    radius = (taps - 1) // 2
    width = [(0, 0), (0, 0), (0, 0)]
    width[axis] = (radius, radius)
    padded = jnp.pad(volume, width)
    length = volume.shape[axis]
    total = jnp.zeros(volume.shape, jnp.float32)
    for tap in range(taps):
        start = tap if adjoint else 2 * radius - tap
        total = total + kernel[tap] * lax.slice_in_dim(padded, start, start + length, axis=axis)
    return total


def operator(volume, kernels, adjoint):
    out = one_pass(volume, kernels[0], 0, adjoint)
    out = one_pass(out, kernels[1], 1, adjoint)
    return one_pass(out, kernels[2], 2, adjoint)


def reference(estimate, view_one, view_two, psf_one, psf_two):
    kern_one = psf_one / jnp.sum(psf_one, axis=1, keepdims=True)
    kern_two = psf_two / jnp.sum(psf_two, axis=1, keepdims=True)
    first = jnp.stack([kern_one[0], kern_one[1], kern_one[2]])
    second = jnp.stack([kern_two[1], kern_two[0], kern_two[2]])
    current = estimate
    for step in range(ITERS):
        ratio_one = view_one / operator(current, first, False)
        ratio_two = view_two / operator(current, second, False)
        back = operator(ratio_one, first, True) + operator(ratio_two, second, True)
        current = current * (back * 0.5)
    return current
```

```python
import jax
import jax.numpy as jnp
from jax import lax
from jax.experimental import pallas as pl
from jax.experimental.pallas import tpu as pltpu
from jax.sharding import PartitionSpec as P

ITERS = 2
F32 = jnp.float32
BF16 = jnp.bfloat16
VMEM_LIMIT = 56 * 1024 * 1024


def round_up(value, unit):
    return (value + unit - 1) // unit * unit


def split(value):
    high = value.astype(BF16)
    low = (value - high.astype(F32)).astype(BF16)
    return high, low


def weights_kernel(one_ref, two_ref, taps_ref, fwd_ref, back_ref, zf_ref, zb_ref):
    taps = one_ref.shape[1]
    radius = (taps - 1) // 2
    cols = fwd_ref.shape[0] // 2
    depth = zf_ref.shape[1] // 2
    rim = fwd_ref.shape[1] // 3 - 0
    one = one_ref[...] / jnp.sum(one_ref[...], axis=1, keepdims=True)
    two = two_ref[...] / jnp.sum(two_ref[...], axis=1, keepdims=True)
    x_rows = (one[0:1], two[1:2])
    y_rows = (one[1:2], two[0:1])
    z_rows = (one[2:3], two[2:3])
    pitch = taps_ref.shape[0] // 2
    taps_ref[...] = jnp.zeros_like(taps_ref)
    for view in range(2):
        for tap in range(taps):
            taps_ref[view * pitch + tap : view * pitch + tap + 1, :] = jnp.broadcast_to(
                x_rows[view][:, tap : tap + 1], (1, taps_ref.shape[1])
            )

    def band(row, offset):
        total = jnp.zeros(offset.shape, F32)
        for tap in range(taps):
            total = jnp.where(offset == tap, row[:, tap : tap + 1], total)
        return total

    def place(count, shape, dim):
        index = lax.broadcasted_iota(jnp.int32, shape, dim)
        spot = jnp.where(index < count, index, index - count - radius)
        spot = jnp.where(index >= count + radius, index - radius, spot)
        return jnp.where(index >= count + 2 * radius, 8 * count, spot)

    rim = fwd_ref.shape[1] // 2 - cols
    side = 32
    for view in range(2):
        rows = pl.ds(view * cols, cols)
        target = lax.broadcasted_iota(jnp.int32, (cols, cols), 0)
        source = lax.broadcasted_iota(jnp.int32, (cols, cols), 1)
        own_high, own_low = split(band(y_rows[view], target - source + radius))
        spots = place(cols, (cols, cols + 128), 1)[:, cols:]
        target = lax.broadcasted_iota(jnp.int32, (cols, 128), 0)
        side_full = band(y_rows[view], target - spots + radius)
        side_high, side_low = split(side_full)
        zero = jnp.zeros((cols, 128 - 3 * side), BF16)
        fwd_ref[rows, 0:cols] = own_high
        fwd_ref[rows, cols : 2 * cols] = own_high
        fwd_ref[rows, 2 * cols : 3 * cols] = own_low
        fwd_ref[rows, 3 * cols : 3 * cols + 128] = jnp.concatenate(
            [side_high[:, :side], side_low[:, :side], side_high[:, :side], zero], axis=1
        )
        full = back_ref.shape[0]
        spots = place(cols, (full, cols), 0)
        source = lax.broadcasted_iota(jnp.int32, (full, cols), 1)
        back_high, back_low = split(band(y_rows[view], source - spots + radius))
        base = view * 3 * cols
        back_ref[:, base : base + cols] = back_high
        back_ref[:, base + cols : base + 2 * cols] = back_high
        back_ref[:, base + 2 * cols : base + 3 * cols] = back_low
        first = lax.broadcasted_iota(jnp.int32, (depth, depth), 0)
        second = lax.broadcasted_iota(jnp.int32, (depth, depth), 1)
        for ref, offset in ((zf_ref, second - first + radius), (zb_ref, first - second + radius)):
            high, low = split(band(z_rows[view], offset))
            ref[view, 0:depth, 0:depth] = high
            ref[view, depth : 2 * depth, 0:depth] = high
            ref[view, 0:depth, depth : 2 * depth] = low
            ref[view, depth : 2 * depth, depth : 2 * depth] = low


def make_weights(psf_one, psf_two, cols, depth):
    return pl.pallas_call(
        weights_kernel,
        out_shape=(
            jax.ShapeDtypeStruct((48, 128), F32),
            jax.ShapeDtypeStruct((2 * cols, 3 * cols + 128), BF16),
            jax.ShapeDtypeStruct((cols + 32, 6 * cols), BF16),
            jax.ShapeDtypeStruct((2, 2 * depth, 2 * depth), BF16),
            jax.ShapeDtypeStruct((2, 2 * depth, 2 * depth), BF16),
        ),
        compiler_params=pltpu.CompilerParams(vmem_limit_bytes=VMEM_LIMIT),
        name="weights",
    )(psf_one, psf_two)


def columns_forward(weights, rows, sides):
    own = jnp.concatenate(rows, axis=1)
    side = jnp.concatenate(sides, axis=1)
    side = jnp.concatenate([side, jnp.zeros((8, side.shape[1]), F32)], axis=0)
    own_high, own_low = split(own)
    side_high, side_low = split(side)
    stacked = jnp.concatenate(
        [own_high, own_low, own_high, side_high, side_high, side_low,
         jnp.zeros((128 - 96, own.shape[1]), BF16)], axis=0)
    return jnp.dot(weights, stacked, preferred_element_type=F32)


def columns_back(weights, first, second):
    first_high, first_low = split(first)
    second_high, second_low = split(second)
    stacked = jnp.concatenate(
        [first_high, first_low, first_high, second_high, second_low, second_high], axis=0)
    return jnp.dot(weights, stacked, preferred_element_type=F32)


def depth_pass(value, matrix):
    high, low = split(value)
    both = jnp.dot(jnp.concatenate([high, low], axis=1), matrix, preferred_element_type=F32)
    depth = value.shape[1]
    return both[:, :depth] + both[:, depth:]


def load_taps(taps_ref, view, taps):
    pitch = taps_ref.shape[0] // 2
    return [
        jnp.broadcast_to(taps_ref[view * pitch + tap : view * pitch + tap + 1, :], (8, 128))
        for tap in range(taps)
    ]


def row_sums(weights, read, write, sources, targets, tap_of, block):
    taps = len(weights)
    for start in range(0, targets, block):
        outs = range(start, min(start + block, targets))
        totals = {}
        for r in range(sources):
            used = [q for q in outs if 0 <= tap_of(q, r) < taps]
            if not used:
                continue
            value = read(r)
            for q in used:
                term = weights[tap_of(q, r)] * value
                totals[q] = totals[q] + term if q in totals else term
        for q in outs:
            write(q, totals[q])


def own_columns_kernel(current_ref, side_ref, fwd_ref, out_ref):
    rows, cols, depth = current_ref.shape

    @pl.loop(0, rows // 2)
    def _(pair):
        at = 2 * pair
        both = columns_forward(
            fwd_ref[...],
            [current_ref[at], current_ref[at + 1]],
            [side_ref[at], side_ref[at + 1]],
        )
        for view in range(2):
            for half in range(2):
                out_ref[view, at + half] = both[
                    view * cols : (view + 1) * cols, half * depth : (half + 1) * depth]


def own_columns(current, side, fwd):
    rows, cols, depth = current.shape
    return pl.pallas_call(
        own_columns_kernel,
        out_shape=jax.ShapeDtypeStruct((2, rows, cols, depth), F32),
        compiler_params=pltpu.CompilerParams(vmem_limit_bytes=VMEM_LIMIT),
        cost_estimate=pl.CostEstimate(
            flops=2 * rows * depth * fwd.shape[0] * fwd.shape[1],
            bytes_accessed=4 * 3 * rows * cols * depth, transcendentals=0),
        name="own_columns",
    )(current, side, fwd)


def ratio_kernel(radius, low_ref, high_ref, own_ref, one_ref, two_ref, taps_ref, fwd_ref, back_ref,
                 zf_ref, zb_ref, rim_low_ref, rim_high_ref, spread_ref, halo, blur, rims):
    _, rows, cols, depth = own_ref.shape
    taps = 2 * radius + 1

    for ref, base in ((low_ref, 0), (high_ref, radius)):
        @pl.loop(0, radius // 2)
        def _(pair):
            at = 2 * pair
            both = columns_forward(
                fwd_ref[...],
                [ref[at, 0:cols], ref[at + 1, 0:cols]],
                [ref[at, cols:], ref[at + 1, cols:]],
            )
            for view in range(2):
                for half in range(2):
                    halo[view, base + at + half] = both[
                        view * cols : (view + 1) * cols, half * depth : (half + 1) * depth]

    for view in range(2):
        weights = load_taps(taps_ref, view, taps)

        @pl.loop(0, cols // 8)
        def _(tile):
            at = pl.ds(pl.multiple_of(tile * 8, 8), 8)

            def read(r):
                if r < radius:
                    return halo[view, r, at, :]
                if r < radius + rows:
                    return own_ref[view, r - radius, at, :]
                return halo[view, r - rows, at, :]

            def write(q, value):
                blur[view, q, at, :] = value

            row_sums(weights, read, write, rows + 2 * radius, rows,
                     lambda q, r: q + 2 * radius - r, 16)

    for view, seen in ((0, one_ref), (1, two_ref)):
        @pl.loop(0, rows)
        def _(row):
            blurred = depth_pass(blur[view, row], zf_ref[view])
            blur[view, row] = depth_pass(seen[row] / blurred, zb_ref[view])

    for view in range(2):
        weights = load_taps(taps_ref, view, taps)

        @pl.loop(0, cols // 8)
        def _(tile):
            at = pl.ds(pl.multiple_of(tile * 8, 8), 8)

            def read(r):
                return blur[view, r, at, :]

            def write(q, value):
                if q < radius:
                    rims[view, q, at, :] = value
                elif q < radius + rows:
                    spread_ref[view, q - radius, at, :] = value
                else:
                    rims[view, q - rows, at, :] = value

            row_sums(weights, read, write, rows, rows + 2 * radius,
                     lambda q, r: r - q + 2 * radius, 16)

    for ref, base in ((rim_low_ref, 0), (rim_high_ref, radius)):
        @pl.loop(0, radius // 2)
        def _(pair):
            at = 2 * pair
            beside = [
                jnp.concatenate([rims[view, base + at], rims[view, base + at + 1]], axis=1)
                for view in range(2)
            ]
            total = columns_back(back_ref[...], *beside)
            for half in range(2):
                ref[at + half] = total[: ref.shape[1], half * depth : (half + 1) * depth]


def ratios(low, high, own, one, two, weights, radius):
    taps, fwd, back, zf, zb = weights
    _, rows, cols, depth = own.shape
    wide = low.shape[1]
    return pl.pallas_call(
        lambda *refs: ratio_kernel(radius, *refs),
        out_shape=(
            jax.ShapeDtypeStruct((radius, wide, depth), F32),
            jax.ShapeDtypeStruct((radius, wide, depth), F32),
            jax.ShapeDtypeStruct((2, rows, cols, depth), F32),
        ),
        scratch_shapes=[
            pltpu.VMEM((2, 2 * radius, cols, depth), F32),
            pltpu.VMEM((2, rows, cols, depth), F32),
            pltpu.VMEM((2, 2 * radius, cols, depth), F32),
        ],
        compiler_params=pltpu.CompilerParams(vmem_limit_bytes=VMEM_LIMIT),
        cost_estimate=pl.CostEstimate(
            flops=40 * rows * cols * depth * 21, bytes_accessed=4 * 6 * rows * cols * depth,
            transcendentals=0),
        name="ratios",
    )(low, high, own, one, two, taps, fwd, back, zf, zb)


def own_back_kernel(spread_ref, back_ref, out_ref):
    _, rows, cols, depth = spread_ref.shape

    @pl.loop(0, rows // 2)
    def _(pair):
        at = 2 * pair
        beside = [
            jnp.concatenate([spread_ref[view, at], spread_ref[view, at + 1]], axis=1)
            for view in range(2)
        ]
        total = columns_back(back_ref[...], *beside)
        for half in range(2):
            out_ref[at + half] = total[: out_ref.shape[1], half * depth : (half + 1) * depth]


def own_back(spread, back, wide):
    _, rows, cols, depth = spread.shape
    return pl.pallas_call(
        own_back_kernel,
        out_shape=jax.ShapeDtypeStruct((rows, wide, depth), F32),
        compiler_params=pltpu.CompilerParams(vmem_limit_bytes=VMEM_LIMIT),
        cost_estimate=pl.CostEstimate(
            flops=2 * rows * depth * back.shape[0] * back.shape[1],
            bytes_accessed=4 * 3 * rows * cols * depth, transcendentals=0),
        name="own_back",
    )(spread, back)


def swap(to_next, to_previous, axis):
    count = lax.axis_size(axis)
    forward = [(i, i + 1) for i in range(count - 1)]
    backward = [(i + 1, i) for i in range(count - 1)]
    return lax.ppermute(to_next, axis, forward), lax.ppermute(to_previous, axis, backward)


def local(estimate, view_one, view_two, psf_one, psf_two):
    rows, cols, depth = estimate.shape
    radius = (psf_one.shape[1] - 1) // 2
    rim = round_up(2 * radius, 8)
    wide = cols + rim
    filler = jnp.zeros((rows, rim - 2 * radius, depth), F32)
    current = estimate
    low, high = swap(current[:, cols - radius :], current[:, :radius], "gy")
    side = jnp.concatenate([low, high, filler], axis=1)
    weights = make_weights(psf_one, psf_two, cols, depth)
    for step in range(ITERS):
        edge_low = jnp.concatenate([current[:radius], side[:radius]], axis=1)
        edge_high = jnp.concatenate([current[rows - radius :], side[rows - radius :]], axis=1)
        low, high = swap(edge_high, edge_low, "gx")
        own = own_columns(current, side, weights[1])
        rim_low, rim_high, spread = ratios(low, high, own, view_one, view_two, weights, radius)
        low, high = swap(rim_high, rim_low, "gx")
        total = own_back(spread, weights[2], wide)
        gap = jnp.zeros((rows - 2 * radius, wide, depth), F32)
        total = total + jnp.concatenate([low, gap, high], axis=0)
        mine = total[:, :cols]
        over_low = total[:, cols : cols + radius]
        over_high = total[:, cols + radius : cols + 2 * radius]
        last = step == ITERS - 1
        if last:
            low, high = swap(over_high, over_low, "gy")
        else:
            low, high = swap(
                jnp.concatenate([over_high, mine[:, cols - radius :]], axis=1),
                jnp.concatenate([over_low, mine[:, :radius]], axis=1), "gy")
            side_sum = jnp.concatenate(
                [over_low + low[:, radius:], over_high + high[:, radius:], filler], axis=1)
            side = side * (side_sum * 0.5)
            low, high = low[:, :radius], high[:, :radius]
        gap = jnp.zeros((rows, cols - 2 * radius, depth), F32)
        mine = mine + jnp.concatenate([low, gap, high], axis=1)
        current = current * (mine * 0.5)
    return current


def solution(mesh):
    in_specs = (P("gx", "gy", None), P("gx", "gy", None), P("gx", "gy", None), P(), P())
    out_specs = P("gx", "gy", None)
    return jax.shard_map(local, mesh=mesh, in_specs=in_specs, out_specs=out_specs, check_vma=False)
```

```python
import jax
import jax.numpy as jnp
from jax import lax
from jax.experimental import pallas as pl
from jax.experimental.pallas import tpu as pltpu
from jax.sharding import PartitionSpec as P

ITERS = 2
F32 = jnp.float32
BF16 = jnp.bfloat16
SMALL_LIMIT = 20 * 1024 * 1024
LARGE_LIMIT = 32 * 1024 * 1024


def round_up(value, unit):
    return (value + unit - 1) // unit * unit


def split(value):
    high = value.astype(BF16)
    low = (value - high.astype(F32)).astype(BF16)
    return high, low


def weights_kernel(one_ref, two_ref, taps_ref, fwd_ref, back_ref, zf_ref, zb_ref):
    taps = one_ref.shape[1]
    radius = (taps - 1) // 2
    cols = fwd_ref.shape[0] // 2
    depth = zf_ref.shape[1] // 2
    one = one_ref[...] / jnp.sum(one_ref[...], axis=1, keepdims=True)
    two = two_ref[...] / jnp.sum(two_ref[...], axis=1, keepdims=True)
    x_rows = (one[0:1], two[1:2])
    y_rows = (one[1:2], two[0:1])
    z_rows = (one[2:3], two[2:3])
    pitch = taps_ref.shape[0] // 2
    taps_ref[...] = jnp.zeros_like(taps_ref)
    for view in range(2):
        for tap in range(taps):
            taps_ref[view * pitch + tap : view * pitch + tap + 1, :] = jnp.broadcast_to(
                x_rows[view][:, tap : tap + 1], (1, taps_ref.shape[1])
            )

    def band(row, offset):
        total = jnp.zeros(offset.shape, F32)
        for tap in range(taps):
            total = jnp.where(offset == tap, row[:, tap : tap + 1], total)
        return total

    def place(count, shape, dim):
        index = lax.broadcasted_iota(jnp.int32, shape, dim)
        spot = jnp.where(index < count, index, index - count - radius)
        spot = jnp.where(index >= count + radius, index - radius, spot)
        return jnp.where(index >= count + 2 * radius, 8 * count, spot)

    side = 32
    for view in range(2):
        rows = pl.ds(view * cols, cols)
        target = lax.broadcasted_iota(jnp.int32, (cols, cols), 0)
        source = lax.broadcasted_iota(jnp.int32, (cols, cols), 1)
        own_high, own_low = split(band(y_rows[view], target - source + radius))
        spots = place(cols, (cols, cols + 128), 1)[:, cols:]
        target = lax.broadcasted_iota(jnp.int32, (cols, 128), 0)
        side_full = band(y_rows[view], target - spots + radius)
        side_high, side_low = split(side_full)
        zero = jnp.zeros((cols, 128 - 3 * side), BF16)
        fwd_ref[rows, 0:cols] = own_high
        fwd_ref[rows, cols : 2 * cols] = own_high
        fwd_ref[rows, 2 * cols : 3 * cols] = own_low
        fwd_ref[rows, 3 * cols : 3 * cols + 128] = jnp.concatenate(
            [side_high[:, :side], side_low[:, :side], side_high[:, :side], zero], axis=1
        )
        full = back_ref.shape[0]
        spots = place(cols, (full, cols), 0)
        source = lax.broadcasted_iota(jnp.int32, (full, cols), 1)
        back_high, back_low = split(band(y_rows[view], source - spots + radius))
        base = view * 3 * cols
        back_ref[:, base : base + cols] = back_high
        back_ref[:, base + cols : base + 2 * cols] = back_high
        back_ref[:, base + 2 * cols : base + 3 * cols] = back_low
        first = lax.broadcasted_iota(jnp.int32, (depth, depth), 0)
        second = lax.broadcasted_iota(jnp.int32, (depth, depth), 1)
        for ref, offset in ((zf_ref, second - first + radius), (zb_ref, first - second + radius)):
            high, low = split(band(z_rows[view], offset))
            ref[view, 0:depth, 0:depth] = high
            ref[view, depth : 2 * depth, 0:depth] = high
            ref[view, 0:depth, depth : 2 * depth] = low
            ref[view, depth : 2 * depth, depth : 2 * depth] = low


def make_weights(psf_one, psf_two, cols, depth):
    return pl.pallas_call(
        weights_kernel,
        out_shape=(
            jax.ShapeDtypeStruct((48, 128), F32),
            jax.ShapeDtypeStruct((2 * cols, 3 * cols + 128), BF16),
            jax.ShapeDtypeStruct((cols + 32, 6 * cols), BF16),
            jax.ShapeDtypeStruct((2, 2 * depth, 2 * depth), BF16),
            jax.ShapeDtypeStruct((2, 2 * depth, 2 * depth), BF16),
        ),
        compiler_params=pltpu.CompilerParams(vmem_limit_bytes=SMALL_LIMIT),
        name="weights",
    )(psf_one, psf_two)


def columns_forward(weights, rows, sides):
    own = jnp.concatenate(rows, axis=1)
    side = jnp.concatenate(sides, axis=1)
    side = jnp.concatenate([side, jnp.zeros((8, side.shape[1]), F32)], axis=0)
    own_high, own_low = split(own)
    side_high, side_low = split(side)
    stacked = jnp.concatenate(
        [own_high, own_low, own_high, side_high, side_high, side_low,
         jnp.zeros((128 - 96, own.shape[1]), BF16)], axis=0)
    return jnp.dot(weights, stacked, preferred_element_type=F32)


def columns_back(weights, first, second):
    first_high, first_low = split(first)
    second_high, second_low = split(second)
    stacked = jnp.concatenate(
        [first_high, first_low, first_high, second_high, second_low, second_high], axis=0)
    return jnp.dot(weights, stacked, preferred_element_type=F32)


def depth_pass(value, matrix):
    high, low = split(value)
    both = jnp.dot(jnp.concatenate([high, low], axis=1), matrix, preferred_element_type=F32)
    depth = value.shape[1]
    return both[:, :depth] + both[:, depth:]


def load_taps(taps_ref, view, taps):
    pitch = taps_ref.shape[0] // 2
    return [
        jnp.broadcast_to(taps_ref[view * pitch + tap : view * pitch + tap + 1, :], (8, 128))
        for tap in range(taps)
    ]


def row_sums(weights, read, write, sources, targets, tap_of, block):
    taps = len(weights)
    for start in range(0, targets, block):
        outs = range(start, min(start + block, targets))
        totals = {}
        for r in range(sources):
            used = [q for q in outs if 0 <= tap_of(q, r) < taps]
            if not used:
                continue
            value = read(r)
            for q in used:
                term = weights[tap_of(q, r)] * value
                totals[q] = totals[q] + term if q in totals else term
        for q in outs:
            write(q, totals[q])


def forward_pairs(fwd_ref, read, write, cols, depth):
    for pair in range(2):
        first, second = read(2 * pair), read(2 * pair + 1)
        both = columns_forward(fwd_ref[...], [first[0], second[0]], [first[1], second[1]])
        for view in range(2):
            for half in range(2):
                write(view, 2 * pair + half, both[
                    view * cols : (view + 1) * cols, half * depth : (half + 1) * depth])


def forward_kernel(radius, current_ref, side_ref, taps_ref, fwd_ref, out_ref, passed):
    rows, cols, depth = current_ref.shape
    taps = 2 * radius + 1

    @pl.loop(0, rows // 4)
    def _(step):
        at = 4 * step

        def write(view, k, block):
            passed[view, at + k] = block

        forward_pairs(
            fwd_ref, lambda k: (current_ref[at + k], side_ref[at + k]), write, cols, depth)

    for view in range(2):
        weights = load_taps(taps_ref, view, taps)

        @pl.loop(0, cols // 8)
        def _(tile):
            at = pl.ds(pl.multiple_of(tile * 8, 8), 8)

            def write(q, value):
                out_ref[view, q, at, :] = value

            row_sums(weights, lambda r: passed[view, r, at, :], write, rows, rows,
                     lambda q, r: q + radius - r, 16)


def forward(current, side, weights, radius):
    taps, fwd = weights[:2]
    rows, cols, depth = current.shape
    return pl.pallas_call(
        lambda *refs: forward_kernel(radius, *refs),
        out_shape=jax.ShapeDtypeStruct((2, rows, cols, depth), F32),
        scratch_shapes=[pltpu.VMEM((2, rows, cols, depth), F32)],
        compiler_params=pltpu.CompilerParams(vmem_limit_bytes=SMALL_LIMIT),
        cost_estimate=pl.CostEstimate(
            flops=2 * rows * depth * fwd.shape[0] * fwd.shape[1],
            bytes_accessed=4 * 3 * rows * cols * depth, transcendentals=0),
        name="forward",
    )(current, side, taps, fwd)


def ratio_kernel(radius, low_ref, high_ref, own_ref, one_ref, two_ref, taps_ref, fwd_ref, back_ref,
                 zf_ref, zb_ref, rim_low_ref, rim_high_ref, spread_ref, halo, edges):
    _, rows, cols, depth = own_ref.shape
    taps = 2 * radius + 1
    wide = low_ref.shape[1]

    @pl.loop(0, radius // 2)
    def _(step):
        at = 2 * step

        def read(k):
            ref = (low_ref, high_ref)[k // 2]
            return ref[at + k % 2, 0:cols], ref[at + k % 2, cols:wide]

        def write(view, k, block):
            halo[view, (k // 2) * radius + at + k % 2] = block

        forward_pairs(fwd_ref, read, write, cols, depth)

    for view in range(2):
        weights = load_taps(taps_ref, view, taps)

        @pl.loop(0, cols // 8)
        def _(tile):
            at = pl.ds(pl.multiple_of(tile * 8, 8), 8)

            def write_low(q, value):
                edges[view, q, at, :] = value + own_ref[view, q, at, :]

            def write_high(q, value):
                edges[view, radius + q, at, :] = value + own_ref[view, rows - radius + q, at, :]

            row_sums(weights, lambda r: halo[view, r, at, :], write_low, radius, radius,
                     lambda q, r: q + 2 * radius - r, radius)
            row_sums(weights, lambda r: halo[view, radius + r, at, :], write_high, radius, radius,
                     lambda q, r: q - r, radius)

    def ratio_rows(start, count, source):
        @pl.loop(0, count // 2)
        def _(step):
            at = 2 * step
            for view, seen in ((0, one_ref), (1, two_ref)):
                value = source(view, at).reshape(2 * cols, depth)
                blurred = depth_pass(value, zf_ref[view])
                recorded = seen[pl.ds(start + at, 2)].reshape(2 * cols, depth)
                spread = depth_pass(recorded / blurred, zb_ref[view])
                spread_ref[view, pl.ds(start + at, 2)] = spread.reshape(2, cols, depth)

    ratio_rows(0, radius, lambda view, at: edges[view, pl.ds(at, 2)])
    ratio_rows(radius, rows - 2 * radius, lambda view, at: own_ref[view, pl.ds(radius + at, 2)])
    ratio_rows(rows - radius, radius, lambda view, at: edges[view, pl.ds(radius + at, 2)])

    for view in range(2):
        weights = load_taps(taps_ref, view, taps)

        @pl.loop(0, cols // 8)
        def _(tile):
            at = pl.ds(pl.multiple_of(tile * 8, 8), 8)

            def write_low(q, value):
                halo[view, q, at, :] = value

            def write_high(q, value):
                halo[view, radius + q, at, :] = value

            row_sums(weights, lambda r: spread_ref[view, r, at, :], write_low, radius, radius,
                     lambda q, r: r - q + 2 * radius, radius)
            row_sums(weights, lambda r: spread_ref[view, rows - radius + r, at, :], write_high,
                     radius, radius, lambda q, r: r - q, radius)

    @pl.loop(0, radius // 2)
    def _(step):
        at = 2 * step
        for ref, base in ((rim_low_ref, 0), (rim_high_ref, radius)):
            beside = [
                jnp.concatenate([halo[view, base + at], halo[view, base + at + 1]], axis=1)
                for view in range(2)
            ]
            total = columns_back(back_ref[...], *beside)
            for half in range(2):
                ref[at + half] = total[:wide, half * depth : (half + 1) * depth]


def ratios(low, high, own, one, two, weights, radius):
    taps, fwd, back, zf, zb = weights
    _, rows, cols, depth = own.shape
    wide = low.shape[1]
    return pl.pallas_call(
        lambda *refs: ratio_kernel(radius, *refs),
        out_shape=(
            jax.ShapeDtypeStruct((radius, wide, depth), F32),
            jax.ShapeDtypeStruct((radius, wide, depth), F32),
            jax.ShapeDtypeStruct((2, rows, cols, depth), F32),
        ),
        scratch_shapes=[
            pltpu.VMEM((2, 2 * radius, cols, depth), F32),
            pltpu.VMEM((2, 2 * radius, cols, depth), F32),
        ],
        compiler_params=pltpu.CompilerParams(vmem_limit_bytes=LARGE_LIMIT),
        cost_estimate=pl.CostEstimate(
            flops=40 * rows * cols * depth * 21, bytes_accessed=4 * 6 * rows * cols * depth,
            transcendentals=0),
        name="ratios",
    )(low, high, own, one, two, taps, fwd, back, zf, zb)


def back_kernel(radius, spread_ref, taps_ref, back_ref, out_ref, summed):
    _, rows, cols, depth = spread_ref.shape
    taps = 2 * radius + 1
    for view in range(2):
        weights = load_taps(taps_ref, view, taps)

        @pl.loop(0, cols // 8)
        def _(tile):
            at = pl.ds(pl.multiple_of(tile * 8, 8), 8)

            def write(q, value):
                summed[view, q, at, :] = value

            row_sums(weights, lambda r: spread_ref[view, r, at, :], write, rows, rows,
                     lambda q, r: r - q + radius, 16)

    @pl.loop(0, rows // 4)
    def _(step):
        for pair in range(2):
            at = 4 * step + 2 * pair
            beside = [
                jnp.concatenate([summed[view, at], summed[view, at + 1]], axis=1)
                for view in range(2)
            ]
            total = columns_back(back_ref[...], *beside)
            for half in range(2):
                out_ref[at + half] = total[: out_ref.shape[1], half * depth : (half + 1) * depth]


def own_back(spread, weights, wide, radius):
    taps, _, back = weights[:3]
    _, rows, cols, depth = spread.shape
    return pl.pallas_call(
        lambda *refs: back_kernel(radius, *refs),
        out_shape=jax.ShapeDtypeStruct((rows, wide, depth), F32),
        scratch_shapes=[pltpu.VMEM((2, rows, cols, depth), F32)],
        compiler_params=pltpu.CompilerParams(vmem_limit_bytes=SMALL_LIMIT),
        cost_estimate=pl.CostEstimate(
            flops=2 * rows * depth * back.shape[0] * back.shape[1],
            bytes_accessed=4 * 3 * rows * cols * depth, transcendentals=0),
        name="own_back",
    )(spread, taps, back)


def swap(to_next, to_previous, axis):
    count = lax.axis_size(axis)
    forward = [(i, i + 1) for i in range(count - 1)]
    backward = [(i + 1, i) for i in range(count - 1)]
    return lax.ppermute(to_next, axis, forward), lax.ppermute(to_previous, axis, backward)


def local(estimate, view_one, view_two, psf_one, psf_two):
    rows, cols, depth = estimate.shape
    radius = (psf_one.shape[1] - 1) // 2
    rim = round_up(2 * radius, 8)
    wide = cols + rim
    filler = jnp.zeros((rows, rim - 2 * radius, depth), F32)
    current = estimate
    low, high = swap(current[:, cols - radius :], current[:, :radius], "gy")
    side = jnp.concatenate([low, high, filler], axis=1)
    weights = make_weights(psf_one, psf_two, cols, depth)
    for step in range(ITERS):
        edge_low = jnp.concatenate([current[:radius], side[:radius]], axis=1)
        edge_high = jnp.concatenate([current[rows - radius :], side[rows - radius :]], axis=1)
        low, high = swap(edge_high, edge_low, "gx")
        own = forward(current, side, weights, radius)
        rim_low, rim_high, spread = ratios(low, high, own, view_one, view_two, weights, radius)
        low, high = swap(rim_high, rim_low, "gx")
        total = own_back(spread, weights, wide, radius)
        gap = jnp.zeros((rows - 2 * radius, wide, depth), F32)
        total = total + jnp.concatenate([low, gap, high], axis=0)
        mine = total[:, :cols]
        over_low = total[:, cols : cols + radius]
        over_high = total[:, cols + radius : cols + 2 * radius]
        last = step == ITERS - 1
        if last:
            low, high = swap(over_high, over_low, "gy")
        else:
            low, high = swap(
                jnp.concatenate([over_high, mine[:, cols - radius :]], axis=1),
                jnp.concatenate([over_low, mine[:, :radius]], axis=1), "gy")
            side_sum = jnp.concatenate(
                [over_low + low[:, radius:], over_high + high[:, radius:], filler], axis=1)
            side = side * (side_sum * 0.5)
            low, high = low[:, :radius], high[:, :radius]
        gap = jnp.zeros((rows, cols - 2 * radius, depth), F32)
        mine = mine + jnp.concatenate([low, gap, high], axis=1)
        current = current * (mine * 0.5)
    return current


def solution(mesh):
    in_specs = (P("gx", "gy", None), P("gx", "gy", None), P("gx", "gy", None), P(), P())
    out_specs = P("gx", "gy", None)
    return jax.shard_map(local, mesh=mesh, in_specs=in_specs, out_specs=out_specs, check_vma=False)
```

```python
import functools
import jax
import jax.numpy as jnp
from jax import lax
from jax.experimental import pallas as pl
from jax.experimental.pallas import tpu as pltpu
from jax.sharding import PartitionSpec as P

ITERS = 2
F32 = jnp.float32
BF16 = jnp.bfloat16
LIMIT = 24 * 1024 * 1024
EDGE = 16
NEAR = 32


def round_up(value, unit):
    return (value + unit - 1) // unit * unit


def edge_width(radius):
    return 2 * EDGE + round_up(2 * radius, 8)


def split(value):
    high = value.astype(BF16)
    low = (value - high.astype(F32)).astype(BF16)
    return high, low


def stack(value):
    high, low = split(value)
    return [high, low, high]


def multiply(weights, value):
    return jnp.dot(weights, value, preferred_element_type=F32)


def call(kernel, name, out_shape, flops, moved, scratch=()):
    return pl.pallas_call(
        kernel,
        out_shape=out_shape,
        scratch_shapes=list(scratch),
        compiler_params=pltpu.CompilerParams(vmem_limit_bytes=LIMIT),
        cost_estimate=pl.CostEstimate(flops=flops, bytes_accessed=moved, transcendentals=0),
        name=name,
    )


def shape(*dims, dtype=F32):
    return jax.ShapeDtypeStruct(dims, dtype)


def weights_kernel(cols, one_ref, two_ref, taps_ref, main_ref, edge_ref, full_ref, back_ref,
                   zf_ref, zb_ref):
    taps = one_ref.shape[1]
    radius = (taps - 1) // 2
    depth = zf_ref.shape[1] // 2
    main = cols - 2 * EDGE
    edge = round_up(edge_width(radius), 16)
    one = one_ref[...] / jnp.sum(one_ref[...], axis=1, keepdims=True)
    two = two_ref[...] / jnp.sum(two_ref[...], axis=1, keepdims=True)
    x_rows = (one[0:1], two[1:2])
    y_rows = (one[1:2], two[0:1])
    z_rows = (one[2:3], two[2:3])
    pitch = taps_ref.shape[0] // 2
    taps_ref[...] = jnp.zeros_like(taps_ref)
    for view in range(2):
        for tap in range(taps):
            taps_ref[view * pitch + tap : view * pitch + tap + 1, :] = jnp.broadcast_to(
                x_rows[view][:, tap : tap + 1], (1, taps_ref.shape[1])
            )

    def iota(dims, dim):
        return lax.broadcasted_iota(jnp.int32, dims, dim)

    def band(row, offset):
        total = jnp.zeros(offset.shape, F32)
        for tap in range(taps):
            total = jnp.where(offset == tap, row[:, tap : tap + 1], total)
        return total

    def edge_place(index):
        place = jnp.where(index < EDGE, index, index + cols - 2 * EDGE)
        place = jnp.where(index >= 2 * EDGE, index - 2 * EDGE - radius, place)
        place = jnp.where(index >= 2 * EDGE + radius, index - 2 * EDGE - radius + cols, place)
        return jnp.where(index >= 2 * EDGE + 2 * radius, 8 * cols, place)

    def laid(value):
        high, low = split(value)
        return jnp.concatenate([high, high, low], axis=1)

    for view in range(2):
        row = y_rows[view]
        rows = pl.ds(view * cols, cols)
        dims = (cols, main)
        left = laid(band(row, iota(dims, 0) - (iota(dims, 1) + EDGE) + radius))
        dims = (cols, edge)
        right = laid(band(row, iota(dims, 0) - edge_place(iota(dims, 1)) + radius))
        main_ref[rows, :] = left
        edge_ref[rows, :] = right
        full_ref[rows, :] = jnp.concatenate([left, right], axis=1)
        part = slice(3 * cols * view, 3 * cols * (view + 1))
        dims = (main, cols)
        back_ref[0:main, part] = laid(band(row, iota(dims, 1) - (iota(dims, 0) + EDGE) + radius))
        dims = (edge, cols)
        back_ref[main:, part] = laid(band(row, iota(dims, 1) - edge_place(iota(dims, 0)) + radius))
        dims = (depth, depth)
        first, second = iota(dims, 0), iota(dims, 1)
        for ref, offset in ((zf_ref, second - first + radius), (zb_ref, first - second + radius)):
            high, low = split(band(z_rows[view], offset))
            both = jnp.concatenate([high, low], axis=1)
            ref[view] = jnp.concatenate([both, both], axis=0)


def make_weights(psf_one, psf_two, cols, depth):
    radius = (psf_one.shape[1] - 1) // 2
    main = cols - 2 * EDGE
    edge = round_up(edge_width(radius), 16)
    return call(
        functools.partial(weights_kernel, cols), "weights",
        (
            shape(48, 128),
            shape(2 * cols, 3 * main, dtype=BF16),
            shape(2 * cols, 3 * edge, dtype=BF16),
            shape(2 * cols, 3 * (main + edge), dtype=BF16),
            shape(main + edge, 6 * cols, dtype=BF16),
            shape(2, 2 * depth, 2 * depth, dtype=BF16),
            shape(2, 2 * depth, 2 * depth, dtype=BF16),
        ), 1 << 22, 1 << 20)(psf_one, psf_two)


def pad_rows(value):
    extra = round_up(value.shape[0], 16) - value.shape[0]
    if not extra:
        return value
    return jnp.concatenate([value, jnp.zeros((extra, value.shape[1]), value.dtype)], axis=0)


def beside(first, second):
    return jnp.concatenate([first, second], axis=1)


def depth_pass(value, matrix):
    both = multiply_depth(value, matrix)
    depth = value.shape[1]
    return both[:, :depth] + both[:, depth:]


def multiply_depth(value, matrix):
    high, low = split(value)
    return multiply(jnp.concatenate([high, low], axis=1), matrix)


def load_taps(taps_ref, view, taps):
    pitch = taps_ref.shape[0] // 2
    return [
        jnp.broadcast_to(taps_ref[view * pitch + tap : view * pitch + tap + 1, :], (8, 128))
        for tap in range(taps)
    ]


def row_sums(weights, read, write, sources, targets, tap_of, block):
    taps = len(weights)
    for start in range(0, targets, block):
        outs = range(start, min(start + block, targets))
        totals = {}
        for r in range(sources):
            used = [q for q in outs if 0 <= tap_of(q, r) < taps]
            if not used:
                continue
            value = read(r)
            for q in used:
                term = weights[tap_of(q, r)] * value
                totals[q] = totals[q] + term if q in totals else term
        for q in outs:
            write(q, totals[q])


def tiles(start, stop):
    def run(body):
        @pl.loop(0, (stop - start) // 8)
        def _(tile):
            inner = pl.multiple_of(tile * 8, 8)
            body(pl.ds(pl.multiple_of(start + inner, 8), 8), pl.ds(inner, 8))
    return run


def own_tap_forward(radius):
    return lambda q, r: q + radius - r


def own_tap_back(radius):
    return lambda q, r: r - q + radius


def each_row(rows, radius, body):
    @pl.loop(0, radius // 2)
    def _(step):
        for k in range(2):
            row = 2 * step + k
            body(row, (0, row))
            body(rows - radius + row, (1, row))

    @pl.loop(0, (rows - 2 * radius) // 2)
    def _(step):
        for k in range(2):
            body(radius + 2 * step + k, None)


def main_pass(radius, rows, read, taps_ref, main_ref, inner_ref, near_ref, passed):
    cols = main_ref.shape[0] // 2
    depth = passed.shape[3]

    @pl.loop(0, rows // 4)
    def _(step):
        for pair in range(2):
            at = 4 * step + 2 * pair
            value = beside(read(at), read(at + 1))
            both = multiply(main_ref[...], jnp.concatenate(stack(value), axis=0))
            for view in range(2):
                for half in range(2):
                    block = both[view * cols : (view + 1) * cols, half * depth : (half + 1) * depth]
                    passed[view, at + half] = block[NEAR : cols - NEAR]
                    near_ref[view, at + half, 0:NEAR] = block[:NEAR]
                    near_ref[view, at + half, NEAR:] = block[cols - NEAR :]

    for view in range(2):
        weights = load_taps(taps_ref, view, 2 * radius + 1)

        @tiles(0, cols - 2 * NEAR)
        def _(at, _inner):
            def write(q, value):
                inner_ref[view, q, at, :] = value

            row_sums(weights, lambda r: passed[view, r, at, :], write, rows, rows,
                     own_tap_forward(radius), 16)


def forward_first_kernel(radius, current_ref, taps_ref, main_ref, inner_ref, near_ref, passed):
    rows, cols, _ = current_ref.shape
    main_pass(radius, rows, lambda row: current_ref[row, EDGE : cols - EDGE],
              taps_ref, main_ref, inner_ref, near_ref, passed)


def forward_next_kernel(radius, base, current_ref, sum_ref, low_ref, high_ref, taps_ref, main_ref,
                        next_ref, inner_ref, near_ref, passed):
    rows, width, _ = sum_ref.shape
    rims = (low_ref, high_ref)

    def update(row, rim):
        total = sum_ref[row]
        if rim is not None:
            total = total + rims[rim[0]][rim[1], 0:width]
        next_ref[row] = current_ref[row, base : base + width] * (total * 0.5)

    each_row(rows, radius, update)
    main_pass(radius, rows, lambda row: next_ref[row], taps_ref, main_ref, inner_ref, near_ref, passed)


def forward_shapes(rows, cols, depth):
    return (
        (shape(2, rows, cols - 2 * NEAR, depth), shape(2, rows, 2 * NEAR, depth)),
        [pltpu.VMEM((2, rows, cols - 2 * NEAR, depth), F32)],
    )


def forward_first(current, weights, radius):
    rows, cols, depth = current.shape
    outs, scratch = forward_shapes(rows, cols, depth)
    return call(
        functools.partial(forward_first_kernel, radius), "forward_first", outs,
        1 << 31, 12 * rows * cols * depth, scratch)(current, weights[0], weights[1])


def forward_next(current, base, main_sum, low, high, weights, radius):
    rows, width, depth = main_sum.shape
    outs, scratch = forward_shapes(rows, width + 2 * EDGE, depth)
    return call(
        functools.partial(forward_next_kernel, radius, base), "forward_next",
        (shape(rows, width, depth),) + outs, 1 << 31, 12 * rows * width * depth, scratch,
    )(current, main_sum, low, high, weights[0], weights[1])


def write_messages(radius, main_row, edge_ref, low_ref, high_ref):
    rows = edge_ref.shape[0]
    width = low_ref.shape[1] - edge_ref.shape[1]

    @pl.loop(0, radius)
    def _(row):
        for ref, at in ((low_ref, row), (high_ref, rows - radius + row)):
            ref[row, 0:width] = main_row(at)
            ref[row, width:] = edge_ref[at]


def edge_first_kernel(radius, current_ref, from_low_ref, from_high_ref, edge_ref, low_ref, high_ref):
    rows, cols, depth = current_ref.shape
    rims = 2 * EDGE

    @pl.loop(0, rows)
    def _(row):
        edge_ref[row, 0:EDGE] = current_ref[row, 0:EDGE]
        edge_ref[row, EDGE:rims] = current_ref[row, cols - EDGE :]
        edge_ref[row, edge_ref.shape[1] - 8 :] = jnp.zeros((8, depth), F32)
        edge_ref[row, rims : rims + radius] = from_low_ref[row]
        edge_ref[row, rims + radius : rims + 2 * radius] = from_high_ref[row]

    write_messages(radius, lambda at: current_ref[at, EDGE : cols - EDGE], edge_ref, low_ref, high_ref)


def add_y(radius, total_ref, row, from_low_ref, from_high_ref):
    rims = 2 * EDGE
    total_ref[0:radius] = total_ref[0:radius] + from_low_ref[row, 0:radius]
    total_ref[rims - radius : rims] = total_ref[rims - radius : rims] + from_high_ref[row, 0:radius]
    if from_low_ref.shape[1] > radius:
        low, high = slice(rims, rims + radius), slice(rims + radius, rims + 2 * radius)
        total_ref[low] = total_ref[low] + from_low_ref[row, radius:]
        total_ref[high] = total_ref[high] + from_high_ref[row, radius:]


def edge_next_kernel(radius, edge_ref, sum_ref, from_low_ref, from_high_ref, main_ref,
                     next_ref, low_ref, high_ref, totals):
    @pl.loop(0, edge_ref.shape[0])
    def _(row):
        totals[row] = sum_ref[row]
        add_y(radius, totals.at[row], row, from_low_ref, from_high_ref)
        next_ref[row] = edge_ref[row] * (totals[row] * 0.5)

    write_messages(radius, lambda at: main_ref[at], next_ref, low_ref, high_ref)


def edge_shapes(rows, cols, depth, radius):
    wide = cols - 2 * EDGE + edge_width(radius)
    return (shape(rows, edge_width(radius), depth), shape(radius, wide, depth), shape(radius, wide, depth))


def edge_first(current, from_low, from_high, radius):
    outs = edge_shapes(*current.shape, radius)
    return call(functools.partial(edge_first_kernel, radius), "edge_first", outs, 1, 1 << 22)(
        current, from_low, from_high)


def edge_next(edge, edge_sum, from_low, from_high, main, radius):
    rows, width, depth = main.shape
    outs = edge_shapes(rows, width + 2 * EDGE, depth, radius)
    return call(
        functools.partial(edge_next_kernel, radius), "edge_next", outs, 1, 1 << 22,
        [pltpu.VMEM(edge.shape, F32)])(edge, edge_sum, from_low, from_high, main)


def y_messages_kernel(radius, whole, edge_ref, low_ref, high_ref, sum_ref, next_ref, previous_ref):
    rows, width, _ = edge_ref.shape
    before = low_ref.shape[1] - width
    refs = (low_ref, high_ref)
    rims = 2 * EDGE

    def row_of(row, rim):
        total = edge_ref[row]
        if rim is not None:
            total = total + refs[rim[0]][rim[1], before:]
        sum_ref[row] = total
        previous_ref[row, 0:radius] = sum_ref[row, rims : rims + radius]
        next_ref[row, 0:radius] = sum_ref[row, rims + radius : rims + 2 * radius]
        if whole:
            previous_ref[row, radius:] = sum_ref[row, 0:radius]
            next_ref[row, radius:] = sum_ref[row, rims - radius : rims]

    each_row(rows, radius, row_of)


def y_messages(edge_sum, low, high, whole, radius):
    rows, width, depth = edge_sum.shape
    sent = shape(rows, 2 * radius if whole else radius, depth)
    return call(
        functools.partial(y_messages_kernel, radius, whole), "y_messages",
        (shape(rows, width, depth), sent, sent), 1, 1 << 22)(edge_sum, low, high)


def ratio_block(values, seen, zf_ref, zb_ref, view):
    blurred = depth_pass(values, zf_ref[view])
    return depth_pass(seen / blurred, zb_ref[view])


def forward_edge_kernel(radius, current_ref, inner_ref, before_ref, one_ref, two_ref, taps_ref, edge_ref,
                        zf_ref, zb_ref, near_ref, middle_ref, passed):
    rows, cols, depth = one_ref.shape
    kept = jnp.concatenate(
        [edge_ref[start : start + NEAR] for start in (0, cols - NEAR, cols, 2 * cols - NEAR)], axis=0)

    @pl.loop(0, rows // 4)
    def _(step):
        for pair in range(2):
            at = 4 * step + 2 * pair
            value = pad_rows(beside(current_ref[at], current_ref[at + 1]))
            both = multiply(kept, jnp.concatenate(stack(value), axis=0))
            for view in range(2):
                for half in range(2):
                    passed[view, at + half] = before_ref[view, at + half] + both[
                        2 * NEAR * view : 2 * NEAR * (view + 1), half * depth : (half + 1) * depth]

    for view in range(2):
        weights = load_taps(taps_ref, view, 2 * radius + 1)

        @tiles(0, 2 * NEAR)
        def _(at, _inner):
            def write(q, value):
                near_ref[view, q, at, :] = value

            row_sums(weights, lambda r: passed[view, r, at, :], write, rows, rows,
                     own_tap_forward(radius), 16)

    @pl.loop(0, (rows - 2 * radius) // 2)
    def _(step):
        at = 2 * step
        for view, seen in ((0, one_ref), (1, two_ref)):
            parts = []
            for row in (radius + at, radius + at + 1):
                parts += [near_ref[view, row, 0:NEAR], inner_ref[view, row], near_ref[view, row, NEAR:]]
            value = ratio_block(
                jnp.concatenate(parts, axis=0), seen[pl.ds(radius + at, 2)].reshape(2 * cols, depth),
                zf_ref, zb_ref, view)
            middle_ref[view, pl.ds(at, 2)] = value.reshape(2, cols, depth)


def forward_edge(current, inner, before, one, two, weights, radius):
    taps, _, edge, _, _, zf, zb = weights
    rows, cols, depth = one.shape
    return call(
        functools.partial(forward_edge_kernel, radius), "forward_edge",
        (shape(2, rows, 2 * NEAR, depth), shape(2, rows - 2 * radius, cols, depth)),
        1 << 31, 24 * rows * NEAR * depth,
        [pltpu.VMEM((2, rows, 2 * NEAR, depth), F32)],
    )(current, inner, before, one, two, taps, edge, zf, zb)


def ratio_kernel(radius, low_ref, high_ref, inner_ref, near_ref, one_ref, two_ref, taps_ref, full_ref,
                 back_ref, zf_ref, zb_ref, rim_low_ref, rim_high_ref, outer_ref, halo, edges):
    rows, cols, depth = one_ref.shape
    main = cols - 2 * EDGE
    taps = 2 * radius + 1

    @pl.loop(0, radius // 2)
    def _(step):
        at = 2 * step
        for side, ref in enumerate((low_ref, high_ref)):
            left = beside(ref[at, 0:main], ref[at + 1, 0:main])
            right = pad_rows(beside(ref[at, main:], ref[at + 1, main:]))
            both = multiply(full_ref[...], jnp.concatenate(stack(left) + stack(right), axis=0))
            for view in range(2):
                for half in range(2):
                    halo[view, side * radius + at + half] = both[
                        view * cols : (view + 1) * cols, half * depth : (half + 1) * depth]

    for view in range(2):
        weights = load_taps(taps_ref, view, taps)
        for ref, start, stop, shift in (
            (near_ref, 0, NEAR, 0), (inner_ref, NEAR, cols - NEAR, 0),
            (near_ref, cols - NEAR, cols, NEAR),
        ):
            @tiles(start, stop)
            def _(at, inner):
                own = pl.ds(pl.multiple_of(inner.start + shift, 8), 8)

                def write_low(q, value):
                    edges[view, q, at, :] = value + ref[view, q, own, :]

                def write_high(q, value):
                    edges[view, radius + q, at, :] = value + ref[view, rows - radius + q, own, :]

                row_sums(weights, lambda r: halo[view, r, at, :], write_low, radius, radius,
                         lambda q, r: q + 2 * radius - r, radius)
                row_sums(weights, lambda r: halo[view, radius + r, at, :], write_high, radius, radius,
                         lambda q, r: q - r, radius)

    @pl.loop(0, radius // 2)
    def _(step):
        at = 2 * step
        for base, start in ((0, 0), (radius, rows - radius)):
            for view, seen in ((0, one_ref), (1, two_ref)):
                value = ratio_block(
                    edges[view, pl.ds(base + at, 2)].reshape(2 * cols, depth),
                    seen[pl.ds(start + at, 2)].reshape(2 * cols, depth), zf_ref, zb_ref, view)
                outer_ref[view, pl.ds(base + at, 2)] = value.reshape(2, cols, depth)

    for view in range(2):
        weights = load_taps(taps_ref, view, taps)

        @tiles(0, cols)
        def _(at, _inner):
            def write_low(q, value):
                halo[view, q, at, :] = value

            def write_high(q, value):
                halo[view, radius + q, at, :] = value

            row_sums(weights, lambda r: outer_ref[view, r, at, :], write_low, radius, radius,
                     lambda q, r: r - q + 2 * radius, radius)
            row_sums(weights, lambda r: outer_ref[view, radius + r, at, :], write_high,
                     radius, radius, lambda q, r: r - q, radius)

    @pl.loop(0, radius // 2)
    def _(step):
        at = 2 * step
        for ref, base in ((rim_low_ref, 0), (rim_high_ref, radius)):
            parts = []
            for view in range(2):
                parts += stack(beside(halo[view, base + at], halo[view, base + at + 1]))
            total = multiply(back_ref[...], jnp.concatenate(parts, axis=0))
            for half in range(2):
                ref[at + half] = total[: ref.shape[1], half * depth : (half + 1) * depth]


def ratios(low, high, inner, near, one, two, weights, radius):
    taps, _, _, full, back, zf, zb = weights
    rows, cols, depth = one.shape
    wide = low.shape[1]
    return call(
        functools.partial(ratio_kernel, radius), "ratios",
        (shape(radius, wide, depth), shape(radius, wide, depth), shape(2, 2 * radius, cols, depth)),
        1 << 33, 24 * rows * cols * depth,
        [pltpu.VMEM((2, 2 * radius, cols, depth), F32)] * 2,
    )(low, high, inner, near, one, two, taps, full, back, zf, zb)


def back_kernel(radius, outer_ref, middle_ref, taps_ref, back_ref, main_ref, edge_ref, summed):
    rows = main_ref.shape[0]
    width = main_ref.shape[1]
    depth = main_ref.shape[2]
    cols = outer_ref.shape[2]
    for view in range(2):
        weights = load_taps(taps_ref, view, 2 * radius + 1)

        @tiles(0, cols)
        def _(at, _inner):
            def read(r):
                if radius <= r < rows - radius:
                    return middle_ref[view, r - radius, at, :]
                return outer_ref[view, r if r < radius else r - rows + 2 * radius, at, :]

            def write(q, value):
                summed[view, q, at, :] = value

            row_sums(weights, read, write, rows, rows, own_tap_back(radius), 16)

    @pl.loop(0, rows // 4)
    def _(step):
        for pair in range(2):
            at = 4 * step + 2 * pair
            parts = []
            for view in range(2):
                parts += stack(beside(summed[view, at], summed[view, at + 1]))
            total = multiply(back_ref[...], jnp.concatenate(parts, axis=0))
            for half in range(2):
                lanes = slice(half * depth, (half + 1) * depth)
                main_ref[at + half] = total[:width, lanes]
                edge_ref[at + half] = total[width : width + edge_ref.shape[1], lanes]


def back(outer, middle, weights, radius):
    _, _, cols, depth = outer.shape
    rows = outer.shape[1] + middle.shape[1]
    return call(
        functools.partial(back_kernel, radius), "back",
        (shape(rows, cols - 2 * EDGE, depth), shape(rows, edge_width(radius), depth)),
        1 << 32, 12 * rows * cols * depth,
        [pltpu.VMEM((2, rows, cols, depth), F32)],
    )(outer, middle, weights[0], weights[4])


def finish_kernel(radius, main_ref, sum_ref, low_ref, high_ref, edge_ref, edge_sum_ref,
                  from_low_ref, from_high_ref, out_ref, totals):
    rows, cols, _ = out_ref.shape
    width = cols - 2 * EDGE
    rims = (low_ref, high_ref)

    def row_of(row, rim):
        total = sum_ref[row]
        if rim is not None:
            total = total + rims[rim[0]][rim[1], 0:width]
        out_ref[row, EDGE : cols - EDGE] = main_ref[row] * (total * 0.5)
        totals[row] = edge_sum_ref[row, 0 : 2 * EDGE]
        add_y(radius, totals.at[row], row, from_low_ref, from_high_ref)
        out_ref[row, 0:EDGE] = edge_ref[row, 0:EDGE] * (totals[row, 0:EDGE] * 0.5)
        out_ref[row, cols - EDGE :] = edge_ref[row, EDGE : 2 * EDGE] * (totals[row, EDGE:] * 0.5)

    each_row(rows, radius, row_of)


def finish(main, main_sum, low, high, edge, edge_sum, from_low, from_high, radius):
    rows, width, depth = main.shape
    return call(
        functools.partial(finish_kernel, radius), "finish", shape(rows, width + 2 * EDGE, depth),
        1, 1 << 22, [pltpu.VMEM((rows, 2 * EDGE, depth), F32)],
    )(main, main_sum, low, high, edge, edge_sum, from_low, from_high)


def swap(to_next, to_previous, axis):
    count = lax.axis_size(axis)
    forward = [(i, i + 1) for i in range(count - 1)]
    backward = [(i + 1, i) for i in range(count - 1)]
    return lax.ppermute(to_next, axis, forward), lax.ppermute(to_previous, axis, backward)


def local(estimate, view_one, view_two, psf_one, psf_two):
    rows, cols, depth = estimate.shape
    radius = (psf_one.shape[1] - 1) // 2
    from_low, from_high = swap(estimate[:, cols - radius :], estimate[:, :radius], "gy")
    weights = make_weights(psf_one, psf_two, cols, depth)
    inner, near = forward_first(estimate, weights, radius)
    from_low, from_high, near = lax.optimization_barrier((from_low, from_high, near))
    edge, to_low, to_high = edge_first(estimate, from_low, from_high, radius)
    main, base = estimate, EDGE
    for step in range(ITERS):
        low, high = swap(to_high, to_low, "gx")
        near, middle = forward_edge(edge, inner, near, view_one, view_two, weights, radius)
        rim_low, rim_high, outer = ratios(low, high, inner, near, view_one, view_two, weights, radius)
        low, high = swap(rim_high, rim_low, "gx")
        main_sum, edge_sum = back(outer, middle, weights, radius)
        last = step == ITERS - 1
        edge_sum, to_next, to_previous = y_messages(edge_sum, low, high, not last, radius)
        from_low, from_high = swap(to_next, to_previous, "gy")
        if not last:
            main, inner, near = forward_next(main, base, main_sum, low, high, weights, radius)
            base = 0
            from_low, from_high, near = lax.optimization_barrier((from_low, from_high, near))
            edge, to_low, to_high = edge_next(edge, edge_sum, from_low, from_high, main, radius)
    return finish(main, main_sum, low, high, edge, edge_sum, from_low, from_high, radius)


def solution(mesh):
    in_specs = (P("gx", "gy", None), P("gx", "gy", None), P("gx", "gy", None), P(), P())
    out_specs = P("gx", "gy", None)
    return jax.shard_map(local, mesh=mesh, in_specs=in_specs, out_specs=out_specs, check_vma=False)
```

```python
import functools
import jax
import jax.numpy as jnp
from jax import lax
from jax.experimental import pallas as pl
from jax.experimental.pallas import tpu as pltpu
from jax.sharding import PartitionSpec as P

ITERS = 2
F32 = jnp.float32
BF16 = jnp.bfloat16
LIMIT = 24 * 1024 * 1024
WIDE_LIMIT = 50 * 1024 * 1024
EDGE = 16
NEAR = 32


def round_up(value, unit):
    return (value + unit - 1) // unit * unit


def edge_width(radius):
    return 2 * EDGE + round_up(2 * radius, 8)


def split(value):
    high = value.astype(BF16)
    low = (value - high.astype(F32)).astype(BF16)
    return high, low


def stack(value):
    high, low = split(value)
    return [high, low, high]


def multiply(weights, value):
    return jnp.dot(weights, value, preferred_element_type=F32)


def call(kernel, name, out_shape, flops, moved, scratch=(), in_specs=None, limit=LIMIT):
    extra = {} if in_specs is None else {"in_specs": in_specs}
    return pl.pallas_call(
        kernel,
        out_shape=out_shape,
        **extra,
        scratch_shapes=list(scratch),
        compiler_params=pltpu.CompilerParams(vmem_limit_bytes=limit),
        cost_estimate=pl.CostEstimate(flops=flops, bytes_accessed=moved, transcendentals=0),
        name=name,
    )


def shape(*dims, dtype=F32):
    return jax.ShapeDtypeStruct(dims, dtype)


def weights_kernel(cols, psf_ref, taps_ref, main_ref, edge_ref, full_ref, back_ref, zf_ref, zb_ref):
    taps = psf_ref.shape[1]
    radius = (taps - 1) // 2
    depth = zf_ref.shape[1] // 2
    main = cols - 2 * EDGE
    edge = round_up(edge_width(radius), 16)
    rows = psf_ref[...] / jnp.sum(psf_ref[...], axis=1, keepdims=True)
    one, two = rows[0:3], rows[3:6]
    x_rows = (one[0:1], two[1:2])
    y_rows = (one[1:2], two[0:1])
    z_rows = (one[2:3], two[2:3])
    pitch = taps_ref.shape[0] // 2
    taps_ref[...] = jnp.zeros_like(taps_ref)
    for view in range(2):
        for tap in range(taps):
            taps_ref[view * pitch + tap : view * pitch + tap + 1, :] = jnp.broadcast_to(
                x_rows[view][:, tap : tap + 1], (1, taps_ref.shape[1])
            )

    def iota(dims, dim):
        return lax.broadcasted_iota(jnp.int32, dims, dim)

    def band(row, offset):
        total = jnp.zeros(offset.shape, F32)
        for tap in range(taps):
            total = jnp.where(offset == tap, row[:, tap : tap + 1], total)
        return total

    def edge_place(index):
        place = jnp.where(index < EDGE, index, index + cols - 2 * EDGE)
        place = jnp.where(index >= 2 * EDGE, index - 2 * EDGE - radius, place)
        place = jnp.where(index >= 2 * EDGE + radius, index - 2 * EDGE - radius + cols, place)
        return jnp.where(index >= 2 * EDGE + 2 * radius, 8 * cols, place)

    def laid(value):
        high, low = split(value)
        return jnp.concatenate([high, high, low], axis=1)

    for view in range(2):
        row = y_rows[view]
        rows = pl.ds(view * cols, cols)
        dims = (cols, main)
        left = laid(band(row, iota(dims, 0) - (iota(dims, 1) + EDGE) + radius))
        dims = (cols, edge)
        right = laid(band(row, iota(dims, 0) - edge_place(iota(dims, 1)) + radius))
        main_ref[rows, :] = left
        edge_ref[rows, :] = right
        full_ref[rows, :] = jnp.concatenate([left, right], axis=1)
        part = slice(3 * cols * view, 3 * cols * (view + 1))
        dims = (main, cols)
        back_ref[0:main, part] = laid(band(row, iota(dims, 1) - (iota(dims, 0) + EDGE) + radius))
        dims = (edge, cols)
        back_ref[main:, part] = laid(band(row, iota(dims, 1) - edge_place(iota(dims, 0)) + radius))
        dims = (depth, depth)
        first, second = iota(dims, 0), iota(dims, 1)
        for ref, offset in ((zf_ref, second - first + radius), (zb_ref, first - second + radius)):
            high, low = split(band(z_rows[view], offset))
            both = jnp.concatenate([high, low], axis=1)
            ref[view] = jnp.concatenate([both, both], axis=0)


def make_weights(psf_one, psf_two, cols, depth):
    radius = (psf_one.shape[1] - 1) // 2
    main = cols - 2 * EDGE
    edge = round_up(edge_width(radius), 16)
    return call(
        functools.partial(weights_kernel, cols), "weights",
        (
            shape(48, 128),
            shape(2 * cols, 3 * main, dtype=BF16),
            shape(2 * cols, 3 * edge, dtype=BF16),
            shape(2 * cols, 3 * (main + edge), dtype=BF16),
            shape(main + edge, 6 * cols, dtype=BF16),
            shape(2, 2 * depth, 2 * depth, dtype=BF16),
            shape(2, 2 * depth, 2 * depth, dtype=BF16),
        ), 1 << 22, 1 << 20,
    )(jnp.concatenate([psf_one, psf_two], axis=0))


def pad_rows(value):
    extra = round_up(value.shape[0], 16) - value.shape[0]
    if not extra:
        return value
    return jnp.concatenate([value, jnp.zeros((extra, value.shape[1]), value.dtype)], axis=0)


def beside(first, second):
    return jnp.concatenate([first, second], axis=1)


def depth_pass(value, matrix):
    both = multiply_depth(value, matrix)
    depth = value.shape[1]
    return both[:, :depth] + both[:, depth:]


def multiply_depth(value, matrix):
    high, low = split(value)
    return multiply(jnp.concatenate([high, low], axis=1), matrix)


def load_taps(taps_ref, view, taps):
    pitch = taps_ref.shape[0] // 2
    return [
        jnp.broadcast_to(taps_ref[view * pitch + tap : view * pitch + tap + 1, :], (8, 128))
        for tap in range(taps)
    ]


def row_sums(weights, read, write, sources, targets, tap_of, block):
    taps = len(weights)
    for start in range(0, targets, block):
        outs = range(start, min(start + block, targets))
        totals = {}
        for r in range(sources):
            used = [q for q in outs if 0 <= tap_of(q, r) < taps]
            if not used:
                continue
            value = read(r)
            for q in used:
                term = weights[tap_of(q, r)] * value
                totals[q] = totals[q] + term if q in totals else term
        for q in outs:
            write(q, totals[q])


def tiles(start, stop):
    def run(body):
        @pl.loop(0, (stop - start) // 8)
        def _(tile):
            inner = pl.multiple_of(tile * 8, 8)
            body(pl.ds(pl.multiple_of(start + inner, 8), 8), pl.ds(inner, 8))
    return run


def own_tap_forward(radius):
    return lambda q, r: q + radius - r


def own_tap_back(radius):
    return lambda q, r: r - q + radius


def sides():
    odd = lax.rem(lax.axis_index("gx"), 2)
    return odd, 1 - odd


def each_row(rows, radius, body):
    starts = [side * (rows - radius) for side in sides()]

    @pl.loop(0, radius // 2)
    def _(step):
        for k in range(2):
            row = 2 * step + k
            for which, start in enumerate(starts):
                body(start + row, (which, row))

    @pl.loop(0, (rows - 2 * radius) // 2)
    def _(step):
        for k in range(2):
            body(radius + 2 * step + k, None)


def main_pass(radius, rows, read, taps_ref, main_ref, inner_ref, near_ref, passed):
    cols = main_ref.shape[0] // 2
    depth = passed.shape[3]

    @pl.loop(0, rows // 4)
    def _(step):
        for pair in range(2):
            at = 4 * step + 2 * pair
            value = beside(read(at), read(at + 1))
            both = multiply(main_ref[...], jnp.concatenate(stack(value), axis=0))
            for view in range(2):
                for half in range(2):
                    block = both[view * cols : (view + 1) * cols, half * depth : (half + 1) * depth]
                    passed[view, at + half] = block[NEAR : cols - NEAR]
                    near_ref[view, at + half, 0:NEAR] = block[:NEAR]
                    near_ref[view, at + half, NEAR:] = block[cols - NEAR :]

    for view in range(2):
        weights = load_taps(taps_ref, view, 2 * radius + 1)

        @tiles(0, cols - 2 * NEAR)
        def _(at, _inner):
            def write(q, value):
                inner_ref[view, q, at, :] = value

            row_sums(weights, lambda r: passed[view, r, at, :], write, rows, rows,
                     own_tap_forward(radius), 16)


def load_kernel(radius, source_ref, current_ref, next_ref, previous_ref, arrived):
    rows, cols, _ = current_ref.shape

    def copy(block):
        part = pl.ds(4 * block, 4)
        return pltpu.make_async_copy(source_ref.at[part], current_ref.at[part], arrived.at[block])

    for block in range(rows // 4):
        copy(block).start()

    @pl.loop(0, rows // 4)
    def _(block):
        copy(block).wait()
        for k in range(4):
            row = 4 * block + k
            next_ref[row] = current_ref[row, cols - radius :]
            previous_ref[row] = current_ref[row, 0:radius]


def load(estimate, radius):
    rows, cols, depth = estimate.shape
    sent = shape(rows, radius, depth)
    return call(
        functools.partial(load_kernel, radius), "load", (shape(rows, cols, depth), sent, sent),
        1, 1 << 22, [pltpu.SemaphoreType.DMA((rows // 4,))],
        [pl.BlockSpec(memory_space=pltpu.HBM)], WIDE_LIMIT)(estimate)


def forward_first_kernel(radius, current_ref, taps_ref, main_ref, inner_ref, near_ref, passed):
    rows, cols, _ = current_ref.shape
    main_pass(radius, rows, lambda row: current_ref[row, EDGE : cols - EDGE],
              taps_ref, main_ref, inner_ref, near_ref, passed)


def forward_next_kernel(radius, base, current_ref, sum_ref, across_ref, inside_ref, taps_ref, main_ref,
                        next_ref, inner_ref, near_ref, passed):
    rows, width, _ = sum_ref.shape
    rims = (across_ref, inside_ref)

    def update(row, rim):
        total = sum_ref[row]
        if rim is not None:
            total = total + rims[rim[0]][rim[1], 0:width]
        next_ref[row] = current_ref[row, base : base + width] * (total * 0.5)

    each_row(rows, radius, update)
    main_pass(radius, rows, lambda row: next_ref[row], taps_ref, main_ref, inner_ref, near_ref, passed)


def forward_shapes(rows, cols, depth):
    return (
        (shape(2, rows, cols - 2 * NEAR, depth), shape(2, rows, 2 * NEAR, depth)),
        [pltpu.VMEM((2, rows, cols - 2 * NEAR, depth), F32)],
    )


def forward_first(current, weights, radius):
    rows, cols, depth = current.shape
    outs, scratch = forward_shapes(rows, cols, depth)
    return call(
        functools.partial(forward_first_kernel, radius), "forward_first",
        outs, 1 << 31, 12 * rows * cols * depth, scratch,
    )(current, weights[0], weights[1])


def forward_next(current, base, main_sum, low, high, weights, radius):
    rows, width, depth = main_sum.shape
    outs, scratch = forward_shapes(rows, width + 2 * EDGE, depth)
    return call(
        functools.partial(forward_next_kernel, radius, base), "forward_next",
        (shape(rows, width, depth),) + outs, 1 << 31, 12 * rows * width * depth, scratch,
    )(current, main_sum, low, high, weights[0], weights[1])


def write_messages(radius, main_row, edge_ref, across_ref, inside_ref):
    rows = edge_ref.shape[0]
    width = across_ref.shape[1] - edge_ref.shape[1]
    starts = [side * (rows - radius) for side in sides()]

    @pl.loop(0, radius // 2)
    def _(step):
        for k in range(2):
            row = 2 * step + k
            for ref, start in zip((across_ref, inside_ref), starts):
                ref[row, 0:width] = main_row(start + row)
                ref[row, width:] = edge_ref[start + row]


def edge_first_kernel(radius, current_ref, from_low_ref, from_high_ref, edge_ref, across_ref, inside_ref):
    rows, cols, depth = current_ref.shape
    rims = 2 * EDGE

    @pl.loop(0, rows)
    def _(row):
        edge_ref[row, 0:EDGE] = current_ref[row, 0:EDGE]
        edge_ref[row, EDGE:rims] = current_ref[row, cols - EDGE :]
        edge_ref[row, edge_ref.shape[1] - 8 :] = jnp.zeros((8, depth), F32)
        edge_ref[row, rims : rims + radius] = from_low_ref[row]
        edge_ref[row, rims + radius : rims + 2 * radius] = from_high_ref[row]

    write_messages(radius, lambda at: current_ref[at, EDGE : cols - EDGE], edge_ref, across_ref, inside_ref)


def add_y(radius, total_ref, row, from_low_ref, from_high_ref):
    rims = 2 * EDGE
    total_ref[0:radius] = total_ref[0:radius] + from_low_ref[row, 0:radius]
    total_ref[rims - radius : rims] = total_ref[rims - radius : rims] + from_high_ref[row, 0:radius]
    if from_low_ref.shape[1] > radius:
        low, high = slice(rims, rims + radius), slice(rims + radius, rims + 2 * radius)
        total_ref[low] = total_ref[low] + from_low_ref[row, radius:]
        total_ref[high] = total_ref[high] + from_high_ref[row, radius:]


def edge_next_kernel(radius, edge_ref, sum_ref, from_low_ref, from_high_ref, main_ref,
                     next_ref, across_ref, inside_ref, totals):
    @pl.loop(0, edge_ref.shape[0])
    def _(row):
        totals[row] = sum_ref[row]
        add_y(radius, totals.at[row], row, from_low_ref, from_high_ref)
        next_ref[row] = edge_ref[row] * (totals[row] * 0.5)

    write_messages(radius, lambda at: main_ref[at], next_ref, across_ref, inside_ref)


def edge_shapes(rows, cols, depth, radius):
    wide = cols - 2 * EDGE + edge_width(radius)
    return (shape(rows, edge_width(radius), depth), shape(radius, wide, depth), shape(radius, wide, depth))


def edge_first(current, from_low, from_high, radius):
    outs = edge_shapes(*current.shape, radius)
    return call(functools.partial(edge_first_kernel, radius), "edge_first", outs, 1, 1 << 22)(
        current, from_low, from_high)


def edge_next(edge, edge_sum, from_low, from_high, main, radius):
    rows, width, depth = main.shape
    outs = edge_shapes(rows, width + 2 * EDGE, depth, radius)
    return call(
        functools.partial(edge_next_kernel, radius), "edge_next", outs, 1, 1 << 22,
        [pltpu.VMEM(edge.shape, F32)])(edge, edge_sum, from_low, from_high, main)


def y_messages_kernel(radius, whole, edge_ref, across_ref, inside_ref, sum_ref, next_ref, previous_ref):
    rows, width, _ = edge_ref.shape
    before = across_ref.shape[1] - width
    refs = (across_ref, inside_ref)
    rims = 2 * EDGE

    def row_of(row, rim):
        total = edge_ref[row]
        if rim is not None:
            total = total + refs[rim[0]][rim[1], before:]
        sum_ref[row] = total
        previous_ref[row, 0:radius] = sum_ref[row, rims : rims + radius]
        next_ref[row, 0:radius] = sum_ref[row, rims + radius : rims + 2 * radius]
        if whole:
            previous_ref[row, radius:] = sum_ref[row, 0:radius]
            next_ref[row, radius:] = sum_ref[row, rims - radius : rims]

    each_row(rows, radius, row_of)


def y_messages(edge_sum, low, high, whole, radius):
    rows, width, depth = edge_sum.shape
    sent = shape(rows, 2 * radius if whole else radius, depth)
    return call(
        functools.partial(y_messages_kernel, radius, whole), "y_messages",
        (shape(rows, width, depth), sent, sent), 1, 1 << 22)(edge_sum, low, high)


def ratio_block(values, seen, zf_ref, zb_ref, view):
    blurred = depth_pass(values, zf_ref[view])
    return depth_pass(seen / blurred, zb_ref[view])


def forward_edge_kernel(radius, current_ref, inner_ref, before_ref, one_ref, two_ref, taps_ref, edge_ref,
                        zf_ref, zb_ref, near_ref, middle_ref, passed):
    rows, cols, depth = one_ref.shape
    kept = jnp.concatenate(
        [edge_ref[start : start + NEAR] for start in (0, cols - NEAR, cols, 2 * cols - NEAR)], axis=0)

    @pl.loop(0, rows // 4)
    def _(step):
        for pair in range(2):
            at = 4 * step + 2 * pair
            value = pad_rows(beside(current_ref[at], current_ref[at + 1]))
            both = multiply(kept, jnp.concatenate(stack(value), axis=0))
            for view in range(2):
                for half in range(2):
                    passed[view, at + half] = before_ref[view, at + half] + both[
                        2 * NEAR * view : 2 * NEAR * (view + 1), half * depth : (half + 1) * depth]

    for view in range(2):
        weights = load_taps(taps_ref, view, 2 * radius + 1)

        @tiles(0, 2 * NEAR)
        def _(at, _inner):
            def write(q, value):
                near_ref[view, q, at, :] = value

            row_sums(weights, lambda r: passed[view, r, at, :], write, rows, rows,
                     own_tap_forward(radius), 16)

    @pl.loop(0, (rows - 2 * radius) // 2)
    def _(step):
        at = 2 * step
        for view, seen in ((0, one_ref), (1, two_ref)):
            parts = []
            for row in (radius + at, radius + at + 1):
                parts += [near_ref[view, row, 0:NEAR], inner_ref[view, row], near_ref[view, row, NEAR:]]
            value = ratio_block(
                jnp.concatenate(parts, axis=0), seen[pl.ds(radius + at, 2)].reshape(2 * cols, depth),
                zf_ref, zb_ref, view)
            middle_ref[view, pl.ds(at, 2)] = value.reshape(2, cols, depth)


def forward_edge(current, inner, before, one, two, weights, radius):
    taps, _, edge, _, _, zf, zb = weights
    rows, cols, depth = one.shape
    return call(
        functools.partial(forward_edge_kernel, radius), "forward_edge",
        (shape(2, rows, 2 * NEAR, depth), shape(2, rows - 2 * radius, cols, depth)),
        1 << 31, 24 * rows * NEAR * depth,
        [pltpu.VMEM((2, rows, 2 * NEAR, depth), F32)],
    )(current, inner, before, one, two, taps, edge, zf, zb)


def ratio_kernel(radius, across_ref, inside_ref, inner_ref, near_ref, one_ref, two_ref, taps_ref, full_ref,
                 back_ref, zf_ref, zb_ref, rim_across_ref, rim_inside_ref, outer_ref, halo, edges):
    rows, cols, depth = one_ref.shape
    main = cols - 2 * EDGE
    taps = 2 * radius + 1

    @pl.loop(0, radius // 2)
    def _(step):
        at = 2 * step
        for side, ref in zip(sides(), (across_ref, inside_ref)):
            left = beside(ref[at, 0:main], ref[at + 1, 0:main])
            right = pad_rows(beside(ref[at, main:], ref[at + 1, main:]))
            both = multiply(full_ref[...], jnp.concatenate(stack(left) + stack(right), axis=0))
            for view in range(2):
                for half in range(2):
                    halo[view, side * radius + at + half] = both[
                        view * cols : (view + 1) * cols, half * depth : (half + 1) * depth]

    for view in range(2):
        weights = load_taps(taps_ref, view, taps)
        for ref, start, stop, shift in (
            (near_ref, 0, NEAR, 0), (inner_ref, NEAR, cols - NEAR, 0),
            (near_ref, cols - NEAR, cols, NEAR),
        ):
            @tiles(start, stop)
            def _(at, inner):
                own = pl.ds(pl.multiple_of(inner.start + shift, 8), 8)

                def write_low(q, value):
                    edges[view, q, at, :] = value + ref[view, q, own, :]

                def write_high(q, value):
                    edges[view, radius + q, at, :] = value + ref[view, rows - radius + q, own, :]

                row_sums(weights, lambda r: halo[view, r, at, :], write_low, radius, radius,
                         lambda q, r: q + 2 * radius - r, radius)
                row_sums(weights, lambda r: halo[view, radius + r, at, :], write_high, radius, radius,
                         lambda q, r: q - r, radius)

    @pl.loop(0, radius // 2)
    def _(step):
        at = 2 * step
        for base, start in ((0, 0), (radius, rows - radius)):
            for view, seen in ((0, one_ref), (1, two_ref)):
                value = ratio_block(
                    edges[view, pl.ds(base + at, 2)].reshape(2 * cols, depth),
                    seen[pl.ds(start + at, 2)].reshape(2 * cols, depth), zf_ref, zb_ref, view)
                outer_ref[view, pl.ds(base + at, 2)] = value.reshape(2, cols, depth)

    for view in range(2):
        weights = load_taps(taps_ref, view, taps)

        @tiles(0, cols)
        def _(at, _inner):
            def write_low(q, value):
                halo[view, q, at, :] = value

            def write_high(q, value):
                halo[view, radius + q, at, :] = value

            row_sums(weights, lambda r: outer_ref[view, r, at, :], write_low, radius, radius,
                     lambda q, r: r - q + 2 * radius, radius)
            row_sums(weights, lambda r: outer_ref[view, radius + r, at, :], write_high,
                     radius, radius, lambda q, r: r - q, radius)

    @pl.loop(0, radius // 2)
    def _(step):
        at = 2 * step
        for side, ref in zip(sides(), (rim_across_ref, rim_inside_ref)):
            base = side * radius
            parts = []
            for view in range(2):
                parts += stack(beside(halo[view, base + at], halo[view, base + at + 1]))
            total = multiply(back_ref[...], jnp.concatenate(parts, axis=0))
            for half in range(2):
                ref[at + half] = total[: ref.shape[1], half * depth : (half + 1) * depth]


def ratios(low, high, inner, near, one, two, weights, radius):
    taps, _, _, full, back, zf, zb = weights
    rows, cols, depth = one.shape
    wide = low.shape[1]
    return call(
        functools.partial(ratio_kernel, radius), "ratios",
        (shape(radius, wide, depth), shape(radius, wide, depth), shape(2, 2 * radius, cols, depth)),
        1 << 33, 24 * rows * cols * depth,
        [pltpu.VMEM((2, 2 * radius, cols, depth), F32)] * 2,
    )(low, high, inner, near, one, two, taps, full, back, zf, zb)


def back_kernel(radius, outer_ref, middle_ref, taps_ref, back_ref, main_ref, edge_ref, summed):
    rows = main_ref.shape[0]
    width = main_ref.shape[1]
    depth = main_ref.shape[2]
    cols = outer_ref.shape[2]
    for view in range(2):
        weights = load_taps(taps_ref, view, 2 * radius + 1)

        @tiles(0, cols)
        def _(at, _inner):
            def read(r):
                if radius <= r < rows - radius:
                    return middle_ref[view, r - radius, at, :]
                return outer_ref[view, r if r < radius else r - rows + 2 * radius, at, :]

            def write(q, value):
                summed[view, q, at, :] = value

            row_sums(weights, read, write, rows, rows, own_tap_back(radius), 16)

    @pl.loop(0, rows // 4)
    def _(step):
        for pair in range(2):
            at = 4 * step + 2 * pair
            parts = []
            for view in range(2):
                parts += stack(beside(summed[view, at], summed[view, at + 1]))
            total = multiply(back_ref[...], jnp.concatenate(parts, axis=0))
            for half in range(2):
                lanes = slice(half * depth, (half + 1) * depth)
                main_ref[at + half] = total[:width, lanes]
                edge_ref[at + half] = total[width : width + edge_ref.shape[1], lanes]


def back(outer, middle, weights, radius):
    _, _, cols, depth = outer.shape
    rows = outer.shape[1] + middle.shape[1]
    return call(
        functools.partial(back_kernel, radius), "back",
        (shape(rows, cols - 2 * EDGE, depth), shape(rows, edge_width(radius), depth)),
        1 << 32, 12 * rows * cols * depth,
        [pltpu.VMEM((2, rows, cols, depth), F32)],
    )(outer, middle, weights[0], weights[4])


def finish_kernel(radius, main_ref, sum_ref, across_ref, inside_ref, edge_ref, edge_sum_ref,
                  from_low_ref, from_high_ref, out_ref, totals):
    rows, cols, _ = out_ref.shape
    width = cols - 2 * EDGE
    rims = (across_ref, inside_ref)

    def row_of(row, rim):
        total = sum_ref[row]
        if rim is not None:
            total = total + rims[rim[0]][rim[1], 0:width]
        out_ref[row, EDGE : cols - EDGE] = main_ref[row] * (total * 0.5)
        totals[row] = edge_sum_ref[row, 0 : 2 * EDGE]
        add_y(radius, totals.at[row], row, from_low_ref, from_high_ref)
        out_ref[row, 0:EDGE] = edge_ref[row, 0:EDGE] * (totals[row, 0:EDGE] * 0.5)
        out_ref[row, cols - EDGE :] = edge_ref[row, EDGE : 2 * EDGE] * (totals[row, EDGE:] * 0.5)

    each_row(rows, radius, row_of)


def finish(main, main_sum, low, high, edge, edge_sum, from_low, from_high, radius):
    rows, width, depth = main.shape
    return call(
        functools.partial(finish_kernel, radius), "finish", shape(rows, width + 2 * EDGE, depth),
        1, 1 << 22, [pltpu.VMEM((rows, 2 * EDGE, depth), F32)],
    )(main, main_sum, low, high, edge, edge_sum, from_low, from_high)


def swap(to_next, to_previous, axis):
    count = lax.axis_size(axis)
    forward = [(i, i + 1) for i in range(count - 1)]
    backward = [(i + 1, i) for i in range(count - 1)]
    return lax.ppermute(to_next, axis, forward), lax.ppermute(to_previous, axis, backward)


def swap_pairs(across, inside, axis):
    count = lax.axis_size(axis)

    def pairs(first):
        return [pair for i in range(first, count - 1, 2) for pair in ((i, i + 1), (i + 1, i))]

    return lax.ppermute(across, axis, pairs(1)), lax.ppermute(inside, axis, pairs(0))


def local(estimate, view_one, view_two, psf_one, psf_two):
    rows, cols, depth = estimate.shape
    radius = (psf_one.shape[1] - 1) // 2
    main, to_next, to_previous = load(estimate, radius)
    from_low, from_high = swap(to_next, to_previous, "gy")
    weights = make_weights(psf_one, psf_two, cols, depth)
    inner, near = forward_first(main, weights, radius)
    base = EDGE
    from_low, from_high, near = lax.optimization_barrier((from_low, from_high, near))
    edge, across, inside = edge_first(main, from_low, from_high, radius)
    for step in range(ITERS):
        from_across, from_inside = swap_pairs(across, inside, "gx")
        near, middle = forward_edge(edge, inner, near, view_one, view_two, weights, radius)
        across, inside, outer = ratios(from_across, from_inside, inner, near, view_one, view_two, weights, radius)
        from_across, from_inside = swap_pairs(across, inside, "gx")
        main_sum, edge_sum = back(outer, middle, weights, radius)
        last = step == ITERS - 1
        edge_sum, to_next, to_previous = y_messages(edge_sum, from_across, from_inside, not last, radius)
        from_low, from_high = swap(to_next, to_previous, "gy")
        if not last:
            main, inner, near = forward_next(main, base, main_sum, from_across, from_inside, weights, radius)
            base = 0
            from_low, from_high, near = lax.optimization_barrier((from_low, from_high, near))
            edge, across, inside = edge_next(edge, edge_sum, from_low, from_high, main, radius)
    return finish(main, main_sum, from_across, from_inside, edge, edge_sum, from_low, from_high, radius)


def solution(mesh):
    in_specs = (P("gx", "gy", None), P("gx", "gy", None), P("gx", "gy", None), P(), P())
    out_specs = P("gx", "gy", None)
    return jax.shard_map(local, mesh=mesh, in_specs=in_specs, out_specs=out_specs, check_vma=False)
```

```python
import functools
import jax
import jax.numpy as jnp
from jax import lax
from jax.experimental import pallas as pl
from jax.experimental.pallas import tpu as pltpu
from jax.sharding import PartitionSpec as P

ITERS = 2
F32 = jnp.float32
BF16 = jnp.bfloat16
LIMIT = 24 * 1024 * 1024
WIDE_LIMIT = 50 * 1024 * 1024
EDGE = 16
NEAR = 32


def round_up(value, unit):
    return (value + unit - 1) // unit * unit


def edge_width(radius):
    return 2 * EDGE + round_up(2 * radius, 8)


def split(value):
    high = value.astype(BF16)
    low = (value - high.astype(F32)).astype(BF16)
    return high, low


def stack(value):
    high, low = split(value)
    return [high, low, high]


def multiply(weights, value):
    return jnp.dot(weights, value, preferred_element_type=F32)


def call(kernel, name, out_shape, flops, moved, scratch=(), in_specs=None, limit=LIMIT):
    extra = {} if in_specs is None else {"in_specs": in_specs}
    return pl.pallas_call(
        kernel,
        out_shape=out_shape,
        **extra,
        scratch_shapes=list(scratch),
        compiler_params=pltpu.CompilerParams(vmem_limit_bytes=limit),
        cost_estimate=pl.CostEstimate(flops=flops, bytes_accessed=moved, transcendentals=0),
        name=name,
    )


def shape(*dims, dtype=F32):
    return jax.ShapeDtypeStruct(dims, dtype)


def weights_kernel(cols, psf_ref, taps_ref, main_ref, edge_ref, full_ref, back_ref, zf_ref, zb_ref):
    taps = psf_ref.shape[1]
    radius = (taps - 1) // 2
    depth = zf_ref.shape[1] // 2
    main = cols - 2 * EDGE
    edge = round_up(edge_width(radius), 16)
    rows = psf_ref[...] / jnp.sum(psf_ref[...], axis=1, keepdims=True)
    one, two = rows[0:3], rows[3:6]
    x_rows = (one[0:1], two[1:2])
    y_rows = (one[1:2], two[0:1])
    z_rows = (one[2:3], two[2:3])
    pitch = taps_ref.shape[0] // 2
    taps_ref[...] = jnp.zeros_like(taps_ref)
    for view in range(2):
        for tap in range(taps):
            taps_ref[view * pitch + tap : view * pitch + tap + 1, :] = jnp.broadcast_to(
                x_rows[view][:, tap : tap + 1], (1, taps_ref.shape[1])
            )

    def iota(dims, dim):
        return lax.broadcasted_iota(jnp.int32, dims, dim)

    def band(row, offset):
        total = jnp.zeros(offset.shape, F32)
        for tap in range(taps):
            total = jnp.where(offset == tap, row[:, tap : tap + 1], total)
        return total

    def edge_place(index):
        place = jnp.where(index < EDGE, index, index + cols - 2 * EDGE)
        place = jnp.where(index >= 2 * EDGE, index - 2 * EDGE - radius, place)
        place = jnp.where(index >= 2 * EDGE + radius, index - 2 * EDGE - radius + cols, place)
        return jnp.where(index >= 2 * EDGE + 2 * radius, 8 * cols, place)

    def laid(value):
        high, low = split(value)
        return jnp.concatenate([high, high, low], axis=1)

    for view in range(2):
        row = y_rows[view]
        rows = pl.ds(view * cols, cols)
        dims = (cols, main)
        left = laid(band(row, iota(dims, 0) - (iota(dims, 1) + EDGE) + radius))
        dims = (cols, edge)
        right = laid(band(row, iota(dims, 0) - edge_place(iota(dims, 1)) + radius))
        main_ref[rows, :] = left
        edge_ref[rows, :] = right
        full_ref[rows, :] = jnp.concatenate([left, right], axis=1)
        part = slice(3 * cols * view, 3 * cols * (view + 1))
        dims = (main, cols)
        back_ref[0:main, part] = laid(band(row, iota(dims, 1) - (iota(dims, 0) + EDGE) + radius))
        dims = (edge, cols)
        back_ref[main:, part] = laid(band(row, iota(dims, 1) - edge_place(iota(dims, 0)) + radius))
        dims = (depth, depth)
        first, second = iota(dims, 0), iota(dims, 1)
        for ref, offset in ((zf_ref, second - first + radius), (zb_ref, first - second + radius)):
            high, low = split(band(z_rows[view], offset))
            both = jnp.concatenate([high, low], axis=1)
            ref[view] = jnp.concatenate([both, both], axis=0)


def make_weights(psf_one, psf_two, cols, depth):
    radius = (psf_one.shape[1] - 1) // 2
    main = cols - 2 * EDGE
    edge = round_up(edge_width(radius), 16)
    return call(
        functools.partial(weights_kernel, cols), "weights",
        (
            shape(48, 128),
            shape(2 * cols, 3 * main, dtype=BF16),
            shape(2 * cols, 3 * edge, dtype=BF16),
            shape(2 * cols, 3 * (main + edge), dtype=BF16),
            shape(main + edge, 6 * cols, dtype=BF16),
            shape(2, 2 * depth, 2 * depth, dtype=BF16),
            shape(2, 2 * depth, 2 * depth, dtype=BF16),
        ), 1 << 22, 1 << 20,
    )(jnp.concatenate([psf_one, psf_two], axis=0))


def pad_rows(value):
    extra = round_up(value.shape[0], 16) - value.shape[0]
    if not extra:
        return value
    return jnp.concatenate([value, jnp.zeros((extra, value.shape[1]), value.dtype)], axis=0)


def beside(first, second):
    return jnp.concatenate([first, second], axis=1)


def depth_pass(value, matrix):
    both = multiply_depth(value, matrix)
    depth = value.shape[1]
    return both[:, :depth] + both[:, depth:]


def multiply_depth(value, matrix):
    high, low = split(value)
    return multiply(jnp.concatenate([high, low], axis=1), matrix)


def load_taps(taps_ref, view, taps):
    pitch = taps_ref.shape[0] // 2
    return [
        jnp.broadcast_to(taps_ref[view * pitch + tap : view * pitch + tap + 1, :], (8, 128))
        for tap in range(taps)
    ]


def row_sums(weights, read, write, sources, targets, tap_of, block):
    taps = len(weights)
    for start in range(0, targets, block):
        outs = range(start, min(start + block, targets))
        totals = {}
        for r in range(sources):
            used = [q for q in outs if 0 <= tap_of(q, r) < taps]
            if not used:
                continue
            value = read(r)
            for q in used:
                term = weights[tap_of(q, r)] * value
                totals[q] = totals[q] + term if q in totals else term
        for q in outs:
            write(q, totals[q])


def tiles(start, stop):
    def run(body):
        @pl.loop(0, (stop - start) // 8)
        def _(tile):
            inner = pl.multiple_of(tile * 8, 8)
            body(pl.ds(pl.multiple_of(start + inner, 8), 8), pl.ds(inner, 8))
    return run


def own_tap_forward(radius):
    return lambda q, r: q + radius - r


def own_tap_back(radius):
    return lambda q, r: r - q + radius


def sides(axis="gx"):
    odd = lax.rem(lax.axis_index(axis), 2)
    return odd, 1 - odd


def in_order(low, high):
    odd = sides("gy")[0] == 1
    return jnp.where(odd, high, low), jnp.where(odd, low, high)


def each_row(rows, radius, body):
    starts = [side * (rows - radius) for side in sides()]

    @pl.loop(0, radius // 2)
    def _(step):
        for k in range(2):
            row = 2 * step + k
            for which, start in enumerate(starts):
                body(start + row, (which, row))

    @pl.loop(0, (rows - 2 * radius) // 2)
    def _(step):
        for k in range(2):
            body(radius + 2 * step + k, None)


def main_pass(radius, rows, read, taps_ref, main_ref, inner_ref, near_ref, passed):
    cols = main_ref.shape[0] // 2
    depth = passed.shape[3]

    @pl.loop(0, rows // 4)
    def _(step):
        for pair in range(2):
            at = 4 * step + 2 * pair
            value = beside(read(at), read(at + 1))
            both = multiply(main_ref[...], jnp.concatenate(stack(value), axis=0))
            for view in range(2):
                for half in range(2):
                    block = both[view * cols : (view + 1) * cols, half * depth : (half + 1) * depth]
                    passed[view, at + half] = block[NEAR : cols - NEAR]
                    near_ref[view, at + half, 0:NEAR] = block[:NEAR]
                    near_ref[view, at + half, NEAR:] = block[cols - NEAR :]

    for view in range(2):
        weights = load_taps(taps_ref, view, 2 * radius + 1)

        @tiles(0, cols - 2 * NEAR)
        def _(at, _inner):
            def write(q, value):
                inner_ref[view, q, at, :] = value

            row_sums(weights, lambda r: passed[view, r, at, :], write, rows, rows,
                     own_tap_forward(radius), 16)


def load_kernel(radius, source_ref, current_ref, first_ref, second_ref, arrived):
    rows, cols, _ = current_ref.shape

    def copy(block):
        part = pl.ds(4 * block, 4)
        return pltpu.make_async_copy(source_ref.at[part], current_ref.at[part], arrived.at[block])

    for block in range(rows // 4):
        copy(block).start()

    @pl.loop(0, rows // 4)
    def _(block):
        copy(block).wait()
        for k in range(4):
            row = 4 * block + k
            first_ref[row], second_ref[row] = in_order(
                current_ref[row, 0:radius], current_ref[row, cols - radius :])


def load(estimate, radius):
    rows, cols, depth = estimate.shape
    sent = shape(rows, radius, depth)
    return call(
        functools.partial(load_kernel, radius), "load", (shape(rows, cols, depth), sent, sent),
        1, 1 << 22, [pltpu.SemaphoreType.DMA((rows // 4,))],
        [pl.BlockSpec(memory_space=pltpu.HBM)], WIDE_LIMIT)(estimate)


def forward_first_kernel(radius, current_ref, taps_ref, main_ref, inner_ref, near_ref, passed):
    rows, cols, _ = current_ref.shape
    main_pass(radius, rows, lambda row: current_ref[row, EDGE : cols - EDGE],
              taps_ref, main_ref, inner_ref, near_ref, passed)


def forward_next_kernel(radius, base, current_ref, sum_ref, across_ref, inside_ref, taps_ref, main_ref,
                        next_ref, inner_ref, near_ref, passed):
    rows, width, _ = sum_ref.shape
    rims = (across_ref, inside_ref)

    def update(row, rim):
        total = sum_ref[row]
        if rim is not None:
            total = total + rims[rim[0]][rim[1], 0:width]
        next_ref[row] = current_ref[row, base : base + width] * (total * 0.5)

    each_row(rows, radius, update)
    main_pass(radius, rows, lambda row: next_ref[row], taps_ref, main_ref, inner_ref, near_ref, passed)


def forward_shapes(rows, cols, depth):
    return (
        (shape(2, rows, cols - 2 * NEAR, depth), shape(2, rows, 2 * NEAR, depth)),
        [pltpu.VMEM((2, rows, cols - 2 * NEAR, depth), F32)],
    )


def forward_first(current, weights, radius):
    rows, cols, depth = current.shape
    outs, scratch = forward_shapes(rows, cols, depth)
    return call(
        functools.partial(forward_first_kernel, radius), "forward_first",
        outs, 1 << 31, 12 * rows * cols * depth, scratch,
    )(current, weights[0], weights[1])


def forward_next(current, base, main_sum, low, high, weights, radius):
    rows, width, depth = main_sum.shape
    outs, scratch = forward_shapes(rows, width + 2 * EDGE, depth)
    return call(
        functools.partial(forward_next_kernel, radius, base), "forward_next",
        (shape(rows, width, depth),) + outs, 1 << 31, 12 * rows * width * depth, scratch,
    )(current, main_sum, low, high, weights[0], weights[1])


def write_messages(radius, main_row, edge_ref, across_ref, inside_ref):
    rows = edge_ref.shape[0]
    width = across_ref.shape[1] - edge_ref.shape[1]
    starts = [side * (rows - radius) for side in sides()]

    @pl.loop(0, radius // 2)
    def _(step):
        for k in range(2):
            row = 2 * step + k
            for ref, start in zip((across_ref, inside_ref), starts):
                ref[row, 0:width] = main_row(start + row)
                ref[row, width:] = edge_ref[start + row]


def edge_first_kernel(radius, current_ref, first_ref, second_ref, edge_ref, across_ref, inside_ref):
    rows, cols, depth = current_ref.shape
    rims = 2 * EDGE

    @pl.loop(0, rows)
    def _(row):
        edge_ref[row, 0:EDGE] = current_ref[row, 0:EDGE]
        edge_ref[row, EDGE:rims] = current_ref[row, cols - EDGE :]
        edge_ref[row, edge_ref.shape[1] - 8 :] = jnp.zeros((8, depth), F32)
        low, high = in_order(first_ref[row], second_ref[row])
        edge_ref[row, rims : rims + radius] = low
        edge_ref[row, rims + radius : rims + 2 * radius] = high

    write_messages(radius, lambda at: current_ref[at, EDGE : cols - EDGE], edge_ref, across_ref, inside_ref)


def add_y(radius, total_ref, row, first_ref, second_ref):
    rims = 2 * EDGE

    def add(start, value):
        part = slice(start, start + radius)
        total_ref[part] = total_ref[part] + value

    low, high = in_order(first_ref[row, 0:radius], second_ref[row, 0:radius])
    add(0, low)
    add(rims - radius, high)
    if first_ref.shape[1] > radius:
        low, high = in_order(first_ref[row, radius:], second_ref[row, radius:])
        add(rims, low)
        add(rims + radius, high)


def edge_next_kernel(radius, edge_ref, sum_ref, first_ref, second_ref, main_ref,
                     next_ref, across_ref, inside_ref, totals):
    @pl.loop(0, edge_ref.shape[0])
    def _(row):
        totals[row] = sum_ref[row]
        add_y(radius, totals.at[row], row, first_ref, second_ref)
        next_ref[row] = edge_ref[row] * (totals[row] * 0.5)

    write_messages(radius, lambda at: main_ref[at], next_ref, across_ref, inside_ref)


def edge_shapes(rows, cols, depth, radius):
    wide = cols - 2 * EDGE + edge_width(radius)
    return (shape(rows, edge_width(radius), depth), shape(radius, wide, depth), shape(radius, wide, depth))


def edge_first(current, from_low, from_high, radius):
    outs = edge_shapes(*current.shape, radius)
    return call(functools.partial(edge_first_kernel, radius), "edge_first", outs, 1, 1 << 22)(
        current, from_low, from_high)


def edge_next(edge, edge_sum, from_low, from_high, main, radius):
    rows, width, depth = main.shape
    outs = edge_shapes(rows, width + 2 * EDGE, depth, radius)
    return call(
        functools.partial(edge_next_kernel, radius), "edge_next", outs, 1, 1 << 22,
        [pltpu.VMEM(edge.shape, F32)])(edge, edge_sum, from_low, from_high, main)


def y_messages_kernel(radius, whole, edge_ref, across_ref, inside_ref, sum_ref, first_ref, second_ref):
    rows, width, _ = edge_ref.shape
    before = across_ref.shape[1] - width
    refs = (across_ref, inside_ref)
    rims = 2 * EDGE

    def row_of(row, rim):
        total = edge_ref[row]
        if rim is not None:
            total = total + refs[rim[0]][rim[1], before:]
        sum_ref[row] = total
        first_ref[row, 0:radius], second_ref[row, 0:radius] = in_order(
            sum_ref[row, rims : rims + radius], sum_ref[row, rims + radius : rims + 2 * radius])
        if whole:
            first_ref[row, radius:], second_ref[row, radius:] = in_order(
                sum_ref[row, 0:radius], sum_ref[row, rims - radius : rims])

    each_row(rows, radius, row_of)


def y_messages(edge_sum, low, high, whole, radius):
    rows, width, depth = edge_sum.shape
    sent = shape(rows, 2 * radius if whole else radius, depth)
    return call(
        functools.partial(y_messages_kernel, radius, whole), "y_messages",
        (shape(rows, width, depth), sent, sent), 1, 1 << 22)(edge_sum, low, high)


def ratio_block(values, seen, zf_ref, zb_ref, view):
    blurred = depth_pass(values, zf_ref[view])
    return depth_pass(seen / blurred, zb_ref[view])


def forward_edge_kernel(radius, current_ref, inner_ref, before_ref, one_ref, two_ref, taps_ref, edge_ref,
                        zf_ref, zb_ref, near_ref, middle_ref, passed):
    rows, cols, depth = one_ref.shape
    kept = jnp.concatenate(
        [edge_ref[start : start + NEAR] for start in (0, cols - NEAR, cols, 2 * cols - NEAR)], axis=0)

    @pl.loop(0, rows // 4)
    def _(step):
        for pair in range(2):
            at = 4 * step + 2 * pair
            value = pad_rows(beside(current_ref[at], current_ref[at + 1]))
            both = multiply(kept, jnp.concatenate(stack(value), axis=0))
            for view in range(2):
                for half in range(2):
                    passed[view, at + half] = before_ref[view, at + half] + both[
                        2 * NEAR * view : 2 * NEAR * (view + 1), half * depth : (half + 1) * depth]

    for view in range(2):
        weights = load_taps(taps_ref, view, 2 * radius + 1)

        @tiles(0, 2 * NEAR)
        def _(at, _inner):
            def write(q, value):
                near_ref[view, q, at, :] = value

            row_sums(weights, lambda r: passed[view, r, at, :], write, rows, rows,
                     own_tap_forward(radius), 16)

    @pl.loop(0, (rows - 2 * radius) // 2)
    def _(step):
        at = 2 * step
        for view, seen in ((0, one_ref), (1, two_ref)):
            parts = []
            for row in (radius + at, radius + at + 1):
                parts += [near_ref[view, row, 0:NEAR], inner_ref[view, row], near_ref[view, row, NEAR:]]
            value = ratio_block(
                jnp.concatenate(parts, axis=0), seen[pl.ds(radius + at, 2)].reshape(2 * cols, depth),
                zf_ref, zb_ref, view)
            middle_ref[view, pl.ds(at, 2)] = value.reshape(2, cols, depth)


def forward_edge(current, inner, before, one, two, weights, radius):
    taps, _, edge, _, _, zf, zb = weights
    rows, cols, depth = one.shape
    return call(
        functools.partial(forward_edge_kernel, radius), "forward_edge",
        (shape(2, rows, 2 * NEAR, depth), shape(2, rows - 2 * radius, cols, depth)),
        1 << 31, 24 * rows * NEAR * depth,
        [pltpu.VMEM((2, rows, 2 * NEAR, depth), F32)],
    )(current, inner, before, one, two, taps, edge, zf, zb)


def ratio_kernel(radius, across_ref, inside_ref, inner_ref, near_ref, one_ref, two_ref, taps_ref, full_ref,
                 back_ref, zf_ref, zb_ref, rim_across_ref, rim_inside_ref, outer_ref, halo, edges):
    rows, cols, depth = one_ref.shape
    main = cols - 2 * EDGE
    taps = 2 * radius + 1

    @pl.loop(0, radius // 2)
    def _(step):
        at = 2 * step
        for side, ref in zip(sides(), (across_ref, inside_ref)):
            left = beside(ref[at, 0:main], ref[at + 1, 0:main])
            right = pad_rows(beside(ref[at, main:], ref[at + 1, main:]))
            both = multiply(full_ref[...], jnp.concatenate(stack(left) + stack(right), axis=0))
            for view in range(2):
                for half in range(2):
                    halo[view, side * radius + at + half] = both[
                        view * cols : (view + 1) * cols, half * depth : (half + 1) * depth]

    for view in range(2):
        weights = load_taps(taps_ref, view, taps)
        for ref, start, stop, shift in (
            (near_ref, 0, NEAR, 0), (inner_ref, NEAR, cols - NEAR, 0),
            (near_ref, cols - NEAR, cols, NEAR),
        ):
            @tiles(start, stop)
            def _(at, inner):
                own = pl.ds(pl.multiple_of(inner.start + shift, 8), 8)

                def write_low(q, value):
                    edges[view, q, at, :] = value + ref[view, q, own, :]

                def write_high(q, value):
                    edges[view, radius + q, at, :] = value + ref[view, rows - radius + q, own, :]

                row_sums(weights, lambda r: halo[view, r, at, :], write_low, radius, radius,
                         lambda q, r: q + 2 * radius - r, radius)
                row_sums(weights, lambda r: halo[view, radius + r, at, :], write_high, radius, radius,
                         lambda q, r: q - r, radius)

    @pl.loop(0, radius // 2)
    def _(step):
        at = 2 * step
        for base, start in ((0, 0), (radius, rows - radius)):
            for view, seen in ((0, one_ref), (1, two_ref)):
                value = ratio_block(
                    edges[view, pl.ds(base + at, 2)].reshape(2 * cols, depth),
                    seen[pl.ds(start + at, 2)].reshape(2 * cols, depth), zf_ref, zb_ref, view)
                outer_ref[view, pl.ds(base + at, 2)] = value.reshape(2, cols, depth)

    for view in range(2):
        weights = load_taps(taps_ref, view, taps)

        @tiles(0, cols)
        def _(at, _inner):
            def write_low(q, value):
                halo[view, q, at, :] = value

            def write_high(q, value):
                halo[view, radius + q, at, :] = value

            row_sums(weights, lambda r: outer_ref[view, r, at, :], write_low, radius, radius,
                     lambda q, r: r - q + 2 * radius, radius)
            row_sums(weights, lambda r: outer_ref[view, radius + r, at, :], write_high,
                     radius, radius, lambda q, r: r - q, radius)

    @pl.loop(0, radius // 2)
    def _(step):
        at = 2 * step
        for side, ref in zip(sides(), (rim_across_ref, rim_inside_ref)):
            base = side * radius
            parts = []
            for view in range(2):
                parts += stack(beside(halo[view, base + at], halo[view, base + at + 1]))
            total = multiply(back_ref[...], jnp.concatenate(parts, axis=0))
            for half in range(2):
                ref[at + half] = total[: ref.shape[1], half * depth : (half + 1) * depth]


def ratios(low, high, inner, near, one, two, weights, radius):
    taps, _, _, full, back, zf, zb = weights
    rows, cols, depth = one.shape
    wide = low.shape[1]
    return call(
        functools.partial(ratio_kernel, radius), "ratios",
        (shape(radius, wide, depth), shape(radius, wide, depth), shape(2, 2 * radius, cols, depth)),
        1 << 33, 24 * rows * cols * depth,
        [pltpu.VMEM((2, 2 * radius, cols, depth), F32)] * 2,
    )(low, high, inner, near, one, two, taps, full, back, zf, zb)


def back_kernel(radius, outer_ref, middle_ref, taps_ref, back_ref, main_ref, edge_ref, summed):
    rows = main_ref.shape[0]
    width = main_ref.shape[1]
    depth = main_ref.shape[2]
    cols = outer_ref.shape[2]
    for view in range(2):
        weights = load_taps(taps_ref, view, 2 * radius + 1)

        @tiles(0, cols)
        def _(at, _inner):
            def read(r):
                if radius <= r < rows - radius:
                    return middle_ref[view, r - radius, at, :]
                return outer_ref[view, r if r < radius else r - rows + 2 * radius, at, :]

            def write(q, value):
                summed[view, q, at, :] = value

            row_sums(weights, read, write, rows, rows, own_tap_back(radius), 16)

    @pl.loop(0, rows // 4)
    def _(step):
        for pair in range(2):
            at = 4 * step + 2 * pair
            parts = []
            for view in range(2):
                parts += stack(beside(summed[view, at], summed[view, at + 1]))
            total = multiply(back_ref[...], jnp.concatenate(parts, axis=0))
            for half in range(2):
                lanes = slice(half * depth, (half + 1) * depth)
                main_ref[at + half] = total[:width, lanes]
                edge_ref[at + half] = total[width : width + edge_ref.shape[1], lanes]


def back(outer, middle, weights, radius):
    _, _, cols, depth = outer.shape
    rows = outer.shape[1] + middle.shape[1]
    return call(
        functools.partial(back_kernel, radius), "back",
        (shape(rows, cols - 2 * EDGE, depth), shape(rows, edge_width(radius), depth)),
        1 << 32, 12 * rows * cols * depth,
        [pltpu.VMEM((2, rows, cols, depth), F32)],
    )(outer, middle, weights[0], weights[4])


def finish_kernel(radius, main_ref, sum_ref, across_ref, inside_ref, edge_ref, edge_sum_ref,
                  first_ref, second_ref, out_ref, totals):
    rows, cols, _ = out_ref.shape
    width = cols - 2 * EDGE
    rims = (across_ref, inside_ref)

    def row_of(row, rim):
        total = sum_ref[row]
        if rim is not None:
            total = total + rims[rim[0]][rim[1], 0:width]
        out_ref[row, EDGE : cols - EDGE] = main_ref[row] * (total * 0.5)
        totals[row] = edge_sum_ref[row, 0 : 2 * EDGE]
        add_y(radius, totals.at[row], row, first_ref, second_ref)
        out_ref[row, 0:EDGE] = edge_ref[row, 0:EDGE] * (totals[row, 0:EDGE] * 0.5)
        out_ref[row, cols - EDGE :] = edge_ref[row, EDGE : 2 * EDGE] * (totals[row, EDGE:] * 0.5)

    each_row(rows, radius, row_of)


def finish(main, main_sum, low, high, edge, edge_sum, from_low, from_high, radius):
    rows, width, depth = main.shape
    return call(
        functools.partial(finish_kernel, radius), "finish", shape(rows, width + 2 * EDGE, depth),
        1, 1 << 22, [pltpu.VMEM((rows, 2 * EDGE, depth), F32)],
    )(main, main_sum, low, high, edge, edge_sum, from_low, from_high)


def swap_pairs(first, second, axis):
    count = lax.axis_size(axis)

    def pairs(start):
        return [pair for i in range(start, count - 1, 2) for pair in ((i, i + 1), (i + 1, i))]

    return lax.ppermute(first, axis, pairs(1)), lax.ppermute(second, axis, pairs(0))


def local(estimate, view_one, view_two, psf_one, psf_two):
    rows, cols, depth = estimate.shape
    radius = (psf_one.shape[1] - 1) // 2
    main, first, second = load(estimate, radius)
    first, second = swap_pairs(first, second, "gy")
    weights = make_weights(psf_one, psf_two, cols, depth)
    inner, near = forward_first(main, weights, radius)
    base = EDGE
    first, second, near = lax.optimization_barrier((first, second, near))
    edge, across, inside = edge_first(main, first, second, radius)
    for step in range(ITERS):
        from_across, from_inside = swap_pairs(across, inside, "gx")
        near, middle = forward_edge(edge, inner, near, view_one, view_two, weights, radius)
        across, inside, outer = ratios(from_across, from_inside, inner, near, view_one, view_two, weights, radius)
        from_across, from_inside = swap_pairs(across, inside, "gx")
        main_sum, edge_sum = back(outer, middle, weights, radius)
        last = step == ITERS - 1
        edge_sum, first, second = y_messages(edge_sum, from_across, from_inside, not last, radius)
        first, second = swap_pairs(first, second, "gy")
        if not last:
            main, inner, near = forward_next(main, base, main_sum, from_across, from_inside, weights, radius)
            base = 0
            first, second, near = lax.optimization_barrier((first, second, near))
            edge, across, inside = edge_next(edge, edge_sum, first, second, main, radius)
    return finish(main, main_sum, from_across, from_inside, edge, edge_sum, first, second, radius)


def solution(mesh):
    in_specs = (P("gx", "gy", None), P("gx", "gy", None), P("gx", "gy", None), P(), P())
    out_specs = P("gx", "gy", None)
    return jax.shard_map(local, mesh=mesh, in_specs=in_specs, out_specs=out_specs, check_vma=False)
```

```python
import functools
import jax
import jax.numpy as jnp
from jax import lax
from jax.experimental import pallas as pl
from jax.experimental.pallas import tpu as pltpu
from jax.sharding import PartitionSpec as P

ITERS = 2
F32 = jnp.float32
BF16 = jnp.bfloat16
LIMIT = 24 * 1024 * 1024
WIDE_LIMIT = 50 * 1024 * 1024
EDGE = 16
NEAR = 32


def round_up(value, unit):
    return (value + unit - 1) // unit * unit


def edge_width(radius):
    return 2 * EDGE + round_up(2 * radius, 8)


def split(value):
    high = value.astype(BF16)
    low = (value - high.astype(F32)).astype(BF16)
    return high, low


def stack(value):
    high, low = split(value)
    return [high, low, high]


def multiply(weights, value):
    return jnp.dot(weights, value, preferred_element_type=F32)


def call(kernel, name, out_shape, flops, moved, scratch=(), in_specs=None, limit=LIMIT):
    extra = {} if in_specs is None else {"in_specs": in_specs}
    return pl.pallas_call(
        kernel,
        out_shape=out_shape,
        **extra,
        scratch_shapes=list(scratch),
        compiler_params=pltpu.CompilerParams(vmem_limit_bytes=limit),
        cost_estimate=pl.CostEstimate(flops=flops, bytes_accessed=moved, transcendentals=0),
        name=name,
    )


def shape(*dims, dtype=F32):
    return jax.ShapeDtypeStruct(dims, dtype)


def weights_kernel(cols, psf_ref, taps_ref, main_ref, edge_ref, full_ref, back_ref, zf_ref, zb_ref):
    taps = psf_ref.shape[1]
    radius = (taps - 1) // 2
    depth = zf_ref.shape[1] // 2
    main = cols - 2 * EDGE
    edge = round_up(edge_width(radius), 16)
    rows = psf_ref[...] / jnp.sum(psf_ref[...], axis=1, keepdims=True)
    one, two = rows[0:3], rows[3:6]
    x_rows = (one[0:1], two[1:2])
    y_rows = (one[1:2], two[0:1])
    z_rows = (one[2:3], two[2:3])
    pitch = taps_ref.shape[0] // 2
    taps_ref[...] = jnp.zeros_like(taps_ref)
    for view in range(2):
        for tap in range(taps):
            taps_ref[view * pitch + tap : view * pitch + tap + 1, :] = jnp.broadcast_to(
                x_rows[view][:, tap : tap + 1], (1, taps_ref.shape[1])
            )

    def iota(dims, dim):
        return lax.broadcasted_iota(jnp.int32, dims, dim)

    def band(row, offset):
        total = jnp.zeros(offset.shape, F32)
        for tap in range(taps):
            total = jnp.where(offset == tap, row[:, tap : tap + 1], total)
        return total

    def edge_place(index):
        place = jnp.where(index < EDGE, index, index + cols - 2 * EDGE)
        place = jnp.where(index >= 2 * EDGE, index - 2 * EDGE - radius, place)
        place = jnp.where(index >= 2 * EDGE + radius, index - 2 * EDGE - radius + cols, place)
        return jnp.where(index >= 2 * EDGE + 2 * radius, 8 * cols, place)

    def laid(value):
        high, low = split(value)
        return jnp.concatenate([high, high, low], axis=1)

    for view in range(2):
        row = y_rows[view]
        rows = pl.ds(view * cols, cols)
        dims = (cols, main)
        left = laid(band(row, iota(dims, 0) - (iota(dims, 1) + EDGE) + radius))
        dims = (cols, edge)
        right = laid(band(row, iota(dims, 0) - edge_place(iota(dims, 1)) + radius))
        main_ref[rows, :] = left
        edge_ref[rows, :] = right
        full_ref[rows, :] = jnp.concatenate([left, right], axis=1)
        part = slice(3 * cols * view, 3 * cols * (view + 1))
        dims = (main, cols)
        back_ref[0:main, part] = laid(band(row, iota(dims, 1) - (iota(dims, 0) + EDGE) + radius))
        dims = (edge, cols)
        back_ref[main:, part] = laid(band(row, iota(dims, 1) - edge_place(iota(dims, 0)) + radius))
        dims = (depth, depth)
        first, second = iota(dims, 0), iota(dims, 1)
        for ref, offset in ((zf_ref, second - first + radius), (zb_ref, first - second + radius)):
            high, low = split(band(z_rows[view], offset))
            both = jnp.concatenate([high, low], axis=1)
            ref[view] = jnp.concatenate([both, both], axis=0)


def make_weights(psf_one, psf_two, cols, depth):
    radius = (psf_one.shape[1] - 1) // 2
    main = cols - 2 * EDGE
    edge = round_up(edge_width(radius), 16)
    return call(
        functools.partial(weights_kernel, cols), "weights",
        (
            shape(48, 128),
            shape(2 * cols, 3 * main, dtype=BF16),
            shape(2 * cols, 3 * edge, dtype=BF16),
            shape(2 * cols, 3 * (main + edge), dtype=BF16),
            shape(main + edge, 6 * cols, dtype=BF16),
            shape(2, 2 * depth, 2 * depth, dtype=BF16),
            shape(2, 2 * depth, 2 * depth, dtype=BF16),
        ), 1 << 22, 1 << 20,
    )(jnp.concatenate([psf_one, psf_two], axis=0))


def pad_rows(value):
    extra = round_up(value.shape[0], 16) - value.shape[0]
    if not extra:
        return value
    return jnp.concatenate([value, jnp.zeros((extra, value.shape[1]), value.dtype)], axis=0)


def beside(first, second):
    return jnp.concatenate([first, second], axis=1)


def depth_pass(value, matrix):
    both = multiply_depth(value, matrix)
    depth = value.shape[1]
    return both[:, :depth] + both[:, depth:]


def multiply_depth(value, matrix):
    high, low = split(value)
    return multiply(jnp.concatenate([high, low], axis=1), matrix)


def load_taps(taps_ref, view, taps):
    pitch = taps_ref.shape[0] // 2
    return [
        jnp.broadcast_to(taps_ref[view * pitch + tap : view * pitch + tap + 1, :], (8, 128))
        for tap in range(taps)
    ]


def row_sums(weights, read, write, sources, targets, tap_of, block):
    taps = len(weights)
    for start in range(0, targets, block):
        outs = range(start, min(start + block, targets))
        totals = {}
        for r in range(sources):
            used = [q for q in outs if 0 <= tap_of(q, r) < taps]
            if not used:
                continue
            value = read(r)
            for q in used:
                term = weights[tap_of(q, r)] * value
                totals[q] = totals[q] + term if q in totals else term
        for q in outs:
            write(q, totals[q])


def tiles(start, stop):
    def run(body):
        @pl.loop(0, (stop - start) // 8)
        def _(tile):
            inner = pl.multiple_of(tile * 8, 8)
            body(pl.ds(pl.multiple_of(start + inner, 8), 8), pl.ds(inner, 8))
    return run


def own_tap_forward(radius):
    return lambda q, r: q + radius - r


def own_tap_back(radius):
    return lambda q, r: r - q + radius


def sides(axis="gx"):
    odd = lax.rem(lax.axis_index(axis), 2)
    return odd, 1 - odd


def in_order(low, high):
    odd = sides("gy")[0] == 1
    return jnp.where(odd, high, low), jnp.where(odd, low, high)


def each_row(rows, radius, body):
    starts = [side * (rows - radius) for side in sides()]

    @pl.loop(0, radius // 2)
    def _(step):
        for k in range(2):
            row = 2 * step + k
            for which, start in enumerate(starts):
                body(start + row, (which, row))

    @pl.loop(0, (rows - 2 * radius) // 2)
    def _(step):
        for k in range(2):
            body(radius + 2 * step + k, None)


def main_pass(radius, rows, read, taps_ref, main_ref, inner_ref, near_ref, passed):
    cols = main_ref.shape[0] // 2
    depth = passed.shape[3]

    @pl.loop(0, rows // 4)
    def _(step):
        for pair in range(2):
            at = 4 * step + 2 * pair
            value = beside(read(at), read(at + 1))
            both = multiply(main_ref[...], jnp.concatenate(stack(value), axis=0))
            for view in range(2):
                for half in range(2):
                    block = both[view * cols : (view + 1) * cols, half * depth : (half + 1) * depth]
                    passed[view, at + half] = block[NEAR : cols - NEAR]
                    near_ref[view, at + half, 0:NEAR] = block[:NEAR]
                    near_ref[view, at + half, NEAR:] = block[cols - NEAR :]

    for view in range(2):
        weights = load_taps(taps_ref, view, 2 * radius + 1)

        @tiles(0, cols - 2 * NEAR)
        def _(at, _inner):
            def write(q, value):
                inner_ref[view, q, at, :] = value

            row_sums(weights, lambda r: passed[view, r, at, :], write, rows, rows,
                     own_tap_forward(radius), 16)


def load_kernel(radius, source_ref, current_ref, first_ref, second_ref, arrived):
    rows, cols, _ = current_ref.shape

    def copy(block):
        part = pl.ds(4 * block, 4)
        return pltpu.make_async_copy(source_ref.at[part], current_ref.at[part], arrived.at[block])

    for block in range(rows // 4):
        copy(block).start()

    @pl.loop(0, rows // 4)
    def _(block):
        copy(block).wait()
        for k in range(4):
            row = 4 * block + k
            part = slice(k * radius, (k + 1) * radius)
            first_ref[block, part], second_ref[block, part] = in_order(
                current_ref[row, 0:radius], current_ref[row, cols - radius :])


def load(estimate, radius):
    rows, cols, depth = estimate.shape
    sent = shape(rows // 4, 4 * radius, depth)
    return call(
        functools.partial(load_kernel, radius), "load", (shape(rows, cols, depth), sent, sent),
        1, 1 << 22, [pltpu.SemaphoreType.DMA((rows // 4,))],
        [pl.BlockSpec(memory_space=pltpu.HBM)], WIDE_LIMIT)(estimate)


def forward_first_kernel(radius, current_ref, taps_ref, main_ref, inner_ref, near_ref, passed):
    rows, cols, _ = current_ref.shape
    main_pass(radius, rows, lambda row: current_ref[row, EDGE : cols - EDGE],
              taps_ref, main_ref, inner_ref, near_ref, passed)


def forward_next_kernel(radius, base, current_ref, sum_ref, across_ref, inside_ref, taps_ref, main_ref,
                        next_ref, inner_ref, near_ref, passed):
    rows, width, _ = sum_ref.shape
    rims = (across_ref, inside_ref)

    def update(row, rim):
        total = sum_ref[row]
        if rim is not None:
            total = total + rims[rim[0]][rim[1], 0:width]
        next_ref[row] = current_ref[row, base : base + width] * (total * 0.5)

    each_row(rows, radius, update)
    main_pass(radius, rows, lambda row: next_ref[row], taps_ref, main_ref, inner_ref, near_ref, passed)


def forward_shapes(rows, cols, depth):
    return (
        (shape(2, rows, cols - 2 * NEAR, depth), shape(2, rows, 2 * NEAR, depth)),
        [pltpu.VMEM((2, rows, cols - 2 * NEAR, depth), F32)],
    )


def forward_first(current, weights, radius):
    rows, cols, depth = current.shape
    outs, scratch = forward_shapes(rows, cols, depth)
    return call(
        functools.partial(forward_first_kernel, radius), "forward_first",
        outs, 1 << 31, 12 * rows * cols * depth, scratch,
    )(current, weights[0], weights[1])


def forward_next(current, base, main_sum, low, high, weights, radius):
    rows, width, depth = main_sum.shape
    outs, scratch = forward_shapes(rows, width + 2 * EDGE, depth)
    return call(
        functools.partial(forward_next_kernel, radius, base), "forward_next",
        (shape(rows, width, depth),) + outs, 1 << 31, 12 * rows * width * depth, scratch,
    )(current, main_sum, low, high, weights[0], weights[1])


def write_messages(radius, main_row, edge_ref, across_ref, inside_ref):
    rows = edge_ref.shape[0]
    width = across_ref.shape[1] - edge_ref.shape[1]
    starts = [side * (rows - radius) for side in sides()]

    @pl.loop(0, radius // 2)
    def _(step):
        for k in range(2):
            row = 2 * step + k
            for ref, start in zip((across_ref, inside_ref), starts):
                ref[row, 0:width] = main_row(start + row)
                ref[row, width:] = edge_ref[start + row]


def edge_first_kernel(radius, current_ref, first_ref, second_ref, edge_ref, across_ref, inside_ref):
    rows, cols, depth = current_ref.shape
    rims = 2 * EDGE

    @pl.loop(0, rows // 4)
    def _(block):
        for k in range(4):
            row = 4 * block + k
            part = slice(k * radius, (k + 1) * radius)
            edge_ref[row, 0:EDGE] = current_ref[row, 0:EDGE]
            edge_ref[row, EDGE:rims] = current_ref[row, cols - EDGE :]
            edge_ref[row, edge_ref.shape[1] - 8 :] = jnp.zeros((8, depth), F32)
            low, high = in_order(first_ref[block, part], second_ref[block, part])
            edge_ref[row, rims : rims + radius] = low
            edge_ref[row, rims + radius : rims + 2 * radius] = high

    write_messages(radius, lambda at: current_ref[at, EDGE : cols - EDGE], edge_ref, across_ref, inside_ref)


def add_y(radius, total_ref, block, k, first_ref, second_ref):
    rims = 2 * EDGE

    def add(start, value):
        part = slice(start, start + radius)
        total_ref[part] = total_ref[part] + value

    part = slice(k * radius, (k + 1) * radius)
    low, high = in_order(first_ref[block, part], second_ref[block, part])
    add(0, low)
    add(rims - radius, high)
    if first_ref.shape[1] > 4 * radius:
        part = slice((4 + k) * radius, (5 + k) * radius)
        low, high = in_order(first_ref[block, part], second_ref[block, part])
        add(rims, low)
        add(rims + radius, high)


def edge_next_kernel(radius, edge_ref, sum_ref, first_ref, second_ref, main_ref,
                     next_ref, across_ref, inside_ref, totals):
    @pl.loop(0, edge_ref.shape[0] // 4)
    def _(block):
        for k in range(4):
            row = 4 * block + k
            totals[row] = sum_ref[row]
            add_y(radius, totals.at[row], block, k, first_ref, second_ref)
            next_ref[row] = edge_ref[row] * (totals[row] * 0.5)

    write_messages(radius, lambda at: main_ref[at], next_ref, across_ref, inside_ref)


def edge_shapes(rows, cols, depth, radius):
    wide = cols - 2 * EDGE + edge_width(radius)
    return (shape(rows, edge_width(radius), depth), shape(radius, wide, depth), shape(radius, wide, depth))


def edge_first(current, from_low, from_high, radius):
    outs = edge_shapes(*current.shape, radius)
    return call(functools.partial(edge_first_kernel, radius), "edge_first", outs, 1, 1 << 22)(
        current, from_low, from_high)


def edge_next(edge, edge_sum, from_low, from_high, main, radius):
    rows, width, depth = main.shape
    outs = edge_shapes(rows, width + 2 * EDGE, depth, radius)
    return call(
        functools.partial(edge_next_kernel, radius), "edge_next", outs, 1, 1 << 22,
        [pltpu.VMEM(edge.shape, F32)])(edge, edge_sum, from_low, from_high, main)


def y_messages_kernel(radius, whole, edge_ref, across_ref, inside_ref, sum_ref, first_ref, second_ref):
    rows, width, _ = edge_ref.shape
    before = across_ref.shape[1] - width
    refs = (across_ref, inside_ref)
    rims = 2 * EDGE

    def row_of(row, rim):
        total = edge_ref[row]
        if rim is not None:
            total = total + refs[rim[0]][rim[1], before:]
        sum_ref[row] = total

    each_row(rows, radius, row_of)

    @pl.loop(0, rows // 4)
    def _(block):
        for k in range(4):
            row = 4 * block + k
            part = slice(k * radius, (k + 1) * radius)
            first_ref[block, part], second_ref[block, part] = in_order(
                sum_ref[row, rims : rims + radius], sum_ref[row, rims + radius : rims + 2 * radius])
            if whole:
                part = slice((4 + k) * radius, (5 + k) * radius)
                first_ref[block, part], second_ref[block, part] = in_order(
                    sum_ref[row, 0:radius], sum_ref[row, rims - radius : rims])


def y_messages(edge_sum, low, high, whole, radius):
    rows, width, depth = edge_sum.shape
    sent = shape(rows // 4, (8 if whole else 4) * radius, depth)
    return call(
        functools.partial(y_messages_kernel, radius, whole), "y_messages",
        (shape(rows, width, depth), sent, sent), 1, 1 << 22)(edge_sum, low, high)


def ratio_block(values, seen, zf_ref, zb_ref, view):
    blurred = depth_pass(values, zf_ref[view])
    return depth_pass(seen / blurred, zb_ref[view])


def forward_edge_kernel(radius, current_ref, inner_ref, before_ref, one_ref, two_ref, taps_ref, edge_ref,
                        zf_ref, zb_ref, near_ref, middle_ref, passed):
    rows, cols, depth = one_ref.shape
    kept = jnp.concatenate(
        [edge_ref[start : start + NEAR] for start in (0, cols - NEAR, cols, 2 * cols - NEAR)], axis=0)

    @pl.loop(0, rows // 4)
    def _(step):
        for pair in range(2):
            at = 4 * step + 2 * pair
            value = pad_rows(beside(current_ref[at], current_ref[at + 1]))
            both = multiply(kept, jnp.concatenate(stack(value), axis=0))
            for view in range(2):
                for half in range(2):
                    passed[view, at + half] = before_ref[view, at + half] + both[
                        2 * NEAR * view : 2 * NEAR * (view + 1), half * depth : (half + 1) * depth]

    for view in range(2):
        weights = load_taps(taps_ref, view, 2 * radius + 1)

        @tiles(0, 2 * NEAR)
        def _(at, _inner):
            def write(q, value):
                near_ref[view, q, at, :] = value

            row_sums(weights, lambda r: passed[view, r, at, :], write, rows, rows,
                     own_tap_forward(radius), 16)

    @pl.loop(0, (rows - 2 * radius) // 2)
    def _(step):
        at = 2 * step
        for view, seen in ((0, one_ref), (1, two_ref)):
            parts = []
            for row in (radius + at, radius + at + 1):
                parts += [near_ref[view, row, 0:NEAR], inner_ref[view, row], near_ref[view, row, NEAR:]]
            value = ratio_block(
                jnp.concatenate(parts, axis=0), seen[pl.ds(radius + at, 2)].reshape(2 * cols, depth),
                zf_ref, zb_ref, view)
            middle_ref[view, pl.ds(at, 2)] = value.reshape(2, cols, depth)


def forward_edge(current, inner, before, one, two, weights, radius):
    taps, _, edge, _, _, zf, zb = weights
    rows, cols, depth = one.shape
    return call(
        functools.partial(forward_edge_kernel, radius), "forward_edge",
        (shape(2, rows, 2 * NEAR, depth), shape(2, rows - 2 * radius, cols, depth)),
        1 << 31, 24 * rows * NEAR * depth,
        [pltpu.VMEM((2, rows, 2 * NEAR, depth), F32)],
    )(current, inner, before, one, two, taps, edge, zf, zb)


def ratio_kernel(radius, across_ref, inside_ref, inner_ref, near_ref, one_ref, two_ref, taps_ref, full_ref,
                 back_ref, zf_ref, zb_ref, rim_across_ref, rim_inside_ref, outer_ref, halo, edges):
    rows, cols, depth = one_ref.shape
    main = cols - 2 * EDGE
    taps = 2 * radius + 1

    @pl.loop(0, radius // 2)
    def _(step):
        at = 2 * step
        for side, ref in zip(sides(), (across_ref, inside_ref)):
            left = beside(ref[at, 0:main], ref[at + 1, 0:main])
            right = pad_rows(beside(ref[at, main:], ref[at + 1, main:]))
            both = multiply(full_ref[...], jnp.concatenate(stack(left) + stack(right), axis=0))
            for view in range(2):
                for half in range(2):
                    halo[view, side * radius + at + half] = both[
                        view * cols : (view + 1) * cols, half * depth : (half + 1) * depth]

    for view in range(2):
        weights = load_taps(taps_ref, view, taps)
        for ref, start, stop, shift in (
            (near_ref, 0, NEAR, 0), (inner_ref, NEAR, cols - NEAR, 0),
            (near_ref, cols - NEAR, cols, NEAR),
        ):
            @tiles(start, stop)
            def _(at, inner):
                own = pl.ds(pl.multiple_of(inner.start + shift, 8), 8)

                def write_low(q, value):
                    edges[view, q, at, :] = value + ref[view, q, own, :]

                def write_high(q, value):
                    edges[view, radius + q, at, :] = value + ref[view, rows - radius + q, own, :]

                row_sums(weights, lambda r: halo[view, r, at, :], write_low, radius, radius,
                         lambda q, r: q + 2 * radius - r, radius)
                row_sums(weights, lambda r: halo[view, radius + r, at, :], write_high, radius, radius,
                         lambda q, r: q - r, radius)

    @pl.loop(0, radius // 2)
    def _(step):
        at = 2 * step
        for base, start in ((0, 0), (radius, rows - radius)):
            for view, seen in ((0, one_ref), (1, two_ref)):
                value = ratio_block(
                    edges[view, pl.ds(base + at, 2)].reshape(2 * cols, depth),
                    seen[pl.ds(start + at, 2)].reshape(2 * cols, depth), zf_ref, zb_ref, view)
                outer_ref[view, pl.ds(base + at, 2)] = value.reshape(2, cols, depth)

    for view in range(2):
        weights = load_taps(taps_ref, view, taps)

        @tiles(0, cols)
        def _(at, _inner):
            def write_low(q, value):
                halo[view, q, at, :] = value

            def write_high(q, value):
                halo[view, radius + q, at, :] = value

            row_sums(weights, lambda r: outer_ref[view, r, at, :], write_low, radius, radius,
                     lambda q, r: r - q + 2 * radius, radius)
            row_sums(weights, lambda r: outer_ref[view, radius + r, at, :], write_high,
                     radius, radius, lambda q, r: r - q, radius)

    @pl.loop(0, radius // 2)
    def _(step):
        at = 2 * step
        for side, ref in zip(sides(), (rim_across_ref, rim_inside_ref)):
            base = side * radius
            parts = []
            for view in range(2):
                parts += stack(beside(halo[view, base + at], halo[view, base + at + 1]))
            total = multiply(back_ref[...], jnp.concatenate(parts, axis=0))
            for half in range(2):
                ref[at + half] = total[: ref.shape[1], half * depth : (half + 1) * depth]


def ratios(low, high, inner, near, one, two, weights, radius):
    taps, _, _, full, back, zf, zb = weights
    rows, cols, depth = one.shape
    wide = low.shape[1]
    return call(
        functools.partial(ratio_kernel, radius), "ratios",
        (shape(radius, wide, depth), shape(radius, wide, depth), shape(2, 2 * radius, cols, depth)),
        1 << 33, 24 * rows * cols * depth,
        [pltpu.VMEM((2, 2 * radius, cols, depth), F32)] * 2,
    )(low, high, inner, near, one, two, taps, full, back, zf, zb)


def back_kernel(radius, outer_ref, middle_ref, taps_ref, back_ref, main_ref, edge_ref, summed):
    rows = main_ref.shape[0]
    width = main_ref.shape[1]
    depth = main_ref.shape[2]
    cols = outer_ref.shape[2]
    for view in range(2):
        weights = load_taps(taps_ref, view, 2 * radius + 1)

        @tiles(0, cols)
        def _(at, _inner):
            def read(r):
                if radius <= r < rows - radius:
                    return middle_ref[view, r - radius, at, :]
                return outer_ref[view, r if r < radius else r - rows + 2 * radius, at, :]

            def write(q, value):
                summed[view, q, at, :] = value

            row_sums(weights, read, write, rows, rows, own_tap_back(radius), 16)

    @pl.loop(0, rows // 4)
    def _(step):
        for pair in range(2):
            at = 4 * step + 2 * pair
            parts = []
            for view in range(2):
                parts += stack(beside(summed[view, at], summed[view, at + 1]))
            total = multiply(back_ref[...], jnp.concatenate(parts, axis=0))
            for half in range(2):
                lanes = slice(half * depth, (half + 1) * depth)
                main_ref[at + half] = total[:width, lanes]
                edge_ref[at + half] = total[width : width + edge_ref.shape[1], lanes]


def back(outer, middle, weights, radius):
    _, _, cols, depth = outer.shape
    rows = outer.shape[1] + middle.shape[1]
    return call(
        functools.partial(back_kernel, radius), "back",
        (shape(rows, cols - 2 * EDGE, depth), shape(rows, edge_width(radius), depth)),
        1 << 32, 12 * rows * cols * depth,
        [pltpu.VMEM((2, rows, cols, depth), F32)],
    )(outer, middle, weights[0], weights[4])


def finish_kernel(radius, main_ref, sum_ref, across_ref, inside_ref, edge_ref, edge_sum_ref,
                  first_ref, second_ref, out_ref, totals):
    rows, cols, _ = out_ref.shape
    width = cols - 2 * EDGE
    rims = (across_ref, inside_ref)

    def row_of(row, rim):
        total = sum_ref[row]
        if rim is not None:
            total = total + rims[rim[0]][rim[1], 0:width]
        out_ref[row, EDGE : cols - EDGE] = main_ref[row] * (total * 0.5)

    each_row(rows, radius, row_of)

    @pl.loop(0, rows // 4)
    def _(block):
        for k in range(4):
            row = 4 * block + k
            totals[row] = edge_sum_ref[row, 0 : 2 * EDGE]
            add_y(radius, totals.at[row], block, k, first_ref, second_ref)
            out_ref[row, 0:EDGE] = edge_ref[row, 0:EDGE] * (totals[row, 0:EDGE] * 0.5)
            out_ref[row, cols - EDGE :] = edge_ref[row, EDGE : 2 * EDGE] * (totals[row, EDGE:] * 0.5)


def finish(main, main_sum, low, high, edge, edge_sum, from_low, from_high, radius):
    rows, width, depth = main.shape
    return call(
        functools.partial(finish_kernel, radius), "finish", shape(rows, width + 2 * EDGE, depth),
        1, 1 << 22, [pltpu.VMEM((rows, 2 * EDGE, depth), F32)],
    )(main, main_sum, low, high, edge, edge_sum, from_low, from_high)


def swap_pairs(first, second, axis):
    count = lax.axis_size(axis)

    def pairs(start):
        return [pair for i in range(start, count - 1, 2) for pair in ((i, i + 1), (i + 1, i))]

    return lax.ppermute(first, axis, pairs(1)), lax.ppermute(second, axis, pairs(0))


def local(estimate, view_one, view_two, psf_one, psf_two):
    rows, cols, depth = estimate.shape
    radius = (psf_one.shape[1] - 1) // 2
    main, first, second = load(estimate, radius)
    first, second = swap_pairs(first, second, "gy")
    weights = make_weights(psf_one, psf_two, cols, depth)
    inner, near = forward_first(main, weights, radius)
    base = EDGE
    first, second, near = lax.optimization_barrier((first, second, near))
    edge, across, inside = edge_first(main, first, second, radius)
    for step in range(ITERS):
        from_across, from_inside = swap_pairs(across, inside, "gx")
        near, middle = forward_edge(edge, inner, near, view_one, view_two, weights, radius)
        across, inside, outer = ratios(from_across, from_inside, inner, near, view_one, view_two, weights, radius)
        from_across, from_inside = swap_pairs(across, inside, "gx")
        main_sum, edge_sum = back(outer, middle, weights, radius)
        last = step == ITERS - 1
        edge_sum, first, second = y_messages(edge_sum, from_across, from_inside, not last, radius)
        first, second = swap_pairs(first, second, "gy")
        if not last:
            main, inner, near = forward_next(main, base, main_sum, from_across, from_inside, weights, radius)
            base = 0
            first, second, near = lax.optimization_barrier((first, second, near))
            edge, across, inside = edge_next(edge, edge_sum, first, second, main, radius)
    return finish(main, main_sum, from_across, from_inside, edge, edge_sum, first, second, radius)


def solution(mesh):
    in_specs = (P("gx", "gy", None), P("gx", "gy", None), P("gx", "gy", None), P(), P())
    out_specs = P("gx", "gy", None)
    return jax.shard_map(local, mesh=mesh, in_specs=in_specs, out_specs=out_specs, check_vma=False)
```

```python
import functools
import jax
import jax.numpy as jnp
from jax import lax
from jax.experimental import pallas as pl
from jax.experimental.pallas import tpu as pltpu
from jax.sharding import PartitionSpec as P

ITERS = 2
F32 = jnp.float32
BF16 = jnp.bfloat16
LIMIT = 24 * 1024 * 1024
WIDE_LIMIT = 50 * 1024 * 1024
EDGE = 16
NEAR = 32


def round_up(value, unit):
    return (value + unit - 1) // unit * unit


def edge_width(radius):
    return 2 * EDGE + round_up(2 * radius, 8)


def split(value):
    high = value.astype(BF16)
    low = (value - high.astype(F32)).astype(BF16)
    return high, low


def stack(value):
    high, low = split(value)
    return [high, low, high]


def multiply(weights, value):
    return jnp.dot(weights, value, preferred_element_type=F32)


def call(kernel, name, out_shape, flops, moved, scratch=(), in_specs=None, limit=LIMIT):
    extra = {} if in_specs is None else {"in_specs": in_specs}
    return pl.pallas_call(
        kernel,
        out_shape=out_shape,
        **extra,
        scratch_shapes=list(scratch),
        compiler_params=pltpu.CompilerParams(vmem_limit_bytes=limit),
        cost_estimate=pl.CostEstimate(flops=flops, bytes_accessed=moved, transcendentals=0),
        name=name,
    )


def shape(*dims, dtype=F32):
    return jax.ShapeDtypeStruct(dims, dtype)


def weights_kernel(cols, psf_ref, taps_ref, main_ref, edge_ref, full_ref, back_ref, zf_ref, zb_ref):
    taps = psf_ref.shape[1]
    radius = (taps - 1) // 2
    depth = zf_ref.shape[1] // 2
    main = cols - 2 * EDGE
    edge = round_up(edge_width(radius), 16)
    rows = psf_ref[...] / jnp.sum(psf_ref[...], axis=1, keepdims=True)
    one, two = rows[0:3], rows[3:6]
    x_rows = (one[0:1], two[1:2])
    y_rows = (one[1:2], two[0:1])
    z_rows = (one[2:3], two[2:3])
    pitch = taps_ref.shape[0] // 2
    taps_ref[...] = jnp.zeros_like(taps_ref)
    for view in range(2):
        for tap in range(taps):
            taps_ref[view * pitch + tap : view * pitch + tap + 1, :] = jnp.broadcast_to(
                x_rows[view][:, tap : tap + 1], (1, taps_ref.shape[1])
            )

    def iota(dims, dim):
        return lax.broadcasted_iota(jnp.int32, dims, dim)

    def band(row, offset):
        total = jnp.zeros(offset.shape, F32)
        for tap in range(taps):
            total = jnp.where(offset == tap, row[:, tap : tap + 1], total)
        return total

    def edge_place(index):
        place = jnp.where(index < EDGE, index, index + cols - 2 * EDGE)
        place = jnp.where(index >= 2 * EDGE, index - 2 * EDGE - radius, place)
        place = jnp.where(index >= 2 * EDGE + radius, index - 2 * EDGE - radius + cols, place)
        return jnp.where(index >= 2 * EDGE + 2 * radius, 8 * cols, place)

    def laid(value):
        high, low = split(value)
        return jnp.concatenate([high, high, low], axis=1)

    for view in range(2):
        row = y_rows[view]
        rows = pl.ds(view * cols, cols)
        dims = (cols, main)
        left = laid(band(row, iota(dims, 0) - (iota(dims, 1) + EDGE) + radius))
        dims = (cols, edge)
        right = laid(band(row, iota(dims, 0) - edge_place(iota(dims, 1)) + radius))
        main_ref[rows, :] = left
        edge_ref[rows, :] = right
        full_ref[rows, :] = jnp.concatenate([left, right], axis=1)
        part = slice(3 * cols * view, 3 * cols * (view + 1))
        dims = (main, cols)
        back_ref[0:main, part] = laid(band(row, iota(dims, 1) - (iota(dims, 0) + EDGE) + radius))
        dims = (edge, cols)
        back_ref[main:, part] = laid(band(row, iota(dims, 1) - edge_place(iota(dims, 0)) + radius))
        dims = (depth, depth)
        first, second = iota(dims, 0), iota(dims, 1)
        for ref, offset in ((zf_ref, second - first + radius), (zb_ref, first - second + radius)):
            high, low = split(band(z_rows[view], offset))
            both = jnp.concatenate([high, low], axis=1)
            ref[view] = jnp.concatenate([both, both], axis=0)


def make_weights(psf_one, psf_two, cols, depth):
    radius = (psf_one.shape[1] - 1) // 2
    main = cols - 2 * EDGE
    edge = round_up(edge_width(radius), 16)
    return call(
        functools.partial(weights_kernel, cols), "weights",
        (
            shape(48, 128),
            shape(2 * cols, 3 * main, dtype=BF16),
            shape(2 * cols, 3 * edge, dtype=BF16),
            shape(2 * cols, 3 * (main + edge), dtype=BF16),
            shape(main + edge, 6 * cols, dtype=BF16),
            shape(2, 2 * depth, 2 * depth, dtype=BF16),
            shape(2, 2 * depth, 2 * depth, dtype=BF16),
        ), 1 << 22, 1 << 20,
    )(jnp.concatenate([psf_one, psf_two], axis=0))


def pad_rows(value):
    extra = round_up(value.shape[0], 16) - value.shape[0]
    if not extra:
        return value
    return jnp.concatenate([value, jnp.zeros((extra, value.shape[1]), value.dtype)], axis=0)


def beside(first, second):
    return jnp.concatenate([first, second], axis=1)


def depth_pass(value, matrix):
    both = multiply_depth(value, matrix)
    depth = value.shape[1]
    return both[:, :depth] + both[:, depth:]


def multiply_depth(value, matrix):
    high, low = split(value)
    return multiply(jnp.concatenate([high, low], axis=1), matrix)


def load_taps(taps_ref, view, taps):
    pitch = taps_ref.shape[0] // 2
    return [
        jnp.broadcast_to(taps_ref[view * pitch + tap : view * pitch + tap + 1, :], (8, 128))
        for tap in range(taps)
    ]


def row_sums(weights, read, write, sources, targets, tap_of, block):
    taps = len(weights)
    for start in range(0, targets, block):
        outs = range(start, min(start + block, targets))
        totals = {}
        for r in range(sources):
            used = [q for q in outs if 0 <= tap_of(q, r) < taps]
            if not used:
                continue
            value = read(r)
            for q in used:
                term = weights[tap_of(q, r)] * value
                totals[q] = totals[q] + term if q in totals else term
        for q in outs:
            write(q, totals[q])


def tiles(start, stop):
    def run(body):
        @pl.loop(0, (stop - start) // 8)
        def _(tile):
            inner = pl.multiple_of(tile * 8, 8)
            body(pl.ds(pl.multiple_of(start + inner, 8), 8), pl.ds(inner, 8))
    return run


def own_tap_forward(radius):
    return lambda q, r: q + radius - r


def own_tap_back(radius):
    return lambda q, r: r - q + radius


def sides(axis="gx"):
    odd = lax.rem(lax.axis_index(axis), 2)
    return odd, 1 - odd


def in_order(low, high):
    odd = sides("gy")[0] == 1
    return jnp.where(odd, high, low), jnp.where(odd, low, high)


def each_row(rows, radius, body):
    starts = [side * (rows - radius) for side in sides()]

    @pl.loop(0, radius // 2)
    def _(step):
        for k in range(2):
            row = 2 * step + k
            for which, start in enumerate(starts):
                body(start + row, (which, row))

    @pl.loop(0, (rows - 2 * radius) // 2)
    def _(step):
        for k in range(2):
            body(radius + 2 * step + k, None)


def main_pass(radius, rows, read, taps_ref, main_ref, inner_ref, near_ref, passed):
    cols = main_ref.shape[0] // 2
    depth = passed.shape[3]

    @pl.loop(0, rows // 4)
    def _(step):
        for pair in range(2):
            at = 4 * step + 2 * pair
            value = beside(read(at), read(at + 1))
            both = multiply(main_ref[...], jnp.concatenate(stack(value), axis=0))
            for view in range(2):
                for half in range(2):
                    block = both[view * cols : (view + 1) * cols, half * depth : (half + 1) * depth]
                    passed[view, at + half] = block[NEAR : cols - NEAR]
                    near_ref[view, at + half, 0:NEAR] = block[:NEAR]
                    near_ref[view, at + half, NEAR:] = block[cols - NEAR :]

    for view in range(2):
        weights = load_taps(taps_ref, view, 2 * radius + 1)

        @tiles(0, cols - 2 * NEAR)
        def _(at, _inner):
            def write(q, value):
                inner_ref[view, q, at, :] = value

            row_sums(weights, lambda r: passed[view, r, at, :], write, rows, rows,
                     own_tap_forward(radius), 16)


def load_kernel(radius, source_ref, current_ref, first_ref, second_ref, arrived):
    rows, cols, _ = current_ref.shape

    def copy(block):
        part = pl.ds(4 * block, 4)
        return pltpu.make_async_copy(source_ref.at[part], current_ref.at[part], arrived.at[block])

    for block in range(rows // 4):
        copy(block).start()

    @pl.loop(0, rows // 4)
    def _(block):
        copy(block).wait()
        for k in range(4):
            row = 4 * block + k
            part = slice(k * radius, (k + 1) * radius)
            first_ref[block, part], second_ref[block, part] = in_order(
                current_ref[row, 0:radius], current_ref[row, cols - radius :])


def load(estimate, radius):
    rows, cols, depth = estimate.shape
    sent = shape(rows // 4, 4 * radius, depth)
    return call(
        functools.partial(load_kernel, radius), "load", (shape(rows, cols, depth), sent, sent),
        1, 1 << 22, [pltpu.SemaphoreType.DMA((rows // 4,))],
        [pl.BlockSpec(memory_space=pltpu.HBM)], WIDE_LIMIT)(estimate)


def forward_main_kernel(radius, base, current_ref, taps_ref, main_ref, inner_ref, near_ref, passed):
    rows = current_ref.shape[0]
    width = main_ref.shape[0] // 2 - 2 * EDGE
    main_pass(radius, rows, lambda row: current_ref[row, base : base + width],
              taps_ref, main_ref, inner_ref, near_ref, passed)


def forward_main(current, base, weights, radius):
    rows, _, depth = current.shape
    cols = weights[1].shape[0] // 2
    return call(
        functools.partial(forward_main_kernel, radius, base), "forward_main",
        (shape(2, rows, cols - 2 * NEAR, depth), shape(2, rows, 2 * NEAR, depth)),
        1 << 31, 12 * rows * cols * depth, [pltpu.VMEM((2, rows, cols - 2 * NEAR, depth), F32)],
    )(current, weights[0], weights[1])


def main_next_kernel(radius, base, current_ref, sum_ref, from_across_ref, from_inside_ref,
                     next_ref, across_ref, inside_ref):
    rows, width, _ = sum_ref.shape
    rims = (from_across_ref, from_inside_ref)

    def update(row, rim):
        total = sum_ref[row]
        if rim is not None:
            total = total + rims[rim[0]][rim[1]]
        next_ref[row] = current_ref[row, base : base + width] * (total * 0.5)

    each_row(rows, radius, update)
    cut_messages(radius, next_ref, across_ref, inside_ref)


def main_next(current, base, main_sum, across, inside, radius):
    rows, width, depth = main_sum.shape
    sent = shape(radius, width, depth)
    return call(
        functools.partial(main_next_kernel, radius, base), "main_next",
        (shape(rows, width, depth), sent, sent), 1, 1 << 22)(current, main_sum, across, inside)


def cut_messages(radius, source_ref, across_ref, inside_ref):
    rows = source_ref.shape[0]
    starts = [side * (rows - radius) for side in sides()]

    @pl.loop(0, radius // 2)
    def _(step):
        for k in range(2):
            row = 2 * step + k
            for ref, start in zip((across_ref, inside_ref), starts):
                ref[row] = source_ref[start + row]


def write_messages(radius, main_row, edge_ref, across_ref, inside_ref):
    rows = edge_ref.shape[0]
    width = across_ref.shape[1] - edge_ref.shape[1]
    starts = [side * (rows - radius) for side in sides()]

    @pl.loop(0, radius // 2)
    def _(step):
        for k in range(2):
            row = 2 * step + k
            for ref, start in zip((across_ref, inside_ref), starts):
                ref[row, 0:width] = main_row(start + row)
                ref[row, width:] = edge_ref[start + row]


def edge_first_kernel(radius, current_ref, first_ref, second_ref, edge_ref, across_ref, inside_ref):
    rows, cols, depth = current_ref.shape
    rims = 2 * EDGE

    @pl.loop(0, rows // 4)
    def _(block):
        for k in range(4):
            row = 4 * block + k
            part = slice(k * radius, (k + 1) * radius)
            edge_ref[row, 0:EDGE] = current_ref[row, 0:EDGE]
            edge_ref[row, EDGE:rims] = current_ref[row, cols - EDGE :]
            edge_ref[row, edge_ref.shape[1] - 8 :] = jnp.zeros((8, depth), F32)
            low, high = in_order(first_ref[block, part], second_ref[block, part])
            edge_ref[row, rims : rims + radius] = low
            edge_ref[row, rims + radius : rims + 2 * radius] = high

    write_messages(radius, lambda at: current_ref[at, EDGE : cols - EDGE], edge_ref, across_ref, inside_ref)


def add_y(radius, total_ref, block, k, first_ref, second_ref):
    rims = 2 * EDGE

    def add(start, value):
        part = slice(start, start + radius)
        total_ref[part] = total_ref[part] + value

    part = slice(k * radius, (k + 1) * radius)
    low, high = in_order(first_ref[block, part], second_ref[block, part])
    add(0, low)
    add(rims - radius, high)
    if first_ref.shape[1] > 4 * radius:
        part = slice((4 + k) * radius, (5 + k) * radius)
        low, high = in_order(first_ref[block, part], second_ref[block, part])
        add(rims, low)
        add(rims + radius, high)


def edge_next_kernel(radius, edge_ref, sum_ref, first_ref, second_ref, next_ref,
                     across_ref, inside_ref, totals):
    @pl.loop(0, edge_ref.shape[0] // 4)
    def _(block):
        for k in range(4):
            row = 4 * block + k
            totals[row] = sum_ref[row]
            add_y(radius, totals.at[row], block, k, first_ref, second_ref)
            next_ref[row] = edge_ref[row] * (totals[row] * 0.5)

    cut_messages(radius, next_ref, across_ref, inside_ref)


def edge_shapes(rows, cols, depth, radius):
    wide = cols - 2 * EDGE + edge_width(radius)
    return (shape(rows, edge_width(radius), depth), shape(radius, wide, depth), shape(radius, wide, depth))


def edge_first(current, from_low, from_high, radius):
    outs = edge_shapes(*current.shape, radius)
    return call(functools.partial(edge_first_kernel, radius), "edge_first", outs, 1, 1 << 22)(
        current, from_low, from_high)


def edge_next(edge, edge_sum, first, second, radius):
    rows, width, depth = edge.shape
    sent = shape(radius, width, depth)
    return call(
        functools.partial(edge_next_kernel, radius), "edge_next",
        (shape(rows, width, depth), sent, sent), 1, 1 << 22,
        [pltpu.VMEM(edge.shape, F32)])(edge, edge_sum, first, second)


def y_messages_kernel(radius, whole, edge_ref, across_ref, inside_ref, sum_ref, first_ref, second_ref):
    rows, width, _ = edge_ref.shape
    refs = (across_ref, inside_ref)
    rims = 2 * EDGE

    def row_of(row, rim):
        total = edge_ref[row]
        if rim is not None:
            total = total + refs[rim[0]][rim[1]]
        sum_ref[row] = total

    each_row(rows, radius, row_of)

    @pl.loop(0, rows // 4)
    def _(block):
        for k in range(4):
            row = 4 * block + k
            part = slice(k * radius, (k + 1) * radius)
            first_ref[block, part], second_ref[block, part] = in_order(
                sum_ref[row, rims : rims + radius], sum_ref[row, rims + radius : rims + 2 * radius])
            if whole:
                part = slice((4 + k) * radius, (5 + k) * radius)
                first_ref[block, part], second_ref[block, part] = in_order(
                    sum_ref[row, 0:radius], sum_ref[row, rims - radius : rims])


def y_messages(edge_sum, low, high, whole, radius):
    rows, width, depth = edge_sum.shape
    sent = shape(rows // 4, (8 if whole else 4) * radius, depth)
    return call(
        functools.partial(y_messages_kernel, radius, whole), "y_messages",
        (shape(rows, width, depth), sent, sent), 1, 1 << 22)(edge_sum, low, high)


def ratio_block(values, seen, zf_ref, zb_ref, view):
    blurred = depth_pass(values, zf_ref[view])
    return depth_pass(seen / blurred, zb_ref[view])


def forward_edge_kernel(radius, current_ref, inner_ref, before_ref, one_ref, two_ref, taps_ref, edge_ref,
                        zf_ref, zb_ref, near_ref, middle_ref, passed):
    rows, cols, depth = one_ref.shape
    kept = jnp.concatenate(
        [edge_ref[start : start + NEAR] for start in (0, cols - NEAR, cols, 2 * cols - NEAR)], axis=0)

    @pl.loop(0, rows // 4)
    def _(step):
        for pair in range(2):
            at = 4 * step + 2 * pair
            value = pad_rows(beside(current_ref[at], current_ref[at + 1]))
            both = multiply(kept, jnp.concatenate(stack(value), axis=0))
            for view in range(2):
                for half in range(2):
                    passed[view, at + half] = before_ref[view, at + half] + both[
                        2 * NEAR * view : 2 * NEAR * (view + 1), half * depth : (half + 1) * depth]

    for view in range(2):
        weights = load_taps(taps_ref, view, 2 * radius + 1)

        @tiles(0, 2 * NEAR)
        def _(at, _inner):
            def write(q, value):
                near_ref[view, q, at, :] = value

            row_sums(weights, lambda r: passed[view, r, at, :], write, rows, rows,
                     own_tap_forward(radius), 16)

    @pl.loop(0, (rows - 2 * radius) // 2)
    def _(step):
        at = 2 * step
        for view, seen in ((0, one_ref), (1, two_ref)):
            parts = []
            for row in (radius + at, radius + at + 1):
                parts += [near_ref[view, row, 0:NEAR], inner_ref[view, row], near_ref[view, row, NEAR:]]
            value = ratio_block(
                jnp.concatenate(parts, axis=0), seen[pl.ds(radius + at, 2)].reshape(2 * cols, depth),
                zf_ref, zb_ref, view)
            middle_ref[view, pl.ds(at, 2)] = value.reshape(2, cols, depth)


def forward_edge(current, inner, before, one, two, weights, radius):
    taps, _, edge, _, _, zf, zb = weights
    rows, cols, depth = one.shape
    return call(
        functools.partial(forward_edge_kernel, radius), "forward_edge",
        (shape(2, rows, 2 * NEAR, depth), shape(2, rows - 2 * radius, cols, depth)),
        1 << 31, 24 * rows * NEAR * depth,
        [pltpu.VMEM((2, rows, 2 * NEAR, depth), F32)],
    )(current, inner, before, one, two, taps, edge, zf, zb)


def ratio_kernel(radius, base, across_ref, across_edge_ref, inside_ref, inside_edge_ref, inner_ref,
                 near_ref, one_ref, two_ref, taps_ref, full_ref, back_ref, zf_ref, zb_ref,
                 rim_across_edge_ref, rim_inside_edge_ref, rim_near_ref, outer_ref, halo, edges):
    rows, cols, depth = one_ref.shape
    main = cols - 2 * EDGE
    taps = 2 * radius + 1

    @pl.loop(0, radius // 2)
    def _(step):
        at = 2 * step
        for side, ref, edge_ref in zip(
            sides(), (across_ref, inside_ref), (across_edge_ref, inside_edge_ref)
        ):
            left = beside(ref[at, 0:main], ref[at + 1, 0:main])
            right = pad_rows(beside(edge_ref[at, base:], edge_ref[at + 1, base:]))
            both = multiply(full_ref[...], jnp.concatenate(stack(left) + stack(right), axis=0))
            for view in range(2):
                for half in range(2):
                    halo[view, side * radius + at + half] = both[
                        view * cols : (view + 1) * cols, half * depth : (half + 1) * depth]

    for view in range(2):
        weights = load_taps(taps_ref, view, taps)
        for ref, start, stop, shift in (
            (near_ref, 0, NEAR, 0), (inner_ref, NEAR, cols - NEAR, 0),
            (near_ref, cols - NEAR, cols, NEAR),
        ):
            @tiles(start, stop)
            def _(at, inner):
                own = pl.ds(pl.multiple_of(inner.start + shift, 8), 8)

                def write_low(q, value):
                    edges[view, q, at, :] = value + ref[view, q, own, :]

                def write_high(q, value):
                    edges[view, radius + q, at, :] = value + ref[view, rows - radius + q, own, :]

                row_sums(weights, lambda r: halo[view, r, at, :], write_low, radius, radius,
                         lambda q, r: q + 2 * radius - r, radius)
                row_sums(weights, lambda r: halo[view, radius + r, at, :], write_high, radius, radius,
                         lambda q, r: q - r, radius)

    @pl.loop(0, radius // 2)
    def _(step):
        at = 2 * step
        for base, start in ((0, 0), (radius, rows - radius)):
            for view, seen in ((0, one_ref), (1, two_ref)):
                value = ratio_block(
                    edges[view, pl.ds(base + at, 2)].reshape(2 * cols, depth),
                    seen[pl.ds(start + at, 2)].reshape(2 * cols, depth), zf_ref, zb_ref, view)
                outer_ref[view, pl.ds(base + at, 2)] = value.reshape(2, cols, depth)

    for start, shift in ((0, 0), (cols - NEAR, NEAR)):
        rim_row_sums(radius, outer_ref, taps_ref, start, start + NEAR, shift, rim_near_ref)
    kept = edge_weights(back_ref, cols)

    @pl.loop(0, radius // 2)
    def _(step):
        at = 2 * step
        for side, ref in zip(sides(), (rim_across_edge_ref, rim_inside_edge_ref)):
            start = side * radius
            parts = []
            for view in range(2):
                parts += stack(beside(rim_near_ref[view, start + at], rim_near_ref[view, start + at + 1]))
            total = multiply(kept, jnp.concatenate(parts, axis=0))
            for half in range(2):
                ref[at + half] = total[: ref.shape[1], half * depth : (half + 1) * depth]


def ratios(main, edge, inner, near, one, two, weights, radius):
    taps, _, _, full, back, zf, zb = weights
    rows, cols, depth = one.shape
    base = edge[0].shape[1] - edge_width(radius)
    sent = shape(radius, edge_width(radius), depth)
    return call(
        functools.partial(ratio_kernel, radius, base), "ratios",
        (sent, sent, shape(2, 2 * radius, 2 * NEAR, depth), shape(2, 2 * radius, cols, depth)), 1 << 33, 24 * rows * cols * depth,
        [pltpu.VMEM((2, 2 * radius, cols, depth), F32)] * 2,
    )(main[0], edge[0], main[1], edge[1], inner, near, one, two, taps, full, back, zf, zb)


def spread_row(radius, outer_ref, middle_ref, view, row, at):
    rows = outer_ref.shape[1] + middle_ref.shape[1]
    if radius <= row < rows - radius:
        return middle_ref[view, row - radius, at, :]
    return outer_ref[view, row if row < radius else row - rows + 2 * radius, at, :]


def edge_weights(back_ref, cols):
    return jnp.concatenate(
        [back_ref[cols - 2 * EDGE :, start + side : start + side + NEAR]
         for start in range(0, 6 * cols, cols) for side in (0, cols - NEAR)], axis=1)


def rim_row_sums(radius, outer_ref, taps_ref, start, stop, shift, out_ref):
    for view in range(2):
        weights = load_taps(taps_ref, view, 2 * radius + 1)

        @tiles(start, stop)
        def _(at, inner):
            to = pl.ds(pl.multiple_of(inner.start + shift, 8), 8)

            def write_low(q, value):
                out_ref[view, q, to, :] = value

            def write_high(q, value):
                out_ref[view, radius + q, to, :] = value

            row_sums(weights, lambda r: outer_ref[view, r, at, :], write_low, radius, radius,
                     lambda q, r: r - q + 2 * radius, radius)
            row_sums(weights, lambda r: outer_ref[view, radius + r, at, :], write_high,
                     radius, radius, lambda q, r: r - q, radius)


def back_edge_kernel(radius, outer_ref, middle_ref, taps_ref, back_ref, out_ref, summed_ref):
    rows = out_ref.shape[0]
    cols, depth = outer_ref.shape[2:]
    kept = edge_weights(back_ref, cols)
    for view in range(2):
        weights = load_taps(taps_ref, view, 2 * radius + 1)
        for start, shift in ((0, 0), (cols - NEAR, NEAR)):
            @tiles(start, start + NEAR)
            def _(at, inner):
                to = pl.ds(pl.multiple_of(inner.start + shift, 8), 8)

                def write(q, value):
                    summed_ref[view, q, to, :] = value

                row_sums(weights, lambda r: spread_row(radius, outer_ref, middle_ref, view, r, at),
                         write, rows, rows, own_tap_back(radius), 16)

    @pl.loop(0, rows // 4)
    def _(step):
        for pair in range(2):
            at = 4 * step + 2 * pair
            parts = []
            for view in range(2):
                parts += stack(beside(summed_ref[view, at], summed_ref[view, at + 1]))
            total = multiply(kept, jnp.concatenate(parts, axis=0))
            for half in range(2):
                out_ref[at + half] = total[: out_ref.shape[1], half * depth : (half + 1) * depth]


def back_edge(outer, middle, weights, radius):
    _, _, cols, depth = outer.shape
    rows = outer.shape[1] + middle.shape[1]
    return call(
        functools.partial(back_edge_kernel, radius), "back_edge",
        (shape(rows, edge_width(radius), depth), shape(2, rows, 2 * NEAR, depth)),
        1 << 31, 24 * rows * NEAR * depth,
    )(outer, middle, weights[0], weights[4])


def rim_main_kernel(radius, outer_ref, rim_near_ref, taps_ref, back_ref, _after, across_ref, inside_ref, rims):
    cols, depth = outer_ref.shape[2:]
    main = cols - 2 * EDGE
    rim_row_sums(radius, outer_ref, taps_ref, NEAR, cols - NEAR, 0, rims)

    @pl.loop(0, radius // 2)
    def _(step):
        at = 2 * step
        for side, ref in zip(sides(), (across_ref, inside_ref)):
            start = side * radius
            parts = []
            for view in range(2):
                parts += stack(beside(*[
                    jnp.concatenate(
                        [rim_near_ref[view, row, 0:NEAR], rims[view, row], rim_near_ref[view, row, NEAR:]],
                        axis=0)
                    for row in (start + at, start + at + 1)
                ]))
            total = multiply(back_ref[0:main], jnp.concatenate(parts, axis=0))
            for half in range(2):
                ref[at + half] = total[:, half * depth : (half + 1) * depth]


def rim_main(outer, rim_near, weights, after, radius):
    _, _, cols, depth = outer.shape
    sent = shape(radius, cols - 2 * EDGE, depth)
    return call(
        functools.partial(rim_main_kernel, radius), "rim_main", (sent, sent), 1 << 29, 1 << 22,
        [pltpu.VMEM((2, 2 * radius, cols - 2 * NEAR, depth), F32)],
        [pl.BlockSpec(memory_space=pltpu.VMEM)] * 4 + [pl.BlockSpec(memory_space=pl.ANY)],
    )(outer, rim_near, weights[0], weights[4], after)


def back_main_kernel(radius, outer_ref, middle_ref, near_ref, taps_ref, back_ref, _after, out_ref, summed):
    rows, main, depth = out_ref.shape
    cols = outer_ref.shape[2]
    for view in range(2):
        weights = load_taps(taps_ref, view, 2 * radius + 1)

        @tiles(NEAR, cols - NEAR)
        def _(at, inner):
            def write(q, value):
                summed[view, q, inner, :] = value

            row_sums(weights, lambda r: spread_row(radius, outer_ref, middle_ref, view, r, at),
                     write, rows, rows, own_tap_back(radius), 16)

    @pl.loop(0, rows // 4)
    def _(step):
        for pair in range(2):
            at = 4 * step + 2 * pair
            parts = []
            for view in range(2):
                parts += stack(beside(*[
                    jnp.concatenate(
                        [near_ref[view, row, 0:NEAR], summed[view, row], near_ref[view, row, NEAR:]], axis=0)
                    for row in (at, at + 1)
                ]))
            total = multiply(back_ref[0:main], jnp.concatenate(parts, axis=0))
            for half in range(2):
                out_ref[at + half] = total[:, half * depth : (half + 1) * depth]


def back_main(outer, middle, near, weights, after, radius):
    _, _, cols, depth = outer.shape
    rows = outer.shape[1] + middle.shape[1]
    return call(
        functools.partial(back_main_kernel, radius), "back_main",
        shape(rows, cols - 2 * EDGE, depth), 1 << 31, 12 * rows * cols * depth,
        [pltpu.VMEM((2, rows, cols - 2 * NEAR, depth), F32)],
        [pl.BlockSpec(memory_space=pltpu.VMEM)] * 5 + [pl.BlockSpec(memory_space=pl.ANY)],
    )(outer, middle, near, weights[0], weights[4], after)


def finish_kernel(radius, main_ref, sum_ref, across_ref, inside_ref, edge_ref, edge_sum_ref,
                  first_ref, second_ref, out_ref, totals):
    rows, cols, _ = out_ref.shape
    rims = (across_ref, inside_ref)

    def row_of(row, rim):
        total = sum_ref[row]
        if rim is not None:
            total = total + rims[rim[0]][rim[1]]
        out_ref[row, EDGE : cols - EDGE] = main_ref[row] * (total * 0.5)

    each_row(rows, radius, row_of)

    @pl.loop(0, rows // 4)
    def _(block):
        for k in range(4):
            row = 4 * block + k
            totals[row] = edge_sum_ref[row, 0 : 2 * EDGE]
            add_y(radius, totals.at[row], block, k, first_ref, second_ref)
            out_ref[row, 0:EDGE] = edge_ref[row, 0:EDGE] * (totals[row, 0:EDGE] * 0.5)
            out_ref[row, cols - EDGE :] = edge_ref[row, EDGE : 2 * EDGE] * (totals[row, EDGE:] * 0.5)


def finish(main, main_sum, low, high, edge, edge_sum, from_low, from_high, radius):
    rows, width, depth = main.shape
    return call(
        functools.partial(finish_kernel, radius), "finish", shape(rows, width + 2 * EDGE, depth),
        1, 1 << 22, [pltpu.VMEM((rows, 2 * EDGE, depth), F32)],
    )(main, main_sum, low, high, edge, edge_sum, from_low, from_high)


def swap_pairs(first, second, axis):
    count = lax.axis_size(axis)

    def pairs(start):
        return [pair for i in range(start, count - 1, 2) for pair in ((i, i + 1), (i + 1, i))]

    return lax.ppermute(first, axis, pairs(1)), lax.ppermute(second, axis, pairs(0))


def local(estimate, view_one, view_two, psf_one, psf_two):
    rows, cols, depth = estimate.shape
    radius = (psf_one.shape[1] - 1) // 2
    main, first, second = load(estimate, radius)
    first, second = swap_pairs(first, second, "gy")
    weights = make_weights(psf_one, psf_two, cols, depth)
    base = EDGE
    inner, near = forward_main(main, base, weights, radius)
    first, second, near = lax.optimization_barrier((first, second, near))
    edge, across, inside = edge_first(main, first, second, radius)
    main_rims = edge_rims = swap_pairs(across, inside, "gx")
    for step in range(ITERS):
        last = step == ITERS - 1
        near, middle = forward_edge(edge, inner, near, view_one, view_two, weights, radius)
        across, inside, rim_near, outer = ratios(
            main_rims, edge_rims, inner, near, view_one, view_two, weights, radius)
        edge_rims = swap_pairs(across, inside, "gx")
        edge_sum, near = back_edge(outer, middle, weights, radius)
        edge_sum, first, second = y_messages(edge_sum, *edge_rims, not last, radius)
        across, inside = rim_main(outer, rim_near, weights, first, radius)
        main_sum = back_main(outer, middle, near, weights, first, radius)
        first, second = swap_pairs(first, second, "gy")
        main_rims = swap_pairs(across, inside, "gx")
        if not last:
            main, across, inside = main_next(main, base, main_sum, *main_rims, radius)
            base = 0
            main_rims = swap_pairs(across, inside, "gx")
            inner, near = forward_main(main, base, weights, radius)
            first, second, near = lax.optimization_barrier((first, second, near))
            edge, across, inside = edge_next(edge, edge_sum, first, second, radius)
            edge_rims = swap_pairs(across, inside, "gx")
    return finish(main, main_sum, *main_rims, edge, edge_sum, first, second, radius)


def solution(mesh):
    in_specs = (P("gx", "gy", None), P("gx", "gy", None), P("gx", "gy", None), P(), P())
    out_specs = P("gx", "gy", None)
    return jax.shard_map(local, mesh=mesh, in_specs=in_specs, out_specs=out_specs, check_vma=False)
```

```python
import functools
import jax
import jax.numpy as jnp
from jax import lax
from jax.experimental import pallas as pl
from jax.experimental.pallas import tpu as pltpu
from jax.sharding import PartitionSpec as P

ITERS = 2
F32 = jnp.float32
BF16 = jnp.bfloat16
LIMIT = 24 * 1024 * 1024
WIDE_LIMIT = 50 * 1024 * 1024
EDGE = 16
NEAR = 32


def round_up(value, unit):
    return (value + unit - 1) // unit * unit


def edge_width(radius):
    return 2 * EDGE + round_up(2 * radius, 8)


def split(value):
    high = value.astype(BF16)
    low = (value - high.astype(F32)).astype(BF16)
    return high, low


def stack(value):
    high, low = split(value)
    return [high, low, high]


def multiply(weights, value):
    return jnp.dot(weights, value, preferred_element_type=F32)


def call(kernel, name, out_shape, flops, moved, scratch=(), in_specs=None, limit=LIMIT):
    extra = {} if in_specs is None else {"in_specs": in_specs}
    return pl.pallas_call(
        kernel,
        out_shape=out_shape,
        **extra,
        scratch_shapes=list(scratch),
        compiler_params=pltpu.CompilerParams(vmem_limit_bytes=limit),
        cost_estimate=pl.CostEstimate(flops=flops, bytes_accessed=moved, transcendentals=0),
        name=name,
    )


def shape(*dims, dtype=F32):
    return jax.ShapeDtypeStruct(dims, dtype)


def weights_kernel(cols, psf_ref, taps_ref, main_ref, edge_ref, full_ref, back_ref, zf_ref, zb_ref):
    taps = psf_ref.shape[1]
    radius = (taps - 1) // 2
    depth = zf_ref.shape[1] // 2
    main = cols - 2 * EDGE
    edge = round_up(edge_width(radius), 16)
    rows = psf_ref[...] / jnp.sum(psf_ref[...], axis=1, keepdims=True)
    one, two = rows[0:3], rows[3:6]
    x_rows = (one[0:1], two[1:2])
    y_rows = (one[1:2], two[0:1])
    z_rows = (one[2:3], two[2:3])
    pitch = taps_ref.shape[0] // 2
    taps_ref[...] = jnp.zeros_like(taps_ref)
    for view in range(2):
        for tap in range(taps):
            taps_ref[view * pitch + tap : view * pitch + tap + 1, :] = jnp.broadcast_to(
                x_rows[view][:, tap : tap + 1], (1, taps_ref.shape[1])
            )

    def iota(dims, dim):
        return lax.broadcasted_iota(jnp.int32, dims, dim)

    def band(row, offset):
        total = jnp.zeros(offset.shape, F32)
        for tap in range(taps):
            total = jnp.where(offset == tap, row[:, tap : tap + 1], total)
        return total

    def edge_place(index):
        place = jnp.where(index < EDGE, index, index + cols - 2 * EDGE)
        place = jnp.where(index >= 2 * EDGE, index - 2 * EDGE - radius, place)
        place = jnp.where(index >= 2 * EDGE + radius, index - 2 * EDGE - radius + cols, place)
        return jnp.where(index >= 2 * EDGE + 2 * radius, 8 * cols, place)

    def laid(value):
        high, low = split(value)
        return jnp.concatenate([high, high, low], axis=1)

    for view in range(2):
        row = y_rows[view]
        rows = pl.ds(view * cols, cols)
        dims = (cols, main)
        left = laid(band(row, iota(dims, 0) - (iota(dims, 1) + EDGE) + radius))
        dims = (cols, edge)
        right = laid(band(row, iota(dims, 0) - edge_place(iota(dims, 1)) + radius))
        main_ref[rows, :] = left
        edge_ref[rows, :] = right
        full_ref[rows, :] = jnp.concatenate([left, right], axis=1)
        part = slice(3 * cols * view, 3 * cols * (view + 1))
        dims = (main, cols)
        back_ref[0:main, part] = laid(band(row, iota(dims, 1) - (iota(dims, 0) + EDGE) + radius))
        dims = (edge, cols)
        back_ref[main:, part] = laid(band(row, iota(dims, 1) - edge_place(iota(dims, 0)) + radius))
        dims = (depth, depth)
        first, second = iota(dims, 0), iota(dims, 1)
        for ref, offset in ((zf_ref, second - first + radius), (zb_ref, first - second + radius)):
            high, low = split(band(z_rows[view], offset))
            both = jnp.concatenate([high, low], axis=1)
            ref[view] = jnp.concatenate([both, both], axis=0)


def make_weights(psf_one, psf_two, cols, depth):
    radius = (psf_one.shape[1] - 1) // 2
    main = cols - 2 * EDGE
    edge = round_up(edge_width(radius), 16)
    return call(
        functools.partial(weights_kernel, cols), "weights",
        (
            shape(48, 128),
            shape(2 * cols, 3 * main, dtype=BF16),
            shape(2 * cols, 3 * edge, dtype=BF16),
            shape(2 * cols, 3 * (main + edge), dtype=BF16),
            shape(main + edge, 6 * cols, dtype=BF16),
            shape(2, 2 * depth, 2 * depth, dtype=BF16),
            shape(2, 2 * depth, 2 * depth, dtype=BF16),
        ), 1 << 22, 1 << 20,
    )(jnp.concatenate([psf_one, psf_two], axis=0))


def pad_rows(value):
    extra = round_up(value.shape[0], 16) - value.shape[0]
    if not extra:
        return value
    return jnp.concatenate([value, jnp.zeros((extra, value.shape[1]), value.dtype)], axis=0)


def beside(first, second):
    return jnp.concatenate([first, second], axis=1)


def depth_pass(value, matrix):
    both = multiply_depth(value, matrix)
    depth = value.shape[1]
    return both[:, :depth] + both[:, depth:]


def multiply_depth(value, matrix):
    high, low = split(value)
    return multiply(jnp.concatenate([high, low], axis=1), matrix)


def load_taps(taps_ref, view, taps):
    pitch = taps_ref.shape[0] // 2
    return [
        jnp.broadcast_to(taps_ref[view * pitch + tap : view * pitch + tap + 1, :], (8, 128))
        for tap in range(taps)
    ]


def row_sums(weights, read, write, sources, targets, tap_of, block):
    taps = len(weights)
    for start in range(0, targets, block):
        outs = range(start, min(start + block, targets))
        totals = {}
        for r in range(sources):
            used = [q for q in outs if 0 <= tap_of(q, r) < taps]
            if not used:
                continue
            value = read(r)
            for q in used:
                term = weights[tap_of(q, r)] * value
                totals[q] = totals[q] + term if q in totals else term
        for q in outs:
            write(q, totals[q])


def tiles(start, stop, unroll=1):
    def run(body):
        @pl.loop(0, (stop - start) // 8, unroll=unroll)
        def _(tile):
            inner = pl.multiple_of(tile * 8, 8)
            body(pl.ds(pl.multiple_of(start + inner, 8), 8), pl.ds(inner, 8))
    return run


def own_tap_forward(radius):
    return lambda q, r: q + radius - r


def own_tap_back(radius):
    return lambda q, r: r - q + radius


def sides(axis="gx"):
    odd = lax.rem(lax.axis_index(axis), 2)
    return odd, 1 - odd


def in_order(low, high):
    odd = sides("gy")[0] == 1
    return jnp.where(odd, high, low), jnp.where(odd, low, high)


def each_row(rows, radius, body):
    starts = [side * (rows - radius) for side in sides()]

    @pl.loop(0, radius // 2)
    def _(step):
        for k in range(2):
            row = 2 * step + k
            for which, start in enumerate(starts):
                body(start + row, (which, row))

    @pl.loop(0, (rows - 2 * radius) // 2)
    def _(step):
        for k in range(2):
            body(radius + 2 * step + k, None)


def main_pass(radius, rows, read, taps_ref, main_ref, inner_ref, near_ref, passed):
    cols = main_ref.shape[0] // 2
    depth = passed.shape[3]

    @pl.loop(0, rows // 4, unroll=2)
    def _(step):
        for pair in range(2):
            at = 4 * step + 2 * pair
            value = beside(read(at), read(at + 1))
            both = multiply(main_ref[...], jnp.concatenate(stack(value), axis=0))
            for view in range(2):
                for half in range(2):
                    block = both[view * cols : (view + 1) * cols, half * depth : (half + 1) * depth]
                    passed[view, at + half] = block[NEAR : cols - NEAR]
                    near_ref[view, at + half, 0:NEAR] = block[:NEAR]
                    near_ref[view, at + half, NEAR:] = block[cols - NEAR :]

    for view in range(2):
        weights = load_taps(taps_ref, view, 2 * radius + 1)

        @tiles(0, cols - 2 * NEAR)
        def _(at, _inner):
            def write(q, value):
                inner_ref[view, q, at, :] = value

            row_sums(weights, lambda r: passed[view, r, at, :], write, rows, rows,
                     own_tap_forward(radius), 16)


def load_kernel(radius, source_ref, current_ref, first_ref, second_ref, arrived):
    rows, cols, _ = current_ref.shape

    def copy(block):
        part = pl.ds(4 * block, 4)
        return pltpu.make_async_copy(source_ref.at[part], current_ref.at[part], arrived.at[block])

    for block in range(rows // 4):
        copy(block).start()

    @pl.loop(0, rows // 4)
    def _(block):
        copy(block).wait()
        for k in range(4):
            row = 4 * block + k
            part = slice(k * radius, (k + 1) * radius)
            first_ref[block, part], second_ref[block, part] = in_order(
                current_ref[row, 0:radius], current_ref[row, cols - radius :])


def load(estimate, radius):
    rows, cols, depth = estimate.shape
    sent = shape(rows // 4, 4 * radius, depth)
    return call(
        functools.partial(load_kernel, radius), "load", (shape(rows, cols, depth), sent, sent),
        1, 1 << 22, [pltpu.SemaphoreType.DMA((rows // 4,))],
        [pl.BlockSpec(memory_space=pltpu.HBM)], WIDE_LIMIT)(estimate)


def forward_main_kernel(radius, base, current_ref, taps_ref, main_ref, inner_ref, near_ref, passed):
    rows = current_ref.shape[0]
    width = main_ref.shape[0] // 2 - 2 * EDGE
    main_pass(radius, rows, lambda row: current_ref[row, base : base + width],
              taps_ref, main_ref, inner_ref, near_ref, passed)


def forward_main(current, base, weights, radius):
    rows, _, depth = current.shape
    cols = weights[1].shape[0] // 2
    return call(
        functools.partial(forward_main_kernel, radius, base), "forward_main",
        (shape(2, rows, cols - 2 * NEAR, depth), shape(2, rows, 2 * NEAR, depth)),
        1 << 31, 12 * rows * cols * depth, [pltpu.VMEM((2, rows, cols - 2 * NEAR, depth), F32)],
    )(current, weights[0], weights[1])


def main_next_kernel(radius, base, current_ref, sum_ref, from_across_ref, from_inside_ref,
                     next_ref, across_ref, inside_ref):
    rows, width, _ = sum_ref.shape
    rims = (from_across_ref, from_inside_ref)

    def update(row, rim):
        total = sum_ref[row]
        if rim is not None:
            total = total + rims[rim[0]][rim[1]]
        next_ref[row] = current_ref[row, base : base + width] * (total * 0.5)

    each_row(rows, radius, update)
    cut_messages(radius, next_ref, across_ref, inside_ref)


def main_next(current, base, main_sum, across, inside, radius):
    rows, width, depth = main_sum.shape
    sent = shape(radius, width, depth)
    return call(
        functools.partial(main_next_kernel, radius, base), "main_next",
        (shape(rows, width, depth), sent, sent), 1, 1 << 22)(current, main_sum, across, inside)


def cut_messages(radius, source_ref, across_ref, inside_ref):
    rows = source_ref.shape[0]
    starts = [side * (rows - radius) for side in sides()]

    @pl.loop(0, radius // 2)
    def _(step):
        for k in range(2):
            row = 2 * step + k
            for ref, start in zip((across_ref, inside_ref), starts):
                ref[row] = source_ref[start + row]


def write_messages(radius, main_row, edge_ref, across_ref, inside_ref):
    rows = edge_ref.shape[0]
    width = across_ref.shape[1] - edge_ref.shape[1]
    starts = [side * (rows - radius) for side in sides()]

    @pl.loop(0, radius // 2)
    def _(step):
        for k in range(2):
            row = 2 * step + k
            for ref, start in zip((across_ref, inside_ref), starts):
                ref[row, 0:width] = main_row(start + row)
                ref[row, width:] = edge_ref[start + row]


def edge_first_kernel(radius, current_ref, first_ref, second_ref, edge_ref, across_ref, inside_ref):
    rows, cols, depth = current_ref.shape
    rims = 2 * EDGE

    @pl.loop(0, rows // 4)
    def _(block):
        for k in range(4):
            row = 4 * block + k
            part = slice(k * radius, (k + 1) * radius)
            edge_ref[row, 0:EDGE] = current_ref[row, 0:EDGE]
            edge_ref[row, EDGE:rims] = current_ref[row, cols - EDGE :]
            edge_ref[row, edge_ref.shape[1] - 8 :] = jnp.zeros((8, depth), F32)
            low, high = in_order(first_ref[block, part], second_ref[block, part])
            edge_ref[row, rims : rims + radius] = low
            edge_ref[row, rims + radius : rims + 2 * radius] = high

    write_messages(radius, lambda at: current_ref[at, EDGE : cols - EDGE], edge_ref, across_ref, inside_ref)


def add_y(radius, total_ref, block, k, first_ref, second_ref):
    rims = 2 * EDGE

    def add(start, value):
        part = slice(start, start + radius)
        total_ref[part] = total_ref[part] + value

    part = slice(k * radius, (k + 1) * radius)
    low, high = in_order(first_ref[block, part], second_ref[block, part])
    add(0, low)
    add(rims - radius, high)
    if first_ref.shape[1] > 4 * radius:
        part = slice((4 + k) * radius, (5 + k) * radius)
        low, high = in_order(first_ref[block, part], second_ref[block, part])
        add(rims, low)
        add(rims + radius, high)


def edge_next_kernel(radius, edge_ref, sum_ref, first_ref, second_ref, next_ref,
                     across_ref, inside_ref, totals):
    @pl.loop(0, edge_ref.shape[0] // 4)
    def _(block):
        for k in range(4):
            row = 4 * block + k
            totals[row] = sum_ref[row]
            add_y(radius, totals.at[row], block, k, first_ref, second_ref)
            next_ref[row] = edge_ref[row] * (totals[row] * 0.5)

    cut_messages(radius, next_ref, across_ref, inside_ref)


def edge_shapes(rows, cols, depth, radius):
    wide = cols - 2 * EDGE + edge_width(radius)
    return (shape(rows, edge_width(radius), depth), shape(radius, wide, depth), shape(radius, wide, depth))


def edge_first(current, from_low, from_high, radius):
    outs = edge_shapes(*current.shape, radius)
    return call(functools.partial(edge_first_kernel, radius), "edge_first", outs, 1, 1 << 22)(
        current, from_low, from_high)


def edge_next(edge, edge_sum, first, second, radius):
    rows, width, depth = edge.shape
    sent = shape(radius, width, depth)
    return call(
        functools.partial(edge_next_kernel, radius), "edge_next",
        (shape(rows, width, depth), sent, sent), 1, 1 << 22,
        [pltpu.VMEM(edge.shape, F32)])(edge, edge_sum, first, second)


def y_messages_kernel(radius, whole, edge_ref, across_ref, inside_ref, sum_ref, first_ref, second_ref):
    rows, width, _ = edge_ref.shape
    refs = (across_ref, inside_ref)
    rims = 2 * EDGE

    def row_of(row, rim):
        total = edge_ref[row]
        if rim is not None:
            total = total + refs[rim[0]][rim[1]]
        sum_ref[row] = total

    each_row(rows, radius, row_of)

    @pl.loop(0, rows // 4)
    def _(block):
        for k in range(4):
            row = 4 * block + k
            part = slice(k * radius, (k + 1) * radius)
            first_ref[block, part], second_ref[block, part] = in_order(
                sum_ref[row, rims : rims + radius], sum_ref[row, rims + radius : rims + 2 * radius])
            if whole:
                part = slice((4 + k) * radius, (5 + k) * radius)
                first_ref[block, part], second_ref[block, part] = in_order(
                    sum_ref[row, 0:radius], sum_ref[row, rims - radius : rims])


def y_messages(edge_sum, low, high, whole, radius):
    rows, width, depth = edge_sum.shape
    sent = shape(rows // 4, (8 if whole else 4) * radius, depth)
    return call(
        functools.partial(y_messages_kernel, radius, whole), "y_messages",
        (shape(rows, width, depth), sent, sent), 1, 1 << 22)(edge_sum, low, high)


def ratio_block(values, seen, zf_ref, zb_ref, view):
    blurred = depth_pass(values, zf_ref[view])
    return depth_pass(seen / blurred, zb_ref[view])


def forward_edge_kernel(radius, current_ref, inner_ref, before_ref, one_ref, two_ref, taps_ref, edge_ref,
                        zf_ref, zb_ref, near_ref, middle_ref, passed):
    rows, cols, depth = one_ref.shape
    kept = jnp.concatenate(
        [edge_ref[start : start + NEAR] for start in (0, cols - NEAR, cols, 2 * cols - NEAR)], axis=0)

    @pl.loop(0, rows // 4, unroll=2)
    def _(step):
        for pair in range(2):
            at = 4 * step + 2 * pair
            value = pad_rows(beside(current_ref[at], current_ref[at + 1]))
            both = multiply(kept, jnp.concatenate(stack(value), axis=0))
            for view in range(2):
                for half in range(2):
                    passed[view, at + half] = before_ref[view, at + half] + both[
                        2 * NEAR * view : 2 * NEAR * (view + 1), half * depth : (half + 1) * depth]

    for view in range(2):
        weights = load_taps(taps_ref, view, 2 * radius + 1)

        @tiles(0, 2 * NEAR)
        def _(at, _inner):
            def write(q, value):
                near_ref[view, q, at, :] = value

            row_sums(weights, lambda r: passed[view, r, at, :], write, rows, rows,
                     own_tap_forward(radius), 16)

    @pl.loop(0, (rows - 2 * radius) // 2, unroll=3)
    def _(step):
        at = 2 * step
        for view, seen in ((0, one_ref), (1, two_ref)):
            parts = []
            for row in (radius + at, radius + at + 1):
                parts += [near_ref[view, row, 0:NEAR], inner_ref[view, row], near_ref[view, row, NEAR:]]
            value = ratio_block(
                jnp.concatenate(parts, axis=0), seen[pl.ds(radius + at, 2)].reshape(2 * cols, depth),
                zf_ref, zb_ref, view)
            middle_ref[view, pl.ds(at, 2)] = value.reshape(2, cols, depth)


def forward_edge(current, inner, before, one, two, weights, radius):
    taps, _, edge, _, _, zf, zb = weights
    rows, cols, depth = one.shape
    return call(
        functools.partial(forward_edge_kernel, radius), "forward_edge",
        (shape(2, rows, 2 * NEAR, depth), shape(2, rows - 2 * radius, cols, depth)),
        1 << 31, 24 * rows * NEAR * depth,
        [pltpu.VMEM((2, rows, 2 * NEAR, depth), F32)],
    )(current, inner, before, one, two, taps, edge, zf, zb)


def ratio_kernel(radius, base, across_ref, across_edge_ref, inside_ref, inside_edge_ref, inner_ref,
                 near_ref, one_ref, two_ref, taps_ref, full_ref, back_ref, zf_ref, zb_ref,
                 rim_across_edge_ref, rim_inside_edge_ref, rim_near_ref, outer_ref, halo, edges):
    rows, cols, depth = one_ref.shape
    main = cols - 2 * EDGE
    taps = 2 * radius + 1

    @pl.loop(0, radius // 2, unroll=5)
    def _(step):
        at = 2 * step
        for side, ref, edge_ref in zip(
            sides(), (across_ref, inside_ref), (across_edge_ref, inside_edge_ref)
        ):
            left = beside(ref[at, 0:main], ref[at + 1, 0:main])
            right = pad_rows(beside(edge_ref[at, base:], edge_ref[at + 1, base:]))
            both = multiply(full_ref[...], jnp.concatenate(stack(left) + stack(right), axis=0))
            for view in range(2):
                for half in range(2):
                    halo[view, side * radius + at + half] = both[
                        view * cols : (view + 1) * cols, half * depth : (half + 1) * depth]

    for view in range(2):
        weights = load_taps(taps_ref, view, taps)
        for ref, start, stop, shift in (
            (near_ref, 0, NEAR, 0), (inner_ref, NEAR, cols - NEAR, 0),
            (near_ref, cols - NEAR, cols, NEAR),
        ):
            @tiles(start, stop, 2)
            def _(at, inner):
                own = pl.ds(pl.multiple_of(inner.start + shift, 8), 8)

                def write_low(q, value):
                    edges[view, q, at, :] = value + ref[view, q, own, :]

                def write_high(q, value):
                    edges[view, radius + q, at, :] = value + ref[view, rows - radius + q, own, :]

                row_sums(weights, lambda r: halo[view, r, at, :], write_low, radius, radius,
                         lambda q, r: q + 2 * radius - r, radius)
                row_sums(weights, lambda r: halo[view, radius + r, at, :], write_high, radius, radius,
                         lambda q, r: q - r, radius)

    @pl.loop(0, radius // 2, unroll=5)
    def _(step):
        at = 2 * step
        for base, start in ((0, 0), (radius, rows - radius)):
            for view, seen in ((0, one_ref), (1, two_ref)):
                value = ratio_block(
                    edges[view, pl.ds(base + at, 2)].reshape(2 * cols, depth),
                    seen[pl.ds(start + at, 2)].reshape(2 * cols, depth), zf_ref, zb_ref, view)
                outer_ref[view, pl.ds(base + at, 2)] = value.reshape(2, cols, depth)

    for start, shift in ((0, 0), (cols - NEAR, NEAR)):
        rim_row_sums(radius, outer_ref, taps_ref, start, start + NEAR, shift, rim_near_ref)
    kept = edge_weights(back_ref, cols)

    @pl.loop(0, radius // 2, unroll=5)
    def _(step):
        at = 2 * step
        for side, ref in zip(sides(), (rim_across_edge_ref, rim_inside_edge_ref)):
            start = side * radius
            parts = []
            for view in range(2):
                parts += stack(beside(rim_near_ref[view, start + at], rim_near_ref[view, start + at + 1]))
            total = multiply(kept, jnp.concatenate(parts, axis=0))
            for half in range(2):
                ref[at + half] = total[: ref.shape[1], half * depth : (half + 1) * depth]


def ratios(main, edge, inner, near, one, two, weights, radius):
    taps, _, _, full, back, zf, zb = weights
    rows, cols, depth = one.shape
    base = edge[0].shape[1] - edge_width(radius)
    sent = shape(radius, edge_width(radius), depth)
    return call(
        functools.partial(ratio_kernel, radius, base), "ratios",
        (sent, sent, shape(2, 2 * radius, 2 * NEAR, depth), shape(2, 2 * radius, cols, depth)), 1 << 33, 24 * rows * cols * depth,
        [pltpu.VMEM((2, 2 * radius, cols, depth), F32)] * 2,
    )(main[0], edge[0], main[1], edge[1], inner, near, one, two, taps, full, back, zf, zb)


def spread_row(radius, outer_ref, middle_ref, view, row, at):
    rows = outer_ref.shape[1] + middle_ref.shape[1]
    if radius <= row < rows - radius:
        return middle_ref[view, row - radius, at, :]
    return outer_ref[view, row if row < radius else row - rows + 2 * radius, at, :]


def edge_weights(back_ref, cols):
    return jnp.concatenate(
        [back_ref[cols - 2 * EDGE :, start + side : start + side + NEAR]
         for start in range(0, 6 * cols, cols) for side in (0, cols - NEAR)], axis=1)


def rim_row_sums(radius, outer_ref, taps_ref, start, stop, shift, out_ref):
    for view in range(2):
        weights = load_taps(taps_ref, view, 2 * radius + 1)

        @tiles(start, stop, 2)
        def _(at, inner):
            to = pl.ds(pl.multiple_of(inner.start + shift, 8), 8)

            def write_low(q, value):
                out_ref[view, q, to, :] = value

            def write_high(q, value):
                out_ref[view, radius + q, to, :] = value

            row_sums(weights, lambda r: outer_ref[view, r, at, :], write_low, radius, radius,
                     lambda q, r: r - q + 2 * radius, radius)
            row_sums(weights, lambda r: outer_ref[view, radius + r, at, :], write_high,
                     radius, radius, lambda q, r: r - q, radius)


def back_edge_kernel(radius, outer_ref, middle_ref, taps_ref, back_ref, out_ref, summed_ref):
    rows = out_ref.shape[0]
    cols, depth = outer_ref.shape[2:]
    kept = edge_weights(back_ref, cols)
    for view in range(2):
        weights = load_taps(taps_ref, view, 2 * radius + 1)
        for start, shift in ((0, 0), (cols - NEAR, NEAR)):
            @tiles(start, start + NEAR)
            def _(at, inner):
                to = pl.ds(pl.multiple_of(inner.start + shift, 8), 8)

                def write(q, value):
                    summed_ref[view, q, to, :] = value

                row_sums(weights, lambda r: spread_row(radius, outer_ref, middle_ref, view, r, at),
                         write, rows, rows, own_tap_back(radius), 16)

    @pl.loop(0, rows // 4, unroll=2)
    def _(step):
        for pair in range(2):
            at = 4 * step + 2 * pair
            parts = []
            for view in range(2):
                parts += stack(beside(summed_ref[view, at], summed_ref[view, at + 1]))
            total = multiply(kept, jnp.concatenate(parts, axis=0))
            for half in range(2):
                out_ref[at + half] = total[: out_ref.shape[1], half * depth : (half + 1) * depth]


def back_edge(outer, middle, weights, radius):
    _, _, cols, depth = outer.shape
    rows = outer.shape[1] + middle.shape[1]
    return call(
        functools.partial(back_edge_kernel, radius), "back_edge",
        (shape(rows, edge_width(radius), depth), shape(2, rows, 2 * NEAR, depth)),
        1 << 31, 24 * rows * NEAR * depth,
    )(outer, middle, weights[0], weights[4])


def rim_main_kernel(radius, outer_ref, rim_near_ref, taps_ref, back_ref, _after, across_ref, inside_ref, rims):
    cols, depth = outer_ref.shape[2:]
    main = cols - 2 * EDGE
    rim_row_sums(radius, outer_ref, taps_ref, NEAR, cols - NEAR, 0, rims)

    @pl.loop(0, radius // 2, unroll=5)
    def _(step):
        at = 2 * step
        for side, ref in zip(sides(), (across_ref, inside_ref)):
            start = side * radius
            parts = []
            for view in range(2):
                parts += stack(beside(*[
                    jnp.concatenate(
                        [rim_near_ref[view, row, 0:NEAR], rims[view, row], rim_near_ref[view, row, NEAR:]],
                        axis=0)
                    for row in (start + at, start + at + 1)
                ]))
            total = multiply(back_ref[0:main], jnp.concatenate(parts, axis=0))
            for half in range(2):
                ref[at + half] = total[:, half * depth : (half + 1) * depth]


def rim_main(outer, rim_near, weights, after, radius):
    _, _, cols, depth = outer.shape
    sent = shape(radius, cols - 2 * EDGE, depth)
    return call(
        functools.partial(rim_main_kernel, radius), "rim_main", (sent, sent), 1 << 29, 1 << 22,
        [pltpu.VMEM((2, 2 * radius, cols - 2 * NEAR, depth), F32)],
        [pl.BlockSpec(memory_space=pltpu.VMEM)] * 4 + [pl.BlockSpec(memory_space=pl.ANY)],
    )(outer, rim_near, weights[0], weights[4], after)


def back_main_kernel(radius, outer_ref, middle_ref, near_ref, taps_ref, back_ref, _after, out_ref, summed):
    rows, main, depth = out_ref.shape
    cols = outer_ref.shape[2]
    for view in range(2):
        weights = load_taps(taps_ref, view, 2 * radius + 1)

        @tiles(NEAR, cols - NEAR)
        def _(at, inner):
            def write(q, value):
                summed[view, q, inner, :] = value

            row_sums(weights, lambda r: spread_row(radius, outer_ref, middle_ref, view, r, at),
                     write, rows, rows, own_tap_back(radius), 16)

    @pl.loop(0, rows // 4, unroll=2)
    def _(step):
        for pair in range(2):
            at = 4 * step + 2 * pair
            parts = []
            for view in range(2):
                parts += stack(beside(*[
                    jnp.concatenate(
                        [near_ref[view, row, 0:NEAR], summed[view, row], near_ref[view, row, NEAR:]], axis=0)
                    for row in (at, at + 1)
                ]))
            total = multiply(back_ref[0:main], jnp.concatenate(parts, axis=0))
            for half in range(2):
                out_ref[at + half] = total[:, half * depth : (half + 1) * depth]


def back_main(outer, middle, near, weights, after, radius):
    _, _, cols, depth = outer.shape
    rows = outer.shape[1] + middle.shape[1]
    return call(
        functools.partial(back_main_kernel, radius), "back_main",
        shape(rows, cols - 2 * EDGE, depth), 1 << 31, 12 * rows * cols * depth,
        [pltpu.VMEM((2, rows, cols - 2 * NEAR, depth), F32)],
        [pl.BlockSpec(memory_space=pltpu.VMEM)] * 5 + [pl.BlockSpec(memory_space=pl.ANY)],
    )(outer, middle, near, weights[0], weights[4], after)


def finish_kernel(radius, main_ref, sum_ref, across_ref, inside_ref, edge_ref, edge_sum_ref,
                  first_ref, second_ref, out_ref, totals):
    rows, cols, _ = out_ref.shape
    rims = (across_ref, inside_ref)

    def row_of(row, rim):
        total = sum_ref[row]
        if rim is not None:
            total = total + rims[rim[0]][rim[1]]
        out_ref[row, EDGE : cols - EDGE] = main_ref[row] * (total * 0.5)

    each_row(rows, radius, row_of)

    @pl.loop(0, rows // 4)
    def _(block):
        for k in range(4):
            row = 4 * block + k
            totals[row] = edge_sum_ref[row, 0 : 2 * EDGE]
            add_y(radius, totals.at[row], block, k, first_ref, second_ref)
            out_ref[row, 0:EDGE] = edge_ref[row, 0:EDGE] * (totals[row, 0:EDGE] * 0.5)
            out_ref[row, cols - EDGE :] = edge_ref[row, EDGE : 2 * EDGE] * (totals[row, EDGE:] * 0.5)


def finish(main, main_sum, low, high, edge, edge_sum, from_low, from_high, radius):
    rows, width, depth = main.shape
    return call(
        functools.partial(finish_kernel, radius), "finish", shape(rows, width + 2 * EDGE, depth),
        1, 1 << 22, [pltpu.VMEM((rows, 2 * EDGE, depth), F32)],
    )(main, main_sum, low, high, edge, edge_sum, from_low, from_high)


def swap_pairs(first, second, axis):
    count = lax.axis_size(axis)

    def pairs(start):
        return [pair for i in range(start, count - 1, 2) for pair in ((i, i + 1), (i + 1, i))]

    return lax.ppermute(first, axis, pairs(1)), lax.ppermute(second, axis, pairs(0))


def local(estimate, view_one, view_two, psf_one, psf_two):
    rows, cols, depth = estimate.shape
    radius = (psf_one.shape[1] - 1) // 2
    main, first, second = load(estimate, radius)
    first, second = swap_pairs(first, second, "gy")
    weights = make_weights(psf_one, psf_two, cols, depth)
    base = EDGE
    inner, near = forward_main(main, base, weights, radius)
    first, second, near = lax.optimization_barrier((first, second, near))
    edge, across, inside = edge_first(main, first, second, radius)
    main_rims = edge_rims = swap_pairs(across, inside, "gx")
    for step in range(ITERS):
        last = step == ITERS - 1
        near, middle = forward_edge(edge, inner, near, view_one, view_two, weights, radius)
        across, inside, rim_near, outer = ratios(
            main_rims, edge_rims, inner, near, view_one, view_two, weights, radius)
        edge_rims = swap_pairs(across, inside, "gx")
        edge_sum, near = back_edge(outer, middle, weights, radius)
        edge_sum, first, second = y_messages(edge_sum, *edge_rims, not last, radius)
        across, inside = rim_main(outer, rim_near, weights, first, radius)
        main_sum = back_main(outer, middle, near, weights, first, radius)
        first, second = swap_pairs(first, second, "gy")
        main_rims = swap_pairs(across, inside, "gx")
        if not last:
            main, across, inside = main_next(main, base, main_sum, *main_rims, radius)
            base = 0
            main_rims = swap_pairs(across, inside, "gx")
            inner, near = forward_main(main, base, weights, radius)
            first, second, near = lax.optimization_barrier((first, second, near))
            edge, across, inside = edge_next(edge, edge_sum, first, second, radius)
            edge_rims = swap_pairs(across, inside, "gx")
    return finish(main, main_sum, *main_rims, edge, edge_sum, first, second, radius)


def solution(mesh):
    in_specs = (P("gx", "gy", None), P("gx", "gy", None), P("gx", "gy", None), P(), P())
    out_specs = P("gx", "gy", None)
    return jax.shard_map(local, mesh=mesh, in_specs=in_specs, out_specs=out_specs, check_vma=False)
```

```python
import functools
import jax
import jax.numpy as jnp
from jax import lax
from jax.experimental import pallas as pl
from jax.experimental.pallas import tpu as pltpu
from jax.sharding import PartitionSpec as P

ITERS = 2
F32 = jnp.float32
BF16 = jnp.bfloat16
LIMIT = 24 * 1024 * 1024
WIDE_LIMIT = 50 * 1024 * 1024
EDGE = 16
NEAR = 32


def round_up(value, unit):
    return (value + unit - 1) // unit * unit


def edge_width(radius):
    return 2 * EDGE + round_up(2 * radius, 8)


def split(value):
    high = value.astype(BF16)
    low = (value - high.astype(F32)).astype(BF16)
    return high, low


def stack(value):
    high, low = split(value)
    return [high, low, high]


def multiply(weights, value):
    return jnp.dot(weights, value, preferred_element_type=F32)


def call(kernel, name, out_shape, flops, moved, scratch=(), in_specs=None, limit=LIMIT):
    extra = {} if in_specs is None else {"in_specs": in_specs}
    return pl.pallas_call(
        kernel,
        out_shape=out_shape,
        **extra,
        scratch_shapes=list(scratch),
        compiler_params=pltpu.CompilerParams(vmem_limit_bytes=limit),
        cost_estimate=pl.CostEstimate(flops=flops, bytes_accessed=moved, transcendentals=0),
        name=name,
    )


def shape(*dims, dtype=F32):
    return jax.ShapeDtypeStruct(dims, dtype)


def weights_kernel(cols, psf_ref, taps_ref, main_ref, edge_ref, full_ref, back_ref, zf_ref, zb_ref):
    taps = psf_ref.shape[1]
    radius = (taps - 1) // 2
    depth = zf_ref.shape[1] // 2
    main = cols - 2 * EDGE
    edge = round_up(edge_width(radius), 16)
    rows = psf_ref[...] / jnp.sum(psf_ref[...], axis=1, keepdims=True)
    one, two = rows[0:3], rows[3:6]
    x_rows = (one[0:1], two[1:2])
    y_rows = (one[1:2], two[0:1])
    z_rows = (one[2:3], two[2:3])
    pitch = taps_ref.shape[0] // 2
    taps_ref[...] = jnp.zeros_like(taps_ref)
    for view in range(2):
        for tap in range(taps):
            taps_ref[view * pitch + tap : view * pitch + tap + 1, :] = jnp.broadcast_to(
                x_rows[view][:, tap : tap + 1], (1, taps_ref.shape[1])
            )

    def iota(dims, dim):
        return lax.broadcasted_iota(jnp.int32, dims, dim)

    def band(row, offset):
        total = jnp.zeros(offset.shape, F32)
        for tap in range(taps):
            total = jnp.where(offset == tap, row[:, tap : tap + 1], total)
        return total

    def edge_place(index):
        place = jnp.where(index < EDGE, index, index + cols - 2 * EDGE)
        place = jnp.where(index >= 2 * EDGE, index - 2 * EDGE - radius, place)
        place = jnp.where(index >= 2 * EDGE + radius, index - 2 * EDGE - radius + cols, place)
        return jnp.where(index >= 2 * EDGE + 2 * radius, 8 * cols, place)

    def laid(value):
        high, low = split(value)
        return jnp.concatenate([high, high, low], axis=1)

    for view in range(2):
        row = y_rows[view]
        rows = pl.ds(view * cols, cols)
        dims = (cols, main)
        left = laid(band(row, iota(dims, 0) - (iota(dims, 1) + EDGE) + radius))
        dims = (cols, edge)
        right = laid(band(row, iota(dims, 0) - edge_place(iota(dims, 1)) + radius))
        main_ref[rows, :] = left
        edge_ref[rows, :] = right
        full_ref[rows, :] = jnp.concatenate([left, right], axis=1)
        part = slice(3 * cols * view, 3 * cols * (view + 1))
        dims = (main, cols)
        back_ref[0:main, part] = laid(band(row, iota(dims, 1) - (iota(dims, 0) + EDGE) + radius))
        dims = (edge, cols)
        back_ref[main:, part] = laid(band(row, iota(dims, 1) - edge_place(iota(dims, 0)) + radius))
        dims = (depth, depth)
        first, second = iota(dims, 0), iota(dims, 1)
        for ref, offset in ((zf_ref, second - first + radius), (zb_ref, first - second + radius)):
            high, low = split(band(z_rows[view], offset))
            both = jnp.concatenate([high, low], axis=1)
            ref[view] = jnp.concatenate([both, both], axis=0)


def make_weights(psf_one, psf_two, cols, depth):
    radius = (psf_one.shape[1] - 1) // 2
    main = cols - 2 * EDGE
    edge = round_up(edge_width(radius), 16)
    return call(
        functools.partial(weights_kernel, cols), "weights",
        (
            shape(48, 128),
            shape(2 * cols, 3 * main, dtype=BF16),
            shape(2 * cols, 3 * edge, dtype=BF16),
            shape(2 * cols, 3 * (main + edge), dtype=BF16),
            shape(main + edge, 6 * cols, dtype=BF16),
            shape(2, 2 * depth, 2 * depth, dtype=BF16),
            shape(2, 2 * depth, 2 * depth, dtype=BF16),
        ), 1 << 22, 1 << 20,
    )(jnp.concatenate([psf_one, psf_two], axis=0))


def pad_rows(value):
    extra = round_up(value.shape[0], 16) - value.shape[0]
    if not extra:
        return value
    return jnp.concatenate([value, jnp.zeros((extra, value.shape[1]), value.dtype)], axis=0)


def beside(first, second):
    return jnp.concatenate([first, second], axis=1)


def depth_pass(value, matrix):
    both = multiply_depth(value, matrix)
    depth = value.shape[1]
    return both[:, :depth] + both[:, depth:]


def multiply_depth(value, matrix):
    high, low = split(value)
    return multiply(jnp.concatenate([high, low], axis=1), matrix)


def load_taps(taps_ref, view, taps):
    pitch = taps_ref.shape[0] // 2
    return [
        jnp.broadcast_to(taps_ref[view * pitch + tap : view * pitch + tap + 1, :], (8, 128))
        for tap in range(taps)
    ]


def row_sums(weights, read, write, sources, targets, tap_of, block):
    taps = len(weights)
    for start in range(0, targets, block):
        outs = range(start, min(start + block, targets))
        totals = {}
        for r in range(sources):
            used = [q for q in outs if 0 <= tap_of(q, r) < taps]
            if not used:
                continue
            value = read(r)
            for q in used:
                term = weights[tap_of(q, r)] * value
                totals[q] = totals[q] + term if q in totals else term
        for q in outs:
            write(q, totals[q])


def tiles(start, stop, unroll=1):
    def run(body):
        @pl.loop(0, (stop - start) // 8, unroll=unroll)
        def _(tile):
            inner = pl.multiple_of(tile * 8, 8)
            body(pl.ds(pl.multiple_of(start + inner, 8), 8), pl.ds(inner, 8))
    return run


def own_tap_forward(radius):
    return lambda q, r: q + radius - r


def own_tap_back(radius):
    return lambda q, r: r - q + radius


def sides(axis="gx"):
    odd = lax.rem(lax.axis_index(axis), 2)
    return odd, 1 - odd


def in_order(low, high):
    odd = sides("gy")[0] == 1
    return jnp.where(odd, high, low), jnp.where(odd, low, high)


def each_row(rows, radius, body):
    starts = [side * (rows - radius) for side in sides()]

    @pl.loop(0, radius // 2, unroll=5)
    def _(step):
        for k in range(2):
            row = 2 * step + k
            for which, start in enumerate(starts):
                body(start + row, (which, row))

    @pl.loop(0, (rows - 2 * radius) // 2, unroll=3)
    def _(step):
        for k in range(2):
            body(radius + 2 * step + k, None)


def main_pass(radius, rows, read, taps_ref, main_ref, inner_ref, near_ref, passed):
    cols = main_ref.shape[0] // 2
    depth = passed.shape[3]

    @pl.loop(0, rows // 4, unroll=4)
    def _(step):
        for pair in range(2):
            at = 4 * step + 2 * pair
            value = beside(read(at), read(at + 1))
            both = multiply(main_ref[...], jnp.concatenate(stack(value), axis=0))
            for view in range(2):
                for half in range(2):
                    block = both[view * cols : (view + 1) * cols, half * depth : (half + 1) * depth]
                    passed[view, at + half] = block[NEAR : cols - NEAR]
                    near_ref[view, at + half, 0:NEAR] = block[:NEAR]
                    near_ref[view, at + half, NEAR:] = block[cols - NEAR :]

    for view in range(2):
        weights = load_taps(taps_ref, view, 2 * radius + 1)

        @tiles(0, cols - 2 * NEAR)
        def _(at, _inner):
            def write(q, value):
                inner_ref[view, q, at, :] = value

            row_sums(weights, lambda r: passed[view, r, at, :], write, rows, rows,
                     own_tap_forward(radius), 16)


def load_kernel(radius, source_ref, current_ref, first_ref, second_ref, across_ref, inside_ref, arrived):
    rows, cols, _ = current_ref.shape

    def copy(block):
        part = pl.ds(4 * block, 4)
        return pltpu.make_async_copy(source_ref.at[part], current_ref.at[part], arrived.at[block])

    for block in range(rows // 4):
        copy(block).start()

    @pl.loop(0, rows // 4, unroll=2)
    def _(block):
        copy(block).wait()
        for k in range(4):
            row = 4 * block + k
            part = slice(k * radius, (k + 1) * radius)
            first_ref[block, part], second_ref[block, part] = in_order(
                current_ref[row, 0:radius], current_ref[row, cols - radius :])

    cut_messages(radius, current_ref, across_ref, inside_ref, EDGE)


def load(estimate, radius):
    rows, cols, depth = estimate.shape
    sent = shape(rows // 4, 4 * radius, depth)
    return call(
        functools.partial(load_kernel, radius), "load",
        (shape(rows, cols, depth), sent, sent) + (shape(radius, cols - 2 * EDGE, depth),) * 2,
        1, 1 << 22, [pltpu.SemaphoreType.DMA((rows // 4,))],
        [pl.BlockSpec(memory_space=pltpu.HBM)], WIDE_LIMIT)(estimate)


def forward_main_kernel(radius, base, current_ref, taps_ref, main_ref, inner_ref, near_ref, passed):
    rows = current_ref.shape[0]
    width = main_ref.shape[0] // 2 - 2 * EDGE
    main_pass(radius, rows, lambda row: current_ref[row, base : base + width],
              taps_ref, main_ref, inner_ref, near_ref, passed)


def forward_main(current, base, weights, radius):
    rows, _, depth = current.shape
    cols = weights[1].shape[0] // 2
    return call(
        functools.partial(forward_main_kernel, radius, base), "forward_main",
        (shape(2, rows, cols - 2 * NEAR, depth), shape(2, rows, 2 * NEAR, depth)),
        1 << 31, 12 * rows * cols * depth, [pltpu.VMEM((2, rows, cols - 2 * NEAR, depth), F32)],
    )(current, weights[0], weights[1])


def main_next_kernel(radius, base, current_ref, sum_ref, from_across_ref, from_inside_ref,
                     next_ref, across_ref, inside_ref):
    rows, width, _ = sum_ref.shape
    rims = (from_across_ref, from_inside_ref)

    def update(row, rim):
        total = sum_ref[row]
        if rim is not None:
            total = total + rims[rim[0]][rim[1]]
        next_ref[row] = current_ref[row, base : base + width] * (total * 0.5)

    each_row(rows, radius, update)
    cut_messages(radius, next_ref, across_ref, inside_ref)


def main_next(current, base, main_sum, across, inside, radius):
    rows, width, depth = main_sum.shape
    sent = shape(radius, width, depth)
    return call(
        functools.partial(main_next_kernel, radius, base), "main_next",
        (shape(rows, width, depth), sent, sent), 1, 1 << 22)(current, main_sum, across, inside)


def cut_messages(radius, source_ref, across_ref, inside_ref, base=0):
    rows = source_ref.shape[0]
    width = across_ref.shape[1]
    starts = [side * (rows - radius) for side in sides()]

    @pl.loop(0, radius // 2, unroll=5)
    def _(step):
        for k in range(2):
            row = 2 * step + k
            for ref, start in zip((across_ref, inside_ref), starts):
                ref[row] = source_ref[start + row, base : base + width]


def edge_first_kernel(radius, current_ref, first_ref, second_ref, edge_ref, across_ref, inside_ref):
    rows, cols, depth = current_ref.shape
    rims = 2 * EDGE

    @pl.loop(0, rows // 4, unroll=2)
    def _(block):
        for k in range(4):
            row = 4 * block + k
            part = slice(k * radius, (k + 1) * radius)
            edge_ref[row, 0:EDGE] = current_ref[row, 0:EDGE]
            edge_ref[row, EDGE:rims] = current_ref[row, cols - EDGE :]
            edge_ref[row, edge_ref.shape[1] - 8 :] = jnp.zeros((8, depth), F32)
            low, high = in_order(first_ref[block, part], second_ref[block, part])
            edge_ref[row, rims : rims + radius] = low
            edge_ref[row, rims + radius : rims + 2 * radius] = high

    cut_messages(radius, edge_ref, across_ref, inside_ref)


def add_y(radius, total_ref, block, k, first_ref, second_ref):
    rims = 2 * EDGE

    def add(start, value):
        part = slice(start, start + radius)
        total_ref[part] = total_ref[part] + value

    part = slice(k * radius, (k + 1) * radius)
    low, high = in_order(first_ref[block, part], second_ref[block, part])
    add(0, low)
    add(rims - radius, high)
    if first_ref.shape[1] > 4 * radius:
        part = slice((4 + k) * radius, (5 + k) * radius)
        low, high = in_order(first_ref[block, part], second_ref[block, part])
        add(rims, low)
        add(rims + radius, high)


def edge_next_kernel(radius, edge_ref, sum_ref, first_ref, second_ref, next_ref,
                     across_ref, inside_ref, totals):
    @pl.loop(0, edge_ref.shape[0] // 4, unroll=2)
    def _(block):
        for k in range(4):
            row = 4 * block + k
            totals[row] = sum_ref[row]
            add_y(radius, totals.at[row], block, k, first_ref, second_ref)
            next_ref[row] = edge_ref[row] * (totals[row] * 0.5)

    cut_messages(radius, next_ref, across_ref, inside_ref)


def edge_first(current, first, second, radius):
    rows, _, depth = current.shape
    sent = shape(radius, edge_width(radius), depth)
    return call(
        functools.partial(edge_first_kernel, radius), "edge_first",
        (shape(rows, edge_width(radius), depth), sent, sent), 1, 1 << 22)(current, first, second)


def edge_next(edge, edge_sum, first, second, radius):
    rows, width, depth = edge.shape
    sent = shape(radius, width, depth)
    return call(
        functools.partial(edge_next_kernel, radius), "edge_next",
        (shape(rows, width, depth), sent, sent), 1, 1 << 22,
        [pltpu.VMEM(edge.shape, F32)])(edge, edge_sum, first, second)


def y_messages_kernel(radius, whole, edge_ref, across_ref, inside_ref, sum_ref, first_ref, second_ref):
    rows, width, _ = edge_ref.shape
    refs = (across_ref, inside_ref)
    rims = 2 * EDGE

    def row_of(row, rim):
        total = edge_ref[row]
        if rim is not None:
            total = total + refs[rim[0]][rim[1]]
        sum_ref[row] = total

    each_row(rows, radius, row_of)

    @pl.loop(0, rows // 4, unroll=2)
    def _(block):
        for k in range(4):
            row = 4 * block + k
            part = slice(k * radius, (k + 1) * radius)
            first_ref[block, part], second_ref[block, part] = in_order(
                sum_ref[row, rims : rims + radius], sum_ref[row, rims + radius : rims + 2 * radius])
            if whole:
                part = slice((4 + k) * radius, (5 + k) * radius)
                first_ref[block, part], second_ref[block, part] = in_order(
                    sum_ref[row, 0:radius], sum_ref[row, rims - radius : rims])


def y_messages(edge_sum, low, high, whole, radius):
    rows, width, depth = edge_sum.shape
    sent = shape(rows // 4, (8 if whole else 4) * radius, depth)
    return call(
        functools.partial(y_messages_kernel, radius, whole), "y_messages",
        (shape(rows, width, depth), sent, sent), 1, 1 << 22)(edge_sum, low, high)


def ratio_block(values, seen, zf_ref, zb_ref, view):
    blurred = depth_pass(values, zf_ref[view])
    return depth_pass(seen / blurred, zb_ref[view])


def forward_edge_kernel(radius, current_ref, inner_ref, before_ref, one_ref, two_ref, taps_ref, edge_ref,
                        zf_ref, zb_ref, near_ref, middle_ref, passed):
    rows, cols, depth = one_ref.shape
    kept = jnp.concatenate(
        [edge_ref[start : start + NEAR] for start in (0, cols - NEAR, cols, 2 * cols - NEAR)], axis=0)

    @pl.loop(0, rows // 4, unroll=4)
    def _(step):
        for pair in range(2):
            at = 4 * step + 2 * pair
            value = pad_rows(beside(current_ref[at], current_ref[at + 1]))
            both = multiply(kept, jnp.concatenate(stack(value), axis=0))
            for view in range(2):
                for half in range(2):
                    passed[view, at + half] = before_ref[view, at + half] + both[
                        2 * NEAR * view : 2 * NEAR * (view + 1), half * depth : (half + 1) * depth]

    for view in range(2):
        weights = load_taps(taps_ref, view, 2 * radius + 1)

        @tiles(0, 2 * NEAR)
        def _(at, _inner):
            def write(q, value):
                near_ref[view, q, at, :] = value

            row_sums(weights, lambda r: passed[view, r, at, :], write, rows, rows,
                     own_tap_forward(radius), 16)

    @pl.loop(0, (rows - 2 * radius) // 2, unroll=3)
    def _(step):
        at = 2 * step
        for view, seen in ((0, one_ref), (1, two_ref)):
            parts = []
            for row in (radius + at, radius + at + 1):
                parts += [near_ref[view, row, 0:NEAR], inner_ref[view, row], near_ref[view, row, NEAR:]]
            value = ratio_block(
                jnp.concatenate(parts, axis=0), seen[pl.ds(radius + at, 2)].reshape(2 * cols, depth),
                zf_ref, zb_ref, view)
            middle_ref[view, pl.ds(at, 2)] = value.reshape(2, cols, depth)


def forward_edge(current, inner, before, one, two, weights, radius):
    taps, _, edge, _, _, zf, zb = weights
    rows, cols, depth = one.shape
    return call(
        functools.partial(forward_edge_kernel, radius), "forward_edge",
        (shape(2, rows, 2 * NEAR, depth), shape(2, rows - 2 * radius, cols, depth)),
        1 << 31, 24 * rows * NEAR * depth,
        [pltpu.VMEM((2, rows, 2 * NEAR, depth), F32)],
    )(current, inner, before, one, two, taps, edge, zf, zb)


def ratio_kernel(radius, across_ref, across_edge_ref, inside_ref, inside_edge_ref, inner_ref,
                 near_ref, one_ref, two_ref, taps_ref, full_ref, back_ref, zf_ref, zb_ref,
                 rim_across_edge_ref, rim_inside_edge_ref, rim_near_ref, outer_ref, halo, edges):
    rows, cols, depth = one_ref.shape
    main = cols - 2 * EDGE
    taps = 2 * radius + 1

    @pl.loop(0, radius // 2, unroll=5)
    def _(step):
        at = 2 * step
        for side, ref, edge_ref in zip(
            sides(), (across_ref, inside_ref), (across_edge_ref, inside_edge_ref)
        ):
            left = beside(ref[at, 0:main], ref[at + 1, 0:main])
            right = pad_rows(beside(edge_ref[at], edge_ref[at + 1]))
            both = multiply(full_ref[...], jnp.concatenate(stack(left) + stack(right), axis=0))
            for view in range(2):
                for half in range(2):
                    halo[view, side * radius + at + half] = both[
                        view * cols : (view + 1) * cols, half * depth : (half + 1) * depth]

    for view in range(2):
        weights = load_taps(taps_ref, view, taps)
        for ref, start, stop, shift in (
            (near_ref, 0, NEAR, 0), (inner_ref, NEAR, cols - NEAR, 0),
            (near_ref, cols - NEAR, cols, NEAR),
        ):
            @tiles(start, stop, 4)
            def _(at, inner):
                own = pl.ds(pl.multiple_of(inner.start + shift, 8), 8)

                def write_low(q, value):
                    edges[view, q, at, :] = value + ref[view, q, own, :]

                def write_high(q, value):
                    edges[view, radius + q, at, :] = value + ref[view, rows - radius + q, own, :]

                row_sums(weights, lambda r: halo[view, r, at, :], write_low, radius, radius,
                         lambda q, r: q + 2 * radius - r, radius)
                row_sums(weights, lambda r: halo[view, radius + r, at, :], write_high, radius, radius,
                         lambda q, r: q - r, radius)

    @pl.loop(0, radius // 2, unroll=5)
    def _(step):
        at = 2 * step
        for base, start in ((0, 0), (radius, rows - radius)):
            for view, seen in ((0, one_ref), (1, two_ref)):
                value = ratio_block(
                    edges[view, pl.ds(base + at, 2)].reshape(2 * cols, depth),
                    seen[pl.ds(start + at, 2)].reshape(2 * cols, depth), zf_ref, zb_ref, view)
                outer_ref[view, pl.ds(base + at, 2)] = value.reshape(2, cols, depth)

    for start, shift in ((0, 0), (cols - NEAR, NEAR)):
        rim_row_sums(radius, outer_ref, taps_ref, start, start + NEAR, shift, rim_near_ref)
    kept = edge_weights(back_ref, cols)

    @pl.loop(0, radius // 2, unroll=5)
    def _(step):
        at = 2 * step
        for side, ref in zip(sides(), (rim_across_edge_ref, rim_inside_edge_ref)):
            start = side * radius
            parts = []
            for view in range(2):
                parts += stack(beside(rim_near_ref[view, start + at], rim_near_ref[view, start + at + 1]))
            total = multiply(kept, jnp.concatenate(parts, axis=0))
            for half in range(2):
                ref[at + half] = total[: ref.shape[1], half * depth : (half + 1) * depth]


def ratios(main, edge, inner, near, one, two, weights, radius):
    taps, _, _, full, back, zf, zb = weights
    rows, cols, depth = one.shape
    sent = shape(radius, edge_width(radius), depth)
    return call(
        functools.partial(ratio_kernel, radius), "ratios",
        (sent, sent, shape(2, 2 * radius, 2 * NEAR, depth), shape(2, 2 * radius, cols, depth)), 1 << 33, 24 * rows * cols * depth,
        [pltpu.VMEM((2, 2 * radius, cols, depth), F32)] * 2,
    )(main[0], edge[0], main[1], edge[1], inner, near, one, two, taps, full, back, zf, zb)


def spread_row(radius, outer_ref, middle_ref, view, row, at):
    rows = outer_ref.shape[1] + middle_ref.shape[1]
    if radius <= row < rows - radius:
        return middle_ref[view, row - radius, at, :]
    return outer_ref[view, row if row < radius else row - rows + 2 * radius, at, :]


def edge_weights(back_ref, cols):
    return jnp.concatenate(
        [back_ref[cols - 2 * EDGE :, start + side : start + side + NEAR]
         for start in range(0, 6 * cols, cols) for side in (0, cols - NEAR)], axis=1)


def rim_row_sums(radius, outer_ref, taps_ref, start, stop, shift, out_ref):
    for view in range(2):
        weights = load_taps(taps_ref, view, 2 * radius + 1)

        @tiles(start, stop, 4)
        def _(at, inner):
            to = pl.ds(pl.multiple_of(inner.start + shift, 8), 8)

            def write_low(q, value):
                out_ref[view, q, to, :] = value

            def write_high(q, value):
                out_ref[view, radius + q, to, :] = value

            row_sums(weights, lambda r: outer_ref[view, r, at, :], write_low, radius, radius,
                     lambda q, r: r - q + 2 * radius, radius)
            row_sums(weights, lambda r: outer_ref[view, radius + r, at, :], write_high,
                     radius, radius, lambda q, r: r - q, radius)


def back_edge_kernel(radius, outer_ref, middle_ref, taps_ref, back_ref, out_ref, summed_ref):
    rows = out_ref.shape[0]
    cols, depth = outer_ref.shape[2:]
    kept = edge_weights(back_ref, cols)
    for view in range(2):
        weights = load_taps(taps_ref, view, 2 * radius + 1)
        for start, shift in ((0, 0), (cols - NEAR, NEAR)):
            @tiles(start, start + NEAR)
            def _(at, inner):
                to = pl.ds(pl.multiple_of(inner.start + shift, 8), 8)

                def write(q, value):
                    summed_ref[view, q, to, :] = value

                row_sums(weights, lambda r: spread_row(radius, outer_ref, middle_ref, view, r, at),
                         write, rows, rows, own_tap_back(radius), 16)

    @pl.loop(0, rows // 4, unroll=4)
    def _(step):
        for pair in range(2):
            at = 4 * step + 2 * pair
            parts = []
            for view in range(2):
                parts += stack(beside(summed_ref[view, at], summed_ref[view, at + 1]))
            total = multiply(kept, jnp.concatenate(parts, axis=0))
            for half in range(2):
                out_ref[at + half] = total[: out_ref.shape[1], half * depth : (half + 1) * depth]


def back_edge(outer, middle, weights, radius):
    _, _, cols, depth = outer.shape
    rows = outer.shape[1] + middle.shape[1]
    return call(
        functools.partial(back_edge_kernel, radius), "back_edge",
        (shape(rows, edge_width(radius), depth), shape(2, rows, 2 * NEAR, depth)),
        1 << 31, 24 * rows * NEAR * depth,
    )(outer, middle, weights[0], weights[4])


def rim_main_kernel(radius, outer_ref, rim_near_ref, taps_ref, back_ref, _after, across_ref, inside_ref, rims):
    cols, depth = outer_ref.shape[2:]
    main = cols - 2 * EDGE
    rim_row_sums(radius, outer_ref, taps_ref, NEAR, cols - NEAR, 0, rims)

    @pl.loop(0, radius // 2, unroll=5)
    def _(step):
        at = 2 * step
        for side, ref in zip(sides(), (across_ref, inside_ref)):
            start = side * radius
            parts = []
            for view in range(2):
                parts += stack(beside(*[
                    jnp.concatenate(
                        [rim_near_ref[view, row, 0:NEAR], rims[view, row], rim_near_ref[view, row, NEAR:]],
                        axis=0)
                    for row in (start + at, start + at + 1)
                ]))
            total = multiply(back_ref[0:main], jnp.concatenate(parts, axis=0))
            for half in range(2):
                ref[at + half] = total[:, half * depth : (half + 1) * depth]


def rim_main(outer, rim_near, weights, after, radius):
    _, _, cols, depth = outer.shape
    sent = shape(radius, cols - 2 * EDGE, depth)
    return call(
        functools.partial(rim_main_kernel, radius), "rim_main", (sent, sent), 1 << 29, 1 << 22,
        [pltpu.VMEM((2, 2 * radius, cols - 2 * NEAR, depth), F32)],
        [pl.BlockSpec(memory_space=pltpu.VMEM)] * 4 + [pl.BlockSpec(memory_space=pl.ANY)],
    )(outer, rim_near, weights[0], weights[4], after)


def back_main_kernel(radius, outer_ref, middle_ref, near_ref, taps_ref, back_ref, _after, out_ref, summed):
    rows, main, depth = out_ref.shape
    cols = outer_ref.shape[2]
    for view in range(2):
        weights = load_taps(taps_ref, view, 2 * radius + 1)

        @tiles(NEAR, cols - NEAR)
        def _(at, inner):
            def write(q, value):
                summed[view, q, inner, :] = value

            row_sums(weights, lambda r: spread_row(radius, outer_ref, middle_ref, view, r, at),
                     write, rows, rows, own_tap_back(radius), 16)

    @pl.loop(0, rows // 4, unroll=4)
    def _(step):
        for pair in range(2):
            at = 4 * step + 2 * pair
            parts = []
            for view in range(2):
                parts += stack(beside(*[
                    jnp.concatenate(
                        [near_ref[view, row, 0:NEAR], summed[view, row], near_ref[view, row, NEAR:]], axis=0)
                    for row in (at, at + 1)
                ]))
            total = multiply(back_ref[0:main], jnp.concatenate(parts, axis=0))
            for half in range(2):
                out_ref[at + half] = total[:, half * depth : (half + 1) * depth]


def back_main(outer, middle, near, weights, after, radius):
    _, _, cols, depth = outer.shape
    rows = outer.shape[1] + middle.shape[1]
    return call(
        functools.partial(back_main_kernel, radius), "back_main",
        shape(rows, cols - 2 * EDGE, depth), 1 << 31, 12 * rows * cols * depth,
        [pltpu.VMEM((2, rows, cols - 2 * NEAR, depth), F32)],
        [pl.BlockSpec(memory_space=pltpu.VMEM)] * 5 + [pl.BlockSpec(memory_space=pl.ANY)],
    )(outer, middle, near, weights[0], weights[4], after)


def finish_kernel(radius, main_ref, sum_ref, across_ref, inside_ref, edge_ref, edge_sum_ref,
                  first_ref, second_ref, out_ref, totals):
    rows, cols, _ = out_ref.shape
    rims = (across_ref, inside_ref)

    def row_of(row, rim):
        total = sum_ref[row]
        if rim is not None:
            total = total + rims[rim[0]][rim[1]]
        out_ref[row, EDGE : cols - EDGE] = main_ref[row] * (total * 0.5)

    each_row(rows, radius, row_of)

    @pl.loop(0, rows // 4, unroll=2)
    def _(block):
        for k in range(4):
            row = 4 * block + k
            totals[row] = edge_sum_ref[row, 0 : 2 * EDGE]
            add_y(radius, totals.at[row], block, k, first_ref, second_ref)
            out_ref[row, 0:EDGE] = edge_ref[row, 0:EDGE] * (totals[row, 0:EDGE] * 0.5)
            out_ref[row, cols - EDGE :] = edge_ref[row, EDGE : 2 * EDGE] * (totals[row, EDGE:] * 0.5)


def finish(main, main_sum, low, high, edge, edge_sum, from_low, from_high, radius):
    rows, width, depth = main.shape
    return call(
        functools.partial(finish_kernel, radius), "finish", shape(rows, width + 2 * EDGE, depth),
        1, 1 << 22, [pltpu.VMEM((rows, 2 * EDGE, depth), F32)],
    )(main, main_sum, low, high, edge, edge_sum, from_low, from_high)


def swap_pairs(first, second, axis):
    count = lax.axis_size(axis)

    def pairs(start):
        return [pair for i in range(start, count - 1, 2) for pair in ((i, i + 1), (i + 1, i))]

    return lax.ppermute(first, axis, pairs(1)), lax.ppermute(second, axis, pairs(0))


def local(estimate, view_one, view_two, psf_one, psf_two):
    rows, cols, depth = estimate.shape
    radius = (psf_one.shape[1] - 1) // 2
    main, first, second, across, inside = load(estimate, radius)
    first, second = swap_pairs(first, second, "gy")
    main_rims = swap_pairs(across, inside, "gx")
    weights = make_weights(psf_one, psf_two, cols, depth)
    base = EDGE
    inner, near = forward_main(main, base, weights, radius)
    first, second, near = lax.optimization_barrier((first, second, near))
    edge, across, inside = edge_first(main, first, second, radius)
    edge_rims = swap_pairs(across, inside, "gx")
    for step in range(ITERS):
        last = step == ITERS - 1
        near, middle = forward_edge(edge, inner, near, view_one, view_two, weights, radius)
        across, inside, rim_near, outer = ratios(
            main_rims, edge_rims, inner, near, view_one, view_two, weights, radius)
        edge_rims = swap_pairs(across, inside, "gx")
        edge_sum, near = back_edge(outer, middle, weights, radius)
        edge_sum, first, second = y_messages(edge_sum, *edge_rims, not last, radius)
        across, inside = rim_main(outer, rim_near, weights, first, radius)
        main_sum = back_main(outer, middle, near, weights, first, radius)
        first, second = swap_pairs(first, second, "gy")
        main_rims = swap_pairs(across, inside, "gx")
        if not last:
            main, across, inside = main_next(main, base, main_sum, *main_rims, radius)
            base = 0
            main_rims = swap_pairs(across, inside, "gx")
            inner, near = forward_main(main, base, weights, radius)
            first, second, near = lax.optimization_barrier((first, second, near))
            edge, across, inside = edge_next(edge, edge_sum, first, second, radius)
            edge_rims = swap_pairs(across, inside, "gx")
    return finish(main, main_sum, *main_rims, edge, edge_sum, first, second, radius)


def solution(mesh):
    in_specs = (P("gx", "gy", None), P("gx", "gy", None), P("gx", "gy", None), P(), P())
    out_specs = P("gx", "gy", None)
    return jax.shard_map(local, mesh=mesh, in_specs=in_specs, out_specs=out_specs, check_vma=False)
```

```python
import functools
import jax
import jax.numpy as jnp
from jax import lax
from jax.experimental import pallas as pl
from jax.experimental.pallas import tpu as pltpu
from jax.sharding import PartitionSpec as P

ITERS = 2
F32 = jnp.float32
BF16 = jnp.bfloat16
LIMIT = 24 * 1024 * 1024
WIDE_LIMIT = 50 * 1024 * 1024
EDGE = 16
NEAR = 32


def round_up(value, unit):
    return (value + unit - 1) // unit * unit


def edge_width(radius):
    return 2 * EDGE + round_up(2 * radius, 8)


def split(value):
    high = value.astype(BF16)
    low = (value - high.astype(F32)).astype(BF16)
    return high, low


def stack(value):
    high, low = split(value)
    return [high, low, high]


def multiply(weights, value):
    return jnp.dot(weights, value, preferred_element_type=F32)


def call(kernel, name, out_shape, flops, moved, scratch=(), in_specs=None, limit=LIMIT):
    extra = {} if in_specs is None else {"in_specs": in_specs}
    return pl.pallas_call(
        kernel,
        out_shape=out_shape,
        **extra,
        scratch_shapes=list(scratch),
        compiler_params=pltpu.CompilerParams(vmem_limit_bytes=limit),
        cost_estimate=pl.CostEstimate(flops=flops, bytes_accessed=moved, transcendentals=0),
        name=name,
    )


def shape(*dims, dtype=F32):
    return jax.ShapeDtypeStruct(dims, dtype)


def weights_kernel(cols, psf_ref, taps_ref, main_ref, edge_ref, full_ref, back_ref, zf_ref, zb_ref):
    taps = psf_ref.shape[1]
    radius = (taps - 1) // 2
    depth = zf_ref.shape[1] // 2
    main = cols - 2 * EDGE
    edge = round_up(edge_width(radius), 16)
    rows = psf_ref[...] / jnp.sum(psf_ref[...], axis=1, keepdims=True)
    one, two = rows[0:3], rows[3:6]
    x_rows = (one[0:1], two[1:2])
    y_rows = (one[1:2], two[0:1])
    z_rows = (one[2:3], two[2:3])
    pitch = taps_ref.shape[0] // 2
    taps_ref[...] = jnp.zeros_like(taps_ref)
    for view in range(2):
        for tap in range(taps):
            taps_ref[view * pitch + tap : view * pitch + tap + 1, :] = jnp.broadcast_to(
                x_rows[view][:, tap : tap + 1], (1, taps_ref.shape[1])
            )

    def iota(dims, dim):
        return lax.broadcasted_iota(jnp.int32, dims, dim)

    def band(row, offset):
        total = jnp.zeros(offset.shape, F32)
        for tap in range(taps):
            total = jnp.where(offset == tap, row[:, tap : tap + 1], total)
        return total

    def edge_place(index):
        place = jnp.where(index < EDGE, index, index + cols - 2 * EDGE)
        place = jnp.where(index >= 2 * EDGE, index - 2 * EDGE - radius, place)
        place = jnp.where(index >= 2 * EDGE + radius, index - 2 * EDGE - radius + cols, place)
        return jnp.where(index >= 2 * EDGE + 2 * radius, 8 * cols, place)

    def laid(value):
        high, low = split(value)
        return jnp.concatenate([high, high, low], axis=1)

    for view in range(2):
        row = y_rows[view]
        rows = pl.ds(view * cols, cols)
        dims = (cols, main)
        left = laid(band(row, iota(dims, 0) - (iota(dims, 1) + EDGE) + radius))
        dims = (cols, edge)
        right = laid(band(row, iota(dims, 0) - edge_place(iota(dims, 1)) + radius))
        main_ref[rows, :] = left
        edge_ref[rows, :] = right
        full_ref[rows, :] = jnp.concatenate([left, right], axis=1)
        part = slice(3 * cols * view, 3 * cols * (view + 1))
        dims = (main, cols)
        back_ref[0:main, part] = laid(band(row, iota(dims, 1) - (iota(dims, 0) + EDGE) + radius))
        dims = (edge, cols)
        back_ref[main:, part] = laid(band(row, iota(dims, 1) - edge_place(iota(dims, 0)) + radius))
        dims = (depth, depth)
        first, second = iota(dims, 0), iota(dims, 1)
        for ref, offset in ((zf_ref, second - first + radius), (zb_ref, first - second + radius)):
            high, low = split(band(z_rows[view], offset))
            both = jnp.concatenate([high, low], axis=1)
            ref[view] = jnp.concatenate([both, both], axis=0)


def make_weights(psf_one, psf_two, cols, depth):
    radius = (psf_one.shape[1] - 1) // 2
    main = cols - 2 * EDGE
    edge = round_up(edge_width(radius), 16)
    return call(
        functools.partial(weights_kernel, cols), "weights",
        (
            shape(48, 128),
            shape(2 * cols, 3 * main, dtype=BF16),
            shape(2 * cols, 3 * edge, dtype=BF16),
            shape(2 * cols, 3 * (main + edge), dtype=BF16),
            shape(main + edge, 6 * cols, dtype=BF16),
            shape(2, 2 * depth, 2 * depth, dtype=BF16),
            shape(2, 2 * depth, 2 * depth, dtype=BF16),
        ), 1 << 22, 1 << 20,
    )(jnp.concatenate([psf_one, psf_two], axis=0))


def pad_rows(value):
    extra = round_up(value.shape[0], 16) - value.shape[0]
    if not extra:
        return value
    return jnp.concatenate([value, jnp.zeros((extra, value.shape[1]), value.dtype)], axis=0)


def beside(first, second):
    return jnp.concatenate([first, second], axis=1)


def depth_pass(value, matrix):
    both = multiply_depth(value, matrix)
    depth = value.shape[1]
    return both[:, :depth] + both[:, depth:]


def multiply_depth(value, matrix):
    high, low = split(value)
    return multiply(jnp.concatenate([high, low], axis=1), matrix)


def load_taps(taps_ref, view, taps):
    pitch = taps_ref.shape[0] // 2
    return [
        jnp.broadcast_to(taps_ref[view * pitch + tap : view * pitch + tap + 1, :], (8, 128))
        for tap in range(taps)
    ]


def row_sums(weights, read, write, sources, targets, tap_of, block):
    taps = len(weights)
    for start in range(0, targets, block):
        outs = range(start, min(start + block, targets))
        totals = {}
        for r in range(sources):
            used = [q for q in outs if 0 <= tap_of(q, r) < taps]
            if not used:
                continue
            value = read(r)
            for q in used:
                term = weights[tap_of(q, r)] * value
                totals[q] = totals[q] + term if q in totals else term
        for q in outs:
            write(q, totals[q])


def tiles(start, stop, unroll=1):
    def run(body):
        @pl.loop(0, (stop - start) // 8, unroll=unroll)
        def _(tile):
            inner = pl.multiple_of(tile * 8, 8)
            body(pl.ds(pl.multiple_of(start + inner, 8), 8), pl.ds(inner, 8))
    return run


def own_tap_forward(radius):
    return lambda q, r: q + radius - r


def own_tap_back(radius):
    return lambda q, r: r - q + radius


def sides(axis="gx"):
    odd = lax.rem(lax.axis_index(axis), 2)
    return odd, 1 - odd


def in_order(low, high):
    odd = sides("gy")[0] == 1
    return jnp.where(odd, high, low), jnp.where(odd, low, high)


def each_row(rows, radius, body):
    starts = [side * (rows - radius) for side in sides()]

    @pl.loop(0, radius // 2, unroll=5)
    def _(step):
        for k in range(2):
            row = 2 * step + k
            for which, start in enumerate(starts):
                body(start + row, (which, row))

    @pl.loop(0, (rows - 2 * radius) // 2, unroll=3)
    def _(step):
        for k in range(2):
            body(radius + 2 * step + k, None)


def main_pass(radius, rows, read, taps_ref, main_ref, inner_ref, near_ref, passed):
    cols = main_ref.shape[0] // 2
    depth = passed.shape[3]

    @pl.loop(0, rows // 4, unroll=4)
    def _(step):
        for pair in range(2):
            at = 4 * step + 2 * pair
            value = beside(read(at), read(at + 1))
            both = multiply(main_ref[...], jnp.concatenate(stack(value), axis=0))
            for view in range(2):
                for half in range(2):
                    block = both[view * cols : (view + 1) * cols, half * depth : (half + 1) * depth]
                    passed[view, at + half] = block[NEAR : cols - NEAR]
                    near_ref[view, at + half, 0:NEAR] = block[:NEAR]
                    near_ref[view, at + half, NEAR:] = block[cols - NEAR :]

    for view in range(2):
        weights = load_taps(taps_ref, view, 2 * radius + 1)

        @tiles(0, cols - 2 * NEAR, 2)
        def _(at, _inner):
            def write(q, value):
                inner_ref[view, q, at, :] = value

            row_sums(weights, lambda r: passed[view, r, at, :], write, rows, rows,
                     own_tap_forward(radius), 16)


def load_kernel(radius, source_ref, current_ref, first_ref, second_ref, across_ref, inside_ref, arrived):
    rows, cols, _ = current_ref.shape

    def copy(block):
        part = pl.ds(4 * block, 4)
        return pltpu.make_async_copy(source_ref.at[part], current_ref.at[part], arrived.at[block])

    for block in range(rows // 4):
        copy(block).start()

    @pl.loop(0, rows // 4, unroll=2)
    def _(block):
        copy(block).wait()
        for k in range(4):
            row = 4 * block + k
            part = slice(k * radius, (k + 1) * radius)
            first_ref[block, part], second_ref[block, part] = in_order(
                current_ref[row, 0:radius], current_ref[row, cols - radius :])

    cut_messages(radius, current_ref, across_ref, inside_ref, EDGE)


def load(estimate, radius):
    rows, cols, depth = estimate.shape
    sent = shape(rows // 4, 4 * radius, depth)
    return call(
        functools.partial(load_kernel, radius), "load",
        (shape(rows, cols, depth), sent, sent) + (shape(radius, cols - 2 * EDGE, depth),) * 2,
        1, 1 << 22, [pltpu.SemaphoreType.DMA((rows // 4,))],
        [pl.BlockSpec(memory_space=pltpu.HBM)], WIDE_LIMIT)(estimate)


def forward_main_kernel(radius, base, current_ref, taps_ref, main_ref, inner_ref, near_ref, passed):
    rows = current_ref.shape[0]
    width = main_ref.shape[0] // 2 - 2 * EDGE
    main_pass(radius, rows, lambda row: current_ref[row, base : base + width],
              taps_ref, main_ref, inner_ref, near_ref, passed)


def forward_main(current, base, weights, radius):
    rows, _, depth = current.shape
    cols = weights[1].shape[0] // 2
    return call(
        functools.partial(forward_main_kernel, radius, base), "forward_main",
        (shape(2, rows, cols - 2 * NEAR, depth), shape(2, rows, 2 * NEAR, depth)),
        1 << 31, 12 * rows * cols * depth, [pltpu.VMEM((2, rows, cols - 2 * NEAR, depth), F32)],
    )(current, weights[0], weights[1])


def main_next_kernel(radius, base, current_ref, sum_ref, from_across_ref, from_inside_ref,
                     next_ref, across_ref, inside_ref):
    rows, width, _ = sum_ref.shape
    rims = (from_across_ref, from_inside_ref)

    def update(row, rim):
        total = sum_ref[row]
        if rim is not None:
            total = total + rims[rim[0]][rim[1]]
        next_ref[row] = current_ref[row, base : base + width] * (total * 0.5)

    each_row(rows, radius, update)
    cut_messages(radius, next_ref, across_ref, inside_ref)


def main_next(current, base, main_sum, across, inside, radius):
    rows, width, depth = main_sum.shape
    sent = shape(radius, width, depth)
    return call(
        functools.partial(main_next_kernel, radius, base), "main_next",
        (shape(rows, width, depth), sent, sent), 1, 1 << 22)(current, main_sum, across, inside)


def cut_messages(radius, source_ref, across_ref, inside_ref, base=0):
    rows = source_ref.shape[0]
    width = across_ref.shape[1]
    starts = [side * (rows - radius) for side in sides()]

    @pl.loop(0, radius // 2, unroll=5)
    def _(step):
        for k in range(2):
            row = 2 * step + k
            for ref, start in zip((across_ref, inside_ref), starts):
                ref[row] = source_ref[start + row, base : base + width]


def edge_first_kernel(radius, current_ref, first_ref, second_ref, edge_ref, across_ref, inside_ref):
    rows, cols, depth = current_ref.shape
    rims = 2 * EDGE

    @pl.loop(0, rows // 4, unroll=2)
    def _(block):
        for k in range(4):
            row = 4 * block + k
            part = slice(k * radius, (k + 1) * radius)
            edge_ref[row, 0:EDGE] = current_ref[row, 0:EDGE]
            edge_ref[row, EDGE:rims] = current_ref[row, cols - EDGE :]
            edge_ref[row, edge_ref.shape[1] - 8 :] = jnp.zeros((8, depth), F32)
            low, high = in_order(first_ref[block, part], second_ref[block, part])
            edge_ref[row, rims : rims + radius] = low
            edge_ref[row, rims + radius : rims + 2 * radius] = high

    cut_messages(radius, edge_ref, across_ref, inside_ref)


def add_y(radius, total_ref, block, k, first_ref, second_ref):
    rims = 2 * EDGE

    def add(start, value):
        part = slice(start, start + radius)
        total_ref[part] = total_ref[part] + value

    part = slice(k * radius, (k + 1) * radius)
    low, high = in_order(first_ref[block, part], second_ref[block, part])
    add(0, low)
    add(rims - radius, high)
    if first_ref.shape[1] > 4 * radius:
        part = slice((4 + k) * radius, (5 + k) * radius)
        low, high = in_order(first_ref[block, part], second_ref[block, part])
        add(rims, low)
        add(rims + radius, high)


def edge_next_kernel(radius, edge_ref, sum_ref, first_ref, second_ref, next_ref,
                     across_ref, inside_ref, totals):
    @pl.loop(0, edge_ref.shape[0] // 4, unroll=2)
    def _(block):
        for k in range(4):
            row = 4 * block + k
            totals[row] = sum_ref[row]
            add_y(radius, totals.at[row], block, k, first_ref, second_ref)
            next_ref[row] = edge_ref[row] * (totals[row] * 0.5)

    cut_messages(radius, next_ref, across_ref, inside_ref)


def edge_first(current, first, second, radius):
    rows, _, depth = current.shape
    sent = shape(radius, edge_width(radius), depth)
    return call(
        functools.partial(edge_first_kernel, radius), "edge_first",
        (shape(rows, edge_width(radius), depth), sent, sent), 1, 1 << 22)(current, first, second)


def edge_next(edge, edge_sum, first, second, radius):
    rows, width, depth = edge.shape
    sent = shape(radius, width, depth)
    return call(
        functools.partial(edge_next_kernel, radius), "edge_next",
        (shape(rows, width, depth), sent, sent), 1, 1 << 22,
        [pltpu.VMEM(edge.shape, F32)])(edge, edge_sum, first, second)


def y_messages_kernel(radius, whole, edge_ref, across_ref, inside_ref, sum_ref, first_ref, second_ref):
    rows, width, _ = edge_ref.shape
    refs = (across_ref, inside_ref)
    rims = 2 * EDGE

    def row_of(row, rim):
        total = edge_ref[row]
        if rim is not None:
            total = total + refs[rim[0]][rim[1]]
        sum_ref[row] = total

    each_row(rows, radius, row_of)

    @pl.loop(0, rows // 4, unroll=2)
    def _(block):
        for k in range(4):
            row = 4 * block + k
            part = slice(k * radius, (k + 1) * radius)
            first_ref[block, part], second_ref[block, part] = in_order(
                sum_ref[row, rims : rims + radius], sum_ref[row, rims + radius : rims + 2 * radius])
            if whole:
                part = slice((4 + k) * radius, (5 + k) * radius)
                first_ref[block, part], second_ref[block, part] = in_order(
                    sum_ref[row, 0:radius], sum_ref[row, rims - radius : rims])


def y_messages(edge_sum, low, high, whole, radius):
    rows, width, depth = edge_sum.shape
    sent = shape(rows // 4, (8 if whole else 4) * radius, depth)
    return call(
        functools.partial(y_messages_kernel, radius, whole), "y_messages",
        (shape(rows, width, depth), sent, sent), 1, 1 << 22)(edge_sum, low, high)


def ratio_block(values, seen, zf_ref, zb_ref, view):
    blurred = depth_pass(values, zf_ref[view])
    return depth_pass(seen / blurred, zb_ref[view])


def forward_edge_kernel(radius, current_ref, inner_ref, before_ref, one_ref, two_ref, taps_ref, edge_ref,
                        zf_ref, zb_ref, near_ref, middle_ref, passed):
    rows, cols, depth = one_ref.shape
    kept = jnp.concatenate(
        [edge_ref[start : start + NEAR] for start in (0, cols - NEAR, cols, 2 * cols - NEAR)], axis=0)

    @pl.loop(0, rows // 4, unroll=4)
    def _(step):
        for pair in range(2):
            at = 4 * step + 2 * pair
            value = pad_rows(beside(current_ref[at], current_ref[at + 1]))
            both = multiply(kept, jnp.concatenate(stack(value), axis=0))
            for view in range(2):
                for half in range(2):
                    passed[view, at + half] = before_ref[view, at + half] + both[
                        2 * NEAR * view : 2 * NEAR * (view + 1), half * depth : (half + 1) * depth]

    for view in range(2):
        weights = load_taps(taps_ref, view, 2 * radius + 1)

        @tiles(0, 2 * NEAR, 2)
        def _(at, _inner):
            def write(q, value):
                near_ref[view, q, at, :] = value

            row_sums(weights, lambda r: passed[view, r, at, :], write, rows, rows,
                     own_tap_forward(radius), 16)

    @pl.loop(0, (rows - 2 * radius) // 2, unroll=3)
    def _(step):
        at = 2 * step
        for view, seen in ((0, one_ref), (1, two_ref)):
            parts = []
            for row in (radius + at, radius + at + 1):
                parts += [near_ref[view, row, 0:NEAR], inner_ref[view, row], near_ref[view, row, NEAR:]]
            value = ratio_block(
                jnp.concatenate(parts, axis=0), seen[pl.ds(radius + at, 2)].reshape(2 * cols, depth),
                zf_ref, zb_ref, view)
            middle_ref[view, pl.ds(at, 2)] = value.reshape(2, cols, depth)


def forward_edge(current, inner, before, one, two, weights, radius):
    taps, _, edge, _, _, zf, zb = weights
    rows, cols, depth = one.shape
    return call(
        functools.partial(forward_edge_kernel, radius), "forward_edge",
        (shape(2, rows, 2 * NEAR, depth), shape(2, rows - 2 * radius, cols, depth)),
        1 << 31, 24 * rows * NEAR * depth,
        [pltpu.VMEM((2, rows, 2 * NEAR, depth), F32)],
    )(current, inner, before, one, two, taps, edge, zf, zb)


def ratio_kernel(radius, across_ref, across_edge_ref, inside_ref, inside_edge_ref, inner_ref,
                 near_ref, one_ref, two_ref, taps_ref, full_ref, back_ref, zf_ref, zb_ref,
                 rim_across_edge_ref, rim_inside_edge_ref, rim_near_ref, outer_ref, halo, edges):
    rows, cols, depth = one_ref.shape
    main = cols - 2 * EDGE
    taps = 2 * radius + 1

    @pl.loop(0, radius // 2, unroll=5)
    def _(step):
        at = 2 * step
        for side, ref, edge_ref in zip(
            sides(), (across_ref, inside_ref), (across_edge_ref, inside_edge_ref)
        ):
            left = beside(ref[at, 0:main], ref[at + 1, 0:main])
            right = pad_rows(beside(edge_ref[at], edge_ref[at + 1]))
            both = multiply(full_ref[...], jnp.concatenate(stack(left) + stack(right), axis=0))
            for view in range(2):
                for half in range(2):
                    halo[view, side * radius + at + half] = both[
                        view * cols : (view + 1) * cols, half * depth : (half + 1) * depth]

    for view in range(2):
        weights = load_taps(taps_ref, view, taps)
        for ref, start, stop, shift in (
            (near_ref, 0, NEAR, 0), (inner_ref, NEAR, cols - NEAR, 0),
            (near_ref, cols - NEAR, cols, NEAR),
        ):
            @tiles(start, stop, 4)
            def _(at, inner):
                own = pl.ds(pl.multiple_of(inner.start + shift, 8), 8)

                def write_low(q, value):
                    edges[view, q, at, :] = value + ref[view, q, own, :]

                def write_high(q, value):
                    edges[view, radius + q, at, :] = value + ref[view, rows - radius + q, own, :]

                row_sums(weights, lambda r: halo[view, r, at, :], write_low, radius, radius,
                         lambda q, r: q + 2 * radius - r, radius)
                row_sums(weights, lambda r: halo[view, radius + r, at, :], write_high, radius, radius,
                         lambda q, r: q - r, radius)

    @pl.loop(0, radius // 2, unroll=5)
    def _(step):
        at = 2 * step
        for base, start in ((0, 0), (radius, rows - radius)):
            for view, seen in ((0, one_ref), (1, two_ref)):
                value = ratio_block(
                    edges[view, pl.ds(base + at, 2)].reshape(2 * cols, depth),
                    seen[pl.ds(start + at, 2)].reshape(2 * cols, depth), zf_ref, zb_ref, view)
                outer_ref[view, pl.ds(base + at, 2)] = value.reshape(2, cols, depth)

    for start, shift in ((0, 0), (cols - NEAR, NEAR)):
        rim_row_sums(radius, outer_ref, taps_ref, start, start + NEAR, shift, rim_near_ref)
    kept = edge_weights(back_ref, cols)

    @pl.loop(0, radius // 2, unroll=5)
    def _(step):
        at = 2 * step
        for side, ref in zip(sides(), (rim_across_edge_ref, rim_inside_edge_ref)):
            start = side * radius
            parts = []
            for view in range(2):
                parts += stack(beside(rim_near_ref[view, start + at], rim_near_ref[view, start + at + 1]))
            total = multiply(kept, jnp.concatenate(parts, axis=0))
            for half in range(2):
                ref[at + half] = total[: ref.shape[1], half * depth : (half + 1) * depth]


def ratios(main, edge, inner, near, one, two, weights, radius):
    taps, _, _, full, back, zf, zb = weights
    rows, cols, depth = one.shape
    sent = shape(radius, edge_width(radius), depth)
    return call(
        functools.partial(ratio_kernel, radius), "ratios",
        (sent, sent, shape(2, 2 * radius, 2 * NEAR, depth), shape(2, 2 * radius, cols, depth)), 1 << 33, 24 * rows * cols * depth,
        [pltpu.VMEM((2, 2 * radius, cols, depth), F32)] * 2,
    )(main[0], edge[0], main[1], edge[1], inner, near, one, two, taps, full, back, zf, zb)


def spread_row(radius, outer_ref, middle_ref, view, row, at):
    rows = outer_ref.shape[1] + middle_ref.shape[1]
    if radius <= row < rows - radius:
        return middle_ref[view, row - radius, at, :]
    return outer_ref[view, row if row < radius else row - rows + 2 * radius, at, :]


def edge_weights(back_ref, cols):
    return jnp.concatenate(
        [back_ref[cols - 2 * EDGE :, start + side : start + side + NEAR]
         for start in range(0, 6 * cols, cols) for side in (0, cols - NEAR)], axis=1)


def rim_row_sums(radius, outer_ref, taps_ref, start, stop, shift, out_ref):
    for view in range(2):
        weights = load_taps(taps_ref, view, 2 * radius + 1)

        @tiles(start, stop, 4)
        def _(at, inner):
            to = pl.ds(pl.multiple_of(inner.start + shift, 8), 8)

            def write_low(q, value):
                out_ref[view, q, to, :] = value

            def write_high(q, value):
                out_ref[view, radius + q, to, :] = value

            row_sums(weights, lambda r: outer_ref[view, r, at, :], write_low, radius, radius,
                     lambda q, r: r - q + 2 * radius, radius)
            row_sums(weights, lambda r: outer_ref[view, radius + r, at, :], write_high,
                     radius, radius, lambda q, r: r - q, radius)


def back_edge_kernel(radius, outer_ref, middle_ref, taps_ref, back_ref, out_ref, summed_ref):
    rows = out_ref.shape[0]
    cols, depth = outer_ref.shape[2:]
    kept = edge_weights(back_ref, cols)
    for view in range(2):
        weights = load_taps(taps_ref, view, 2 * radius + 1)
        for start, shift in ((0, 0), (cols - NEAR, NEAR)):
            @tiles(start, start + NEAR, 2)
            def _(at, inner):
                to = pl.ds(pl.multiple_of(inner.start + shift, 8), 8)

                def write(q, value):
                    summed_ref[view, q, to, :] = value

                row_sums(weights, lambda r: spread_row(radius, outer_ref, middle_ref, view, r, at),
                         write, rows, rows, own_tap_back(radius), 16)

    @pl.loop(0, rows // 4, unroll=4)
    def _(step):
        for pair in range(2):
            at = 4 * step + 2 * pair
            parts = []
            for view in range(2):
                parts += stack(beside(summed_ref[view, at], summed_ref[view, at + 1]))
            total = multiply(kept, jnp.concatenate(parts, axis=0))
            for half in range(2):
                out_ref[at + half] = total[: out_ref.shape[1], half * depth : (half + 1) * depth]


def back_edge(outer, middle, weights, radius):
    _, _, cols, depth = outer.shape
    rows = outer.shape[1] + middle.shape[1]
    return call(
        functools.partial(back_edge_kernel, radius), "back_edge",
        (shape(rows, edge_width(radius), depth), shape(2, rows, 2 * NEAR, depth)),
        1 << 31, 24 * rows * NEAR * depth,
    )(outer, middle, weights[0], weights[4])


def rim_main_kernel(radius, outer_ref, rim_near_ref, taps_ref, back_ref, _after, across_ref, inside_ref, rims):
    cols, depth = outer_ref.shape[2:]
    main = cols - 2 * EDGE
    rim_row_sums(radius, outer_ref, taps_ref, NEAR, cols - NEAR, 0, rims)

    @pl.loop(0, radius // 2, unroll=5)
    def _(step):
        at = 2 * step
        for side, ref in zip(sides(), (across_ref, inside_ref)):
            start = side * radius
            parts = []
            for view in range(2):
                parts += stack(beside(*[
                    jnp.concatenate(
                        [rim_near_ref[view, row, 0:NEAR], rims[view, row], rim_near_ref[view, row, NEAR:]],
                        axis=0)
                    for row in (start + at, start + at + 1)
                ]))
            total = multiply(back_ref[0:main], jnp.concatenate(parts, axis=0))
            for half in range(2):
                ref[at + half] = total[:, half * depth : (half + 1) * depth]


def rim_main(outer, rim_near, weights, after, radius):
    _, _, cols, depth = outer.shape
    sent = shape(radius, cols - 2 * EDGE, depth)
    return call(
        functools.partial(rim_main_kernel, radius), "rim_main", (sent, sent), 1 << 29, 1 << 22,
        [pltpu.VMEM((2, 2 * radius, cols - 2 * NEAR, depth), F32)],
        [pl.BlockSpec(memory_space=pltpu.VMEM)] * 4 + [pl.BlockSpec(memory_space=pl.ANY)],
    )(outer, rim_near, weights[0], weights[4], after)


def back_main_kernel(radius, outer_ref, middle_ref, near_ref, taps_ref, back_ref, _after, out_ref, summed):
    rows, main, depth = out_ref.shape
    cols = outer_ref.shape[2]
    for view in range(2):
        weights = load_taps(taps_ref, view, 2 * radius + 1)

        @tiles(NEAR, cols - NEAR, 2)
        def _(at, inner):
            def write(q, value):
                summed[view, q, inner, :] = value

            row_sums(weights, lambda r: spread_row(radius, outer_ref, middle_ref, view, r, at),
                     write, rows, rows, own_tap_back(radius), 16)

    @pl.loop(0, rows // 4, unroll=4)
    def _(step):
        for pair in range(2):
            at = 4 * step + 2 * pair
            parts = []
            for view in range(2):
                parts += stack(beside(*[
                    jnp.concatenate(
                        [near_ref[view, row, 0:NEAR], summed[view, row], near_ref[view, row, NEAR:]], axis=0)
                    for row in (at, at + 1)
                ]))
            total = multiply(back_ref[0:main], jnp.concatenate(parts, axis=0))
            for half in range(2):
                out_ref[at + half] = total[:, half * depth : (half + 1) * depth]


def back_main(outer, middle, near, weights, after, radius):
    _, _, cols, depth = outer.shape
    rows = outer.shape[1] + middle.shape[1]
    return call(
        functools.partial(back_main_kernel, radius), "back_main",
        shape(rows, cols - 2 * EDGE, depth), 1 << 31, 12 * rows * cols * depth,
        [pltpu.VMEM((2, rows, cols - 2 * NEAR, depth), F32)],
        [pl.BlockSpec(memory_space=pltpu.VMEM)] * 5 + [pl.BlockSpec(memory_space=pl.ANY)],
    )(outer, middle, near, weights[0], weights[4], after)


def finish_kernel(radius, main_ref, sum_ref, across_ref, inside_ref, edge_ref, edge_sum_ref,
                  first_ref, second_ref, out_ref, totals):
    rows, cols, _ = out_ref.shape
    rims = (across_ref, inside_ref)

    def row_of(row, rim):
        total = sum_ref[row]
        if rim is not None:
            total = total + rims[rim[0]][rim[1]]
        out_ref[row, EDGE : cols - EDGE] = main_ref[row] * (total * 0.5)

    each_row(rows, radius, row_of)

    @pl.loop(0, rows // 4, unroll=2)
    def _(block):
        for k in range(4):
            row = 4 * block + k
            totals[row] = edge_sum_ref[row, 0 : 2 * EDGE]
            add_y(radius, totals.at[row], block, k, first_ref, second_ref)
            out_ref[row, 0:EDGE] = edge_ref[row, 0:EDGE] * (totals[row, 0:EDGE] * 0.5)
            out_ref[row, cols - EDGE :] = edge_ref[row, EDGE : 2 * EDGE] * (totals[row, EDGE:] * 0.5)


def finish(main, main_sum, low, high, edge, edge_sum, from_low, from_high, radius):
    rows, width, depth = main.shape
    return call(
        functools.partial(finish_kernel, radius), "finish", shape(rows, width + 2 * EDGE, depth),
        1, 1 << 22, [pltpu.VMEM((rows, 2 * EDGE, depth), F32)],
    )(main, main_sum, low, high, edge, edge_sum, from_low, from_high)


def swap_pairs(first, second, axis):
    count = lax.axis_size(axis)

    def pairs(start):
        return [pair for i in range(start, count - 1, 2) for pair in ((i, i + 1), (i + 1, i))]

    return lax.ppermute(first, axis, pairs(1)), lax.ppermute(second, axis, pairs(0))


def local(estimate, view_one, view_two, psf_one, psf_two):
    rows, cols, depth = estimate.shape
    radius = (psf_one.shape[1] - 1) // 2
    main, first, second, across, inside = load(estimate, radius)
    first, second = swap_pairs(first, second, "gy")
    main_rims = swap_pairs(across, inside, "gx")
    weights = make_weights(psf_one, psf_two, cols, depth)
    base = EDGE
    inner, near = forward_main(main, base, weights, radius)
    first, second, near = lax.optimization_barrier((first, second, near))
    edge, across, inside = edge_first(main, first, second, radius)
    edge_rims = swap_pairs(across, inside, "gx")
    for step in range(ITERS):
        last = step == ITERS - 1
        near, middle = forward_edge(edge, inner, near, view_one, view_two, weights, radius)
        across, inside, rim_near, outer = ratios(
            main_rims, edge_rims, inner, near, view_one, view_two, weights, radius)
        edge_rims = swap_pairs(across, inside, "gx")
        edge_sum, near = back_edge(outer, middle, weights, radius)
        edge_sum, first, second = y_messages(edge_sum, *edge_rims, not last, radius)
        across, inside = rim_main(outer, rim_near, weights, first, radius)
        main_sum = back_main(outer, middle, near, weights, first, radius)
        first, second = swap_pairs(first, second, "gy")
        main_rims = swap_pairs(across, inside, "gx")
        if not last:
            main, across, inside = main_next(main, base, main_sum, *main_rims, radius)
            base = 0
            main_rims = swap_pairs(across, inside, "gx")
            inner, near = forward_main(main, base, weights, radius)
            first, second, near = lax.optimization_barrier((first, second, near))
            edge, across, inside = edge_next(edge, edge_sum, first, second, radius)
            edge_rims = swap_pairs(across, inside, "gx")
    return finish(main, main_sum, *main_rims, edge, edge_sum, first, second, radius)


def solution(mesh):
    in_specs = (P("gx", "gy", None), P("gx", "gy", None), P("gx", "gy", None), P(), P())
    out_specs = P("gx", "gy", None)
    return jax.shard_map(local, mesh=mesh, in_specs=in_specs, out_specs=out_specs, check_vma=False)
```
